128 devices in a mesh: tm: 8 (over x_hi, y), row: 8 (over z, core), col: 2 (over x_lo).
Axes of the slice: x: 4 (x_hi: 2, x_lo: 2; x = x_hi * 2 + x_lo), y: 4, z: 4, core: 2. Of those that a mesh axis runs over, the one named last changes fastest.
Arguments:
- states: bfloat16 [6144, 1024], P('tm'), may hold values from -4.5 to 4.5
- projection: bfloat16 [1024, 8192], P(None, ('row', 'col')), may hold values from -0.375 to 0.375
- offsets: float32 [8192], P(('row', 'col')), may hold values from -1 to 1
Outputs:
- instant_cov: float32 [8192, 8, 1024], P('row', 'tm', 'col')
- lagged_cov: float32 [8192, 8, 1024], P('row', 'tm', 'col')
The draws below stay inside these ranges and needn't reach their ends.
All inputs are finite; a program needn't handle non-finite values.
Results may differ from the reference program's by a relative error of at most 0.00032.
Values may be sent and summed in bfloat16 or wider, within the bound.
No kernel may reach another device: no remote copies, remote signals or barrier semaphores. Data moves between devices by JAX's collectives and lax.ppermute only.
A program may use at most 128 MiB of HBM per device.

```python
import math
import jax
import jax.numpy as jnp

F = 8192
R = 1024
LAG = 64
TIME = 6144
N_ROW = 8


def draw_states(key, part):
    key = jax.random.fold_in(key, 11)
    key_period = jax.random.fold_in(key, 0)
    key_phase = jax.random.fold_in(key, 1)
    key_amp = jax.random.fold_in(key, 2)
    key_noise = jax.random.fold_in(key, 4)
    periods = jnp.exp(jax.random.uniform(key_period, (R,), jnp.float32, math.log(128.0), math.log(4.0 * TIME)))
    phases = jax.random.uniform(key_phase, (R,), jnp.float32, -math.pi, math.pi)
    amplitude = jax.random.uniform(key_amp, (R,), jnp.float32, 0.5, 1.5)
    noise_part = 0.5 * jax.random.truncated_normal(key_noise, -3.0, 3.0, (TIME, R), jnp.float32)
    times_col = jnp.arange(TIME, dtype=jnp.float32)[:, None]
    values = amplitude * jnp.cos(2.0 * math.pi * times_col / periods + phases) + noise_part
    return values.astype(jnp.bfloat16)


def level_of(own_key, extent, pieces, smallest, largest):
    factor_of = 1.0
    for axis_at, parts in pieces:
        draws = jax.random.uniform(jax.random.fold_in(jax.random.fold_in(own_key, 6), axis_at), (parts,), jnp.float32, smallest / len(pieces), largest / len(pieces))
        factor_of = factor_of * jnp.repeat(jnp.exp(draws), extent[axis_at] // parts).reshape((-1,) + (1,) * (len(extent) - 1 - axis_at))
    return factor_of


def gaussian(key, extent, width, limit, cuts=(), kind=jnp.bfloat16):
    entries = width * jax.random.normal(key, extent, jnp.float32)
    if cuts:
        entries = entries * level_of(key, extent, cuts, -0.22, 0.18)
    return jnp.clip(entries, -limit, limit).astype(kind)


def setup_inputs(seed: int = 0) -> dict:
    key_list = jax.random.split(jax.random.key(seed), 4)
    return {
        "states": draw_states(jax.random.fold_in(key_list[3], 71), 0),
        "projection": gaussian(key_list[1], (R, F), (R // 4) ** -0.5, 0.375, ((1, 16),)),
        "offsets": jnp.clip(jax.random.uniform(key_list[2], (F,), jnp.float32, -1.0, 1.0) * level_of(key_list[2], (F,), ((0, 16),), -0.4, 0.0), -1.0, 1.0),
    }


def reference(states, projection, offsets):
    features = jnp.tanh(jnp.dot(states, projection, preferred_element_type=jnp.float32) + offsets).astype(jnp.bfloat16)
    valid_rows = TIME - LAG
    head_rows = features[:valid_rows]
    tail_rows = features[LAG:]
    instant = jnp.dot(head_rows.T, head_rows, preferred_element_type=jnp.float32) / valid_rows
    lagged = jnp.dot(head_rows.T, tail_rows, preferred_element_type=jnp.float32) / valid_rows
    return instant.reshape(F, N_ROW, F // N_ROW), lagged.reshape(F, N_ROW, F // N_ROW)
```

```python
import functools
import jax
import jax.numpy as jnp
from jax import lax
from jax.experimental import pallas as pl
from jax.experimental.pallas import tpu as pltpu
from jax.sharding import PartitionSpec as P

LAG = 64
Y = 4
AXES = ("tm", "row", "col")


def route(target):
    tm_count, row_count, col_count = (lax.axis_size(a) for a in AXES)
    flat = lambda tm, row, col: (tm * row_count + row) * col_count + col
    pairs = []
    for tm in range(tm_count):
        for row in range(row_count):
            for col in range(col_count):
                to = target(tm // Y, tm % Y, row // 2, row % 2, col)
                if to is not None:
                    x_hi, y, z, core, x_lo = to
                    pairs.append((flat(tm, row, col), flat(x_hi * Y + y % Y, z * 2 + core, x_lo)))
    return pairs


def move(block, target):
    return lax.ppermute(block, AXES, route(target))


def crossing(x_hi, y, z, core, x_lo):
    return 1 - x_hi, y, z, core, 1 - x_lo


def inner(x_hi, y, z, core, x_lo):
    return x_hi, y, z, core, 1 - x_lo


def other_core(x_hi, y, z, core, x_lo):
    return x_hi, y, z, 1 - core, x_lo


def along_y(step):
    return lambda x_hi, y, z, core, x_lo: (x_hi, y + step, z, core, x_lo)


def out_y(x_hi, y, z, core, x_lo):
    return x_hi, y + 1 - 2 * core, z, core, x_lo


def back_y(x_hi, y, z, core, x_lo):
    return x_hi, y - 1 + 2 * core, z, core, x_lo


def swap_roles(x_hi, y, z, core, x_lo):
    tm, row = x_hi * Y + y, z * 2 + core
    return row // Y, row % Y, tm // 2, tm % 2, x_lo


def moments_kernel(count, whole_first, first, last, valid_rows, *refs):
    refs = list(refs)
    ids = refs.pop(0)
    pieces = []
    for k in range(count):
        n = 1 if whole_first and k == 0 else 2
        pieces.append(refs[:n])
        refs = refs[n:]
    heads, row_proj, col_proj, row_off, col_off = refs[:5]
    refs = refs[5:]
    if not first:
        instant_in, lagged_in = refs[:2]
        refs = refs[2:]
    instant_out, lagged_out, slab, instant, lagged, row_a, row_b, col_a, col_b = refs[:9]
    refs = refs[9:]
    if last:
        instant_end, lagged_end = refs[:2]
        refs = refs[2:]
    in_sem, acc_sem, out_sem = refs
    rows, cols = instant.shape
    slab_rows = slab.shape[1] - LAG
    half = slab_rows // 2
    time_tile, col_tile = slab_rows // 3, cols // 2
    core = ids[2 * count]

    loads = []
    for k in range(count):
        if len(pieces[k]) == 1:
            copies = [pltpu.make_async_copy(pieces[k][0], slab.at[k, pl.ds(0, slab_rows)], in_sem.at[k, 0])]
        else:
            copies = [
                pltpu.make_async_copy(
                    piece, slab.at[k, pl.ds(pl.multiple_of(place * half, 16), half)], in_sem.at[k, n]
                )
                for n, (piece, place) in enumerate(zip(pieces[k], (core, 1 - core)))
            ]
        copies.append(
            pltpu.make_async_copy(heads.at[ids[count + k]], slab.at[k, pl.ds(slab_rows, LAG)], in_sem.at[k, 2])
        )
        for copy in copies:
            copy.start()
        loads.append(copies)
    if not first:
        acc_loads = [
            pltpu.make_async_copy(instant_in, instant, acc_sem.at[0]),
            pltpu.make_async_copy(lagged_in, lagged, acc_sem.at[1]),
        ]
        for copy in acc_loads:
            copy.start()

    row_bufs, col_bufs = (row_a, row_b), (col_a, col_b)

    def row_tile(k, u):
        span = slice(u * time_tile, (u + 1) * time_tile)
        features = jnp.tanh(
            lax.dot_general(row_proj[...], slab[k, span], (((1,), (1,)), ((), ())),
                            preferred_element_type=jnp.float32) + row_off[...]
        )
        position = ids[k] * slab_rows + u * time_tile + lax.broadcasted_iota(jnp.int32, (1, time_tile), 1)
        features = jnp.where(position < valid_rows, features, 0.0)
        row_bufs[k % 2][:, span] = features.astype(jnp.bfloat16)

    def col_tile_features(k, n):
        span = slice(n * col_tile, (n + 1) * col_tile)
        features = jnp.tanh(
            jnp.dot(slab[k], col_proj[:, span], preferred_element_type=jnp.float32) + col_off[:, span]
        )
        col_bufs[k % 2][:, span] = features.astype(jnp.bfloat16)

    def moment_tile(k, lag, n):
        span = slice(n * col_tile, (n + 1) * col_tile)
        acc, end = (lagged, lagged_end if last else None) if lag else (instant, instant_end if last else None)
        value = jnp.dot(row_bufs[k % 2][...], col_bufs[k % 2][lag:lag + slab_rows, span],
                        preferred_element_type=jnp.float32)
        if k > 0 or not first:
            value = acc[:, span] + value
        if last and k == count - 1:
            value = value * (1.0 / valid_rows)
            groups = cols // 128
            for g in range(col_tile // 128):
                at = n * (col_tile // 128) + g
                end[pl.ds(at, rows, stride=groups), :] = value[:, g * 128:(g + 1) * 128]
        else:
            acc[:, span] = value

    def feature_steps(k):
        return [functools.partial(row_tile, k, 0), functools.partial(row_tile, k, 1),
                functools.partial(row_tile, k, 2), functools.partial(col_tile_features, k, 0),
                functools.partial(col_tile_features, k, 1)]

    def arrive(k):
        for copy in loads[k]:
            copy.wait()

    stores = [
        pltpu.make_async_copy(instant_end if last else instant, instant_out, out_sem.at[0]),
        pltpu.make_async_copy(lagged_end if last else lagged, lagged_out, out_sem.at[1]),
    ]
    arrive(0)
    for step in feature_steps(0):
        step()
    if not first:
        for copy in acc_loads:
            copy.wait()
    for k in range(count):
        ahead = []
        if k + 1 < count:
            arrive(k + 1)
            ahead = feature_steps(k + 1)
        for t, (lag, n) in enumerate(((0, 0), (0, 1), (LAG, 0), (LAG, 1))):
            if ahead:
                ahead.pop(0)()
            moment_tile(k, lag, n)
            if k == count - 1 and n == 1:
                stores[0 if lag == 0 else 1].start()
        for step in ahead:
            step()
    for copy in stores:
        copy.wait()


def moments(slabs, ids, halos, core, heads, row_proj, col_proj, row_off, col_off, acc, last, slab_rows, valid_rows):
    rows, units = row_proj.shape
    cols = col_proj.shape[1]
    count, first = len(slabs), acc is None
    whole_first = not isinstance(slabs[0], tuple)
    numbers = jnp.stack([*ids, *halos, core]).astype(jnp.int32)
    pieces = [p for s in slabs for p in (s if isinstance(s, tuple) else (s,))]
    any_spec = pl.BlockSpec(memory_space=pl.ANY)
    vmem_spec = pl.BlockSpec(memory_space=pltpu.VMEM)
    end_shape = (rows * cols // 128, 128)
    out = jax.ShapeDtypeStruct(end_shape if last else (rows, cols), jnp.float32)
    scratch = [
        pltpu.VMEM((count, slab_rows + LAG, units), jnp.bfloat16),
        pltpu.VMEM((rows, cols), jnp.float32),
        pltpu.VMEM((rows, cols), jnp.float32),
        pltpu.VMEM((rows, slab_rows), jnp.bfloat16),
        pltpu.VMEM((rows, slab_rows), jnp.bfloat16),
        pltpu.VMEM((slab_rows + LAG, cols), jnp.bfloat16),
        pltpu.VMEM((slab_rows + LAG, cols), jnp.bfloat16),
    ]
    if last:
        scratch += [pltpu.VMEM(end_shape, jnp.float32)] * 2
    scratch += [pltpu.SemaphoreType.DMA((count, 3)), pltpu.SemaphoreType.DMA((2,)), pltpu.SemaphoreType.DMA((2,))]
    accs = [] if first else list(acc)
    return pl.pallas_call(
        functools.partial(moments_kernel, count, whole_first, first, last, valid_rows),
        in_specs=[pl.BlockSpec(memory_space=pltpu.SMEM)] + [any_spec] * (len(pieces) + 1) + [vmem_spec] * 4
        + [any_spec] * len(accs),
        out_specs=[any_spec, any_spec],
        out_shape=[out, out],
        scratch_shapes=scratch,
        compiler_params=pltpu.CompilerParams(vmem_limit_bytes=48 * 1024 * 1024),
        cost_estimate=pl.CostEstimate(
            flops=2 * count * slab_rows * (units * (rows + cols) + 2 * rows * cols),
            bytes_accessed=2 * count * slab_rows * units + 8 * rows * cols,
            transcendentals=count * slab_rows * (rows + cols),
        ),
    )(numbers, *pieces, heads, row_proj, col_proj, row_off, col_off, *accs)


def on_device(states, projection, offsets):
    slab_rows = states.shape[0]
    tm_count = lax.axis_size("tm")
    tm, row, col = (lax.axis_index(a) for a in AXES)
    x_hi, y, core = tm // Y, tm % Y, row % 2
    cols = projection.shape[1]
    half = slab_rows // 2
    valid_rows = slab_rows * tm_count - LAG

    head = states[:LAG]
    near = jnp.stack([head] + [move(head, along_y(-d)) for d in range(1, Y)])
    heads = jnp.concatenate([near, move(near, crossing)], axis=0)

    turned = projection.T
    cut = turned.shape[0] // 2
    partner = [move(turned[:cut], inner), move(turned[cut:], crossing)]
    swapped = jnp.concatenate(partner, axis=0)
    low, high = jnp.where(col == 0, turned, swapped), jnp.where(col == 0, swapped, turned)
    row_proj = jnp.concatenate([low, high], axis=0)
    off_partner = move(offsets, inner)
    row_off = jnp.concatenate(
        [jnp.where(col == 0, offsets, off_partner), jnp.where(col == 0, off_partner, offsets)]
    )[:, None]
    col_proj = move(projection, swap_roles)
    col_off = move(offsets, swap_roles)[None, :]

    mine = lax.dynamic_slice_in_dim(states, core * half, half, axis=0)
    swap = lambda piece: move(piece, other_core)
    y_out, y_back = move(mine, out_y), move(mine, back_y)
    y_far = move(y_out, out_y)
    over = move(mine, crossing)
    over_out, over_back = move(over, out_y), move(over, back_y)
    over_far = move(y_far, crossing)

    y_first, y_second = y - 1 + 2 * core, y + 1 - 2 * core
    place = lambda other, at: (jnp.where(other, 1 - x_hi, x_hi), at % Y)

    def numbers(at):
        x_at, y_at = at
        x_next = jnp.where(y_at == Y - 1, 1, x_at)
        y_next = (y_at + 1) % Y
        return x_at * Y + y_at, jnp.where(x_next == x_hi, 0, Y) + (y_next - y) % Y

    slabs = [
        (states, place(False, y)),
        ((y_out, swap(y_back)), place(False, y_first)),
        ((y_back, swap(y_out)), place(False, y_second)),
        ((over, swap(over)), place(True, y)),
        ((y_far, swap(y_far)), place(False, y + 2)),
        ((over_out, swap(over_back)), place(True, y_first)),
        ((over_back, swap(over_out)), place(True, y_second)),
        ((over_far, swap(over_far)), place(True, y + 2)),
    ]
    acc = None
    calls = ((0, 1, 2), (3, 4), (5, 6, 7))
    for at, members in enumerate(calls):
        ids, halos = zip(*(numbers(slabs[m][1]) for m in members))
        acc = moments([slabs[m][0] for m in members], ids, halos, core, heads, row_proj, col_proj, row_off, col_off,
                      acc, at == len(calls) - 1, slab_rows, valid_rows)
    shape = (2 * cols, 1, cols)
    return acc[0].reshape(shape), acc[1].reshape(shape)


def solution(mesh):
    return jax.shard_map(
        on_device,
        mesh=mesh,
        in_specs=(P("tm", None), P(None, ("row", "col")), P(("row", "col"))),
        out_specs=(P("row", "tm", "col"), P("row", "tm", "col")),
        check_vma=False,
    )
```

```python
import functools
import jax
import jax.numpy as jnp
from jax import lax
from jax.experimental import pallas as pl
from jax.experimental.pallas import tpu as pltpu
from jax.sharding import PartitionSpec as P

LAG = 64
Y = 4
AXES = ("tm", "row", "col")
SPARE = 16
VMEM_LIMIT = 40 * 1024 * 1024


def route(target):
    tm_count, row_count, col_count = (lax.axis_size(a) for a in AXES)
    flat = lambda tm, row, col: (tm * row_count + row) * col_count + col
    pairs = []
    for tm in range(tm_count):
        for row in range(row_count):
            for col in range(col_count):
                to = target(tm // Y, tm % Y, row // 2, row % 2, col)
                if to is not None:
                    x_hi, y, z, core, x_lo = to
                    pairs.append((flat(tm, row, col), flat(x_hi * Y + y % Y, z * 2 + core, x_lo)))
    return pairs


def move(block, target):
    return lax.ppermute(block, AXES, route(target))


def crossing(x_hi, y, z, core, x_lo):
    return 1 - x_hi, y, z, core, 1 - x_lo


def inner(x_hi, y, z, core, x_lo):
    return x_hi, y, z, core, 1 - x_lo


def other_core(x_hi, y, z, core, x_lo):
    return x_hi, y, z, 1 - core, x_lo


def along_y(step):
    return lambda x_hi, y, z, core, x_lo: (x_hi, y + step, z, core, x_lo)


def out_y(x_hi, y, z, core, x_lo):
    return x_hi, y + 1 - 2 * core, z, core, x_lo


def back_y(x_hi, y, z, core, x_lo):
    return x_hi, y - 1 + 2 * core, z, core, x_lo


def to_columns(x_hi, y, z, core, x_lo):
    if z // 2 != x_hi:
        return None
    t = (z % 2) * 2 + core
    step = {0: 1, 1: -1, Y - 1: 2}.get((y - t) % Y)
    return None if step is None else (x_hi, t, (z + step) % 4, core, x_lo)


def other_core_of_holder(x_hi, y, z, core, x_lo):
    return other_core(x_hi, y, z, core, x_lo) if (z // 2, (z % 2) * 2 + core) == (x_hi, y) else None


def any_spec():
    return pl.BlockSpec(memory_space=pl.ANY)


def vmem_spec():
    return pl.BlockSpec(memory_space=pltpu.VMEM)


def hbm_spec():
    return pl.BlockSpec(memory_space=pltpu.HBM)


def in_hbm(x):
    return pltpu.with_memory_space_constraint(x, pltpu.HBM)


def smem_spec():
    return pl.BlockSpec(memory_space=pltpu.SMEM)


def row_features(row_proj, states, row_off, start, valid_rows):
    features = jnp.tanh(
        lax.dot_general(row_proj, states, (((1,), (1,)), ((), ())), preferred_element_type=jnp.float32) + row_off
    )
    position = start + lax.broadcasted_iota(jnp.int32, (1, states.shape[0]), 1)
    return jnp.where(position < valid_rows, features, 0.0).astype(jnp.bfloat16)


def col_features(states, col_proj, col_off):
    return jnp.tanh(
        jnp.dot(states, col_proj, preferred_element_type=jnp.float32) + col_off
    ).astype(jnp.bfloat16)


def prepare_kernel(core, projection, offsets, states, columns, turned, mine, sem):
    half = mine.shape[0]
    copy = pltpu.make_async_copy(states.at[pl.ds(pl.multiple_of(core[0] * half, 16), half)], mine, sem)
    copy.start()
    units, cols = projection.shape
    columns[:units] = projection[...]
    turned[:cols] = projection[...].T
    high = offsets[...].astype(jnp.bfloat16)
    rest = offsets[...] - high.astype(jnp.float32)
    middle = rest.astype(jnp.bfloat16)
    low = (rest - middle.astype(jnp.float32)).astype(jnp.bfloat16)
    parts = jnp.concatenate([high, middle, low, jnp.zeros((SPARE - 3, cols), jnp.bfloat16)], axis=0)
    columns[units:] = parts
    turned[cols:] = jnp.zeros_like(turned[cols:])
    turned[cols:, :cols] = parts
    copy.wait()


def prepare(core, projection, offsets, states):
    units, cols = projection.shape
    half = states.shape[0] // 2
    return pl.pallas_call(
        prepare_kernel,
        in_specs=[smem_spec(), vmem_spec(), vmem_spec(), hbm_spec()],
        out_specs=[vmem_spec(), vmem_spec(), any_spec()],
        out_shape=[jax.ShapeDtypeStruct((units + SPARE, cols), jnp.bfloat16),
                   jax.ShapeDtypeStruct((cols + SPARE, units), jnp.bfloat16),
                   jax.ShapeDtypeStruct((half, units), jnp.bfloat16)],
        scratch_shapes=[pltpu.SemaphoreType.DMA],
        compiler_params=pltpu.CompilerParams(vmem_limit_bytes=VMEM_LIMIT),
    )(core.reshape(1).astype(jnp.int32), projection, offsets[None, :], in_hbm(states))


class OneOf:
    def __init__(self, number, sources, dst, sem):
        self.number, self.copies = number, [pltpu.make_async_copy(x, dst, sem) for x in sources]

    def start(self):
        for n, copy in enumerate(self.copies):
            pl.when(self.number == n)(copy.start)

    def wait(self):
        self.copies[0].wait()


def moments_kernel(count, first, last, slab_rows, valid_rows, *refs):
    refs = list(refs)
    take = lambda n: [refs.pop(0) for _ in range(n)]
    (ids,) = take(1)
    slabs = (valid_rows + LAG) // slab_rows if last else count
    pieces = [take(1 if (first or last) and k == 0 else 2) for k in range(slabs)]
    here = pieces[slabs - count:]
    turned, partner, *columns, row_off = take(7)
    acc_in = [] if first else take(2)
    acc_out = take(2)
    slab, row_proj, col_proj, instant, lagged, row_a, row_b, col_a, col_b = take(9)
    if last:
        instant_end, lagged_end, tails, heads = take(4)
    in_sem, proj_sem, acc_sem, out_sem = take(4)
    if last:
        (edge_sem,) = take(1)
    rows, cols = instant.shape
    units = col_proj.shape[0] - SPARE
    half = slab_rows // 2
    time_tile, col_tile = slab_rows // 3, cols // 2
    core, col, source = ids[slabs], ids[slabs + 1], ids[slabs + 2]
    number = lambda k: ids[slabs - count + k]

    def slab_copies(k):
        if len(here[k]) == 1:
            return [pltpu.make_async_copy(here[k][0], slab.at[k], in_sem.at[k, 0])]
        return [
            pltpu.make_async_copy(
                piece, slab.at[k, pl.ds(pl.multiple_of(place * half, 16), half)], in_sem.at[k, n]
            )
            for n, (piece, place) in enumerate(zip(here[k], (core, 1 - core)))
        ]

    loads = [slab_copies(k) for k in range(count)]
    col_load = OneOf(source, columns, col_proj, proj_sem.at[0])
    row_loads = [
        pltpu.make_async_copy(turned.at[pl.ds(0, rows // 2)], row_proj.at[pl.ds(0, rows // 2)], proj_sem.at[1]),
        pltpu.make_async_copy(partner.at[pl.ds(0, rows // 2)], row_proj.at[pl.ds(rows // 2, rows // 2)], proj_sem.at[2]),
    ]
    acc_loads = [pltpu.make_async_copy(a, b, acc_sem.at[n]) for n, (a, b) in enumerate(zip(acc_in, (instant, lagged)))]
    edge_loads = []
    if last:
        for k, piece in enumerate(pieces):
            tail, head = tails.at[ids[k]], heads.at[lax.rem(ids[k] + slabs - 1, slabs)]
            if len(piece) == 1:
                edge_loads.append(pltpu.make_async_copy(piece[0].at[pl.ds(slab_rows - LAG, LAG)], tail, edge_sem.at[k, 0]))
                edge_loads.append(pltpu.make_async_copy(piece[0].at[pl.ds(0, LAG)], head, edge_sem.at[k, 1]))
            else:
                ends = [p.at[pl.ds(half - LAG, LAG)] for p in piece]
                starts = [p.at[pl.ds(0, LAG)] for p in piece]
                edge_loads.append(OneOf(1 - core, ends, tail, edge_sem.at[k, 0]))
                edge_loads.append(OneOf(core, starts, head, edge_sem.at[k, 1]))

    def start(copies):
        for copy in copies:
            copy.start()

    def wait(copies):
        for copy in copies:
            copy.wait()

    start([col_load, *loads[0]])

    row_bufs, col_bufs = (row_a, row_b), (col_a, col_b)
    for buf in col_bufs:
        buf[slab_rows:] = jnp.zeros_like(buf[slab_rows:])

    def row_tile(k, u):
        span = slice(u * time_tile, (u + 1) * time_tile)
        row_bufs[k % 2][:, span] = row_features(
            row_proj[...], slab[k, span], row_off[...], number(k) * slab_rows + u * time_tile, valid_rows
        )

    def col_tile_features(k, n):
        span = slice(n * col_tile, (n + 1) * col_tile)
        off = jnp.sum(col_proj[units:, span].astype(jnp.float32), axis=0, keepdims=True)
        col_bufs[k % 2][:slab_rows, span] = col_features(slab[k], col_proj[:units, span], off)

    def edge_rows(u):
        tile = slabs * LAG // 2
        states = tails[u * slabs // 2:(u + 1) * slabs // 2].reshape(tile, units)
        row_bufs[count % 2][:, u * tile:(u + 1) * tile] = row_features(
            row_proj[...], states, row_off[...], u * tile, (slabs - 1) * LAG
        )

    def edge_cols(n):
        span = slice(n * col_tile, (n + 1) * col_tile)
        off = jnp.sum(col_proj[units:, span].astype(jnp.float32), axis=0, keepdims=True)
        col_bufs[count % 2][:slabs * LAG, span] = col_features(
            heads[...].reshape(slabs * LAG, units), col_proj[:units, span], off
        )

    def moment_tile(k, lag, n):
        span = slice(n * col_tile, (n + 1) * col_tile)
        acc = lagged if lag else instant
        buf_r, buf_c = row_bufs[k % 2], col_bufs[k % 2]
        if k < count:
            value = jnp.dot(buf_r[...], buf_c[lag:lag + slab_rows, span], preferred_element_type=jnp.float32)
        else:
            value = jnp.dot(buf_r[:, :slabs * LAG], buf_c[:slabs * LAG, span], preferred_element_type=jnp.float32)
        if k > 0 or not first:
            value = acc[:, span] + value
        if last and k == (count if lag else count - 1):
            end = lagged_end if lag else instant_end
            value = value * (1.0 / valid_rows)
            groups = cols // 128
            for g in range(col_tile // 128):
                at = n * (col_tile // 128) + g
                end[pl.ds(at, rows, stride=groups), :] = value[:, g * 128:(g + 1) * 128]
        else:
            acc[:, span] = value

    def feature_steps(k):
        steps = [functools.partial(row_tile, k, u) for u in range(3)]
        return [functools.partial(col_tile_features, k, n) for n in range(2)] + steps

    stores = []
    for m, (a, b) in enumerate(zip((instant_end, lagged_end) if last else (instant, lagged), acc_out)):
        if last:
            size = a.shape[0] // 2
            stores.append([
                pltpu.make_async_copy(
                    a.at[pl.ds(n * size, size)], b.at[pl.ds(pl.multiple_of(at * size, 8), size)], out_sem.at[m, n]
                )
                for n, at in enumerate((col, 1 - col))
            ])
        else:
            stores.append([pltpu.make_async_copy(a, b, out_sem.at[m, 0])])

    wait([col_load, *loads[0]])
    start([*row_loads, *loads[1]])
    col_steps, row_steps = feature_steps(0)[:2], feature_steps(0)[2:]
    for step in col_steps:
        step()
    wait(row_loads)
    start([*acc_loads, *(c for load in loads[2:] for c in load), *edge_loads])
    for step in row_steps:
        step()
    wait(acc_loads)
    for k in range(count):
        ahead = []
        if k + 1 < count:
            wait(loads[k + 1])
            ahead = feature_steps(k + 1)
        elif last:
            wait(edge_loads)
            ahead = [functools.partial(edge_cols, n) for n in range(2)] + [functools.partial(edge_rows, u) for u in range(2)]
        for lag, n in ((0, 0), (0, 1), (LAG, 0), (LAG, 1)):
            if ahead:
                ahead.pop(0)()
            moment_tile(k, lag, n)
            if k == count - 1 and lag == 0 and n == 1:
                start(stores[0])
        for step in ahead:
            step()
    if last:
        moment_tile(count, LAG, 0)
        moment_tile(count, LAG, 1)
    start(stores[1])
    wait(stores[0] + stores[1])


def moments(slabs, count, numbers, panels, acc, last, slab_rows, valid_rows):
    turned = panels[0]
    rows, units = 2 * (turned.shape[0] - SPARE), turned.shape[1]
    cols = rows // 2
    first = acc is None
    accs = [] if first else [in_hbm(a) for a in acc]
    pieces = [p for s in slabs for p in s]
    end_shape = (rows * cols // 128, 128)
    out = pltpu.HBM(end_shape if last else (rows, cols), jnp.float32)
    scratch = [
        pltpu.VMEM((count, slab_rows, units), jnp.bfloat16),
        pltpu.VMEM((rows, units), jnp.bfloat16),
        pltpu.VMEM((units + SPARE, cols), jnp.bfloat16),
        pltpu.VMEM((rows, cols), jnp.float32),
        pltpu.VMEM((rows, cols), jnp.float32),
        pltpu.VMEM((rows, slab_rows), jnp.bfloat16),
        pltpu.VMEM((rows, slab_rows), jnp.bfloat16),
        pltpu.VMEM((slab_rows + LAG, cols), jnp.bfloat16),
        pltpu.VMEM((slab_rows + LAG, cols), jnp.bfloat16),
    ]
    if last:
        scratch += [pltpu.VMEM(end_shape, jnp.float32)] * 2
        scratch += [pltpu.VMEM((len(slabs), LAG, units), jnp.bfloat16)] * 2
    dma = pltpu.SemaphoreType.DMA
    scratch += [dma((count, 2)), dma((3,)), dma((2,)), dma((2, 2))]
    if last:
        scratch.append(dma((len(slabs), 2)))
    return pl.pallas_call(
        functools.partial(moments_kernel, count, first, last, slab_rows, valid_rows),
        in_specs=[smem_spec()] + [any_spec()] * (len(pieces) + 6) + [vmem_spec()] + [hbm_spec()] * len(accs),
        out_specs=[hbm_spec(), hbm_spec()],
        out_shape=[out, out],
        scratch_shapes=scratch,
        compiler_params=pltpu.CompilerParams(vmem_limit_bytes=VMEM_LIMIT),
        cost_estimate=pl.CostEstimate(
            flops=2 * count * slab_rows * (units * (rows + cols) + 2 * rows * cols),
            bytes_accessed=2 * count * slab_rows * units,
            transcendentals=count * slab_rows * (rows + cols),
        ),
    )(numbers, *pieces, *panels, *accs)


def on_device(states, projection, offsets):
    slab_rows = states.shape[0]
    tm_count = lax.axis_size("tm")
    tm, row, col = (lax.axis_index(a) for a in AXES)
    x_hi, y, core = tm // Y, tm % Y, row % 2
    valid_rows = slab_rows * tm_count - LAG
    cols = projection.shape[1]
    swap = lambda piece: move(piece, other_core)

    columns, turned, mine = prepare(core, projection, offsets, states)
    partner = move(turned, inner)
    direct = move(columns, to_columns)
    y_out, y_back, over = move(mine, out_y), move(mine, back_y), move(mine, crossing)

    y_far, over_out, over_back = move(y_out, out_y), move(over, out_y), move(y_back, crossing)
    direct_b, y_out_b, y_back_b, over_b, partner = lax.optimization_barrier((direct, y_out, y_back, over, partner))
    swapped, held = swap(direct_b), move(columns, other_core_of_holder)
    swapped_out, swapped_back = swap(y_out_b), swap(y_back_b)
    partner_off = jnp.sum(partner[cols:cols + 3, :cols].astype(jnp.float32), axis=0)
    row_off = jnp.concatenate([offsets, partner_off])[:, None]
    panels = (turned, partner, columns, direct_b, held, swapped, row_off)

    y_first, y_second = y - 1 + 2 * core, y + 1 - 2 * core
    place = lambda other, at: jnp.where(other, 1 - x_hi, x_hi) * Y + at % Y
    source = jnp.where(core == y % 2, 0, 2) + jnp.where(row // 2 == tm // 2, 0, 1)
    numbers = lambda ids: jnp.stack([*ids, core, col, source]).astype(jnp.int32)

    slabs = [(in_hbm(states),), (y_out_b, swapped_back), (y_back_b, swapped_out)]
    ids = [tm, place(False, y_first), place(False, y_second)]
    acc = moments(slabs, 3, numbers(ids), panels, None, False, slab_rows, valid_rows)

    swapped_far, swapped_over = swap(y_far), swap(over_b)
    far_over = move(swapped_far, crossing)
    *acc, over_out, over_back = lax.optimization_barrier((*acc, over_out, over_back))
    slabs += [(over_b, swapped_over), (y_far, swapped_far)]
    ids += [place(True, y), place(False, y + 2)]
    acc = moments(slabs[3:], 2, numbers(ids[3:]), panels, acc, False, slab_rows, valid_rows)

    slabs += [(over_out, swap(over_back)), (over_back, swap(over_out)), (move(over_out, out_y), far_over)]
    ids += [place(True, y_first), place(True, y_second), place(True, y + 2)]
    instant, lagged = moments(slabs, 3, numbers(ids), panels, acc, True, slab_rows, valid_rows)
    shape = (2 * cols, 1, cols)
    return instant.reshape(shape), lagged.reshape(shape)


def solution(mesh):
    return jax.shard_map(
        on_device,
        mesh=mesh,
        in_specs=(P("tm", None), P(None, ("row", "col")), P(("row", "col"))),
        out_specs=(P("row", "tm", "col"), P("row", "tm", "col")),
        check_vma=False,
    )
```

```python
import functools
import jax
import jax.numpy as jnp
from jax import lax
from jax.experimental import pallas as pl
from jax.experimental.pallas import tpu as pltpu
from jax.sharding import PartitionSpec as P

LAG = 64
Y = 4
AXES = ("tm", "row", "col")
SPARE = 16
VMEM_LIMIT = 40 * 1024 * 1024


def route(target):
    tm_count, row_count, col_count = (lax.axis_size(a) for a in AXES)
    flat = lambda tm, row, col: (tm * row_count + row) * col_count + col
    pairs = []
    for tm in range(tm_count):
        for row in range(row_count):
            for col in range(col_count):
                to = target(tm // Y, tm % Y, row // 2, row % 2, col)
                if to is not None:
                    x_hi, y, z, core, x_lo = to
                    pairs.append((flat(tm, row, col), flat(x_hi * Y + y % Y, z * 2 + core, x_lo)))
    return pairs


def move(block, target):
    return lax.ppermute(block, AXES, route(target))


def crossing(x_hi, y, z, core, x_lo):
    return 1 - x_hi, y, z, core, 1 - x_lo


def inner(x_hi, y, z, core, x_lo):
    return x_hi, y, z, core, 1 - x_lo


def other_core(x_hi, y, z, core, x_lo):
    return x_hi, y, z, 1 - core, x_lo


def along_y(step):
    return lambda x_hi, y, z, core, x_lo: (x_hi, y + step, z, core, x_lo)


def out_y(x_hi, y, z, core, x_lo):
    return x_hi, y + 1 - 2 * core, z, core, x_lo


def back_y(x_hi, y, z, core, x_lo):
    return x_hi, y - 1 + 2 * core, z, core, x_lo


def along_z(step):
    def target(x_hi, y, z, core, x_lo):
        return (x_hi, y, (z + step) % 4, core, x_lo) if x_hi * Y + y == z * 2 + core else None
    return target


def any_spec():
    return pl.BlockSpec(memory_space=pl.ANY)


def vmem_spec():
    return pl.BlockSpec(memory_space=pltpu.VMEM)


def hbm_spec():
    return pl.BlockSpec(memory_space=pltpu.HBM)


def in_hbm(x):
    return pltpu.with_memory_space_constraint(x, pltpu.HBM)


def in_vmem(x):
    return pltpu.with_memory_space_constraint(x, pltpu.VMEM)


def smem_spec():
    return pl.BlockSpec(memory_space=pltpu.SMEM)


def row_features(row_proj, states, row_off, start, valid_rows):
    features = jnp.tanh(
        lax.dot_general(row_proj, states, (((1,), (1,)), ((), ())), preferred_element_type=jnp.float32) + row_off
    )
    position = start + lax.broadcasted_iota(jnp.int32, (1, states.shape[0]), 1)
    return jnp.where(position < valid_rows, features, 0.0).astype(jnp.bfloat16)


def col_features(states, col_proj, col_off):
    return jnp.tanh(
        jnp.dot(states, col_proj, preferred_element_type=jnp.float32) + col_off
    ).astype(jnp.bfloat16)


def prepare_kernel(core, projection, offsets, states, columns, turned, mine, sem):
    half = mine.shape[0]
    copy = pltpu.make_async_copy(states.at[pl.ds(pl.multiple_of(core[0] * half, 16), half)], mine, sem)
    copy.start()
    units, cols = projection.shape
    columns[:units] = projection[...]
    turned[:cols] = projection[...].T
    high = offsets[...].astype(jnp.bfloat16)
    rest = offsets[...] - high.astype(jnp.float32)
    middle = rest.astype(jnp.bfloat16)
    low = (rest - middle.astype(jnp.float32)).astype(jnp.bfloat16)
    parts = jnp.concatenate([high, middle, low, jnp.zeros((SPARE - 3, cols), jnp.bfloat16)], axis=0)
    columns[units:] = parts
    turned[cols:] = jnp.zeros_like(turned[cols:])
    turned[cols:, :cols] = parts
    copy.wait()


def prepare(core, projection, offsets, states):
    units, cols = projection.shape
    half = states.shape[0] // 2
    return pl.pallas_call(
        prepare_kernel,
        in_specs=[smem_spec(), vmem_spec(), vmem_spec(), hbm_spec()],
        out_specs=[vmem_spec(), vmem_spec(), any_spec()],
        out_shape=[jax.ShapeDtypeStruct((units + SPARE, cols), jnp.bfloat16),
                   jax.ShapeDtypeStruct((cols + SPARE, units), jnp.bfloat16),
                   jax.ShapeDtypeStruct((half, units), jnp.bfloat16)],
        scratch_shapes=[pltpu.SemaphoreType.DMA],
        compiler_params=pltpu.CompilerParams(vmem_limit_bytes=VMEM_LIMIT),
    )(core.reshape(1).astype(jnp.int32), projection, offsets[None, :], in_hbm(states))


class OneOf:
    def __init__(self, number, sources, dst, sem):
        self.number, self.copies = number, [pltpu.make_async_copy(x, dst, sem) for x in sources]

    def start(self):
        for n, copy in enumerate(self.copies):
            pl.when(self.number == n)(copy.start)

    def wait(self):
        self.copies[0].wait()


def moments_kernel(count, at, first, last, slab_rows, valid_rows, *refs):
    refs = list(refs)
    take = lambda n: [refs.pop(0) for _ in range(n)]
    (ids,) = take(1)
    slabs = (valid_rows + LAG) // slab_rows
    pieces = [take(1 if (first or last) and k == 0 else 2) for k in range(slabs if last else count)]
    here = pieces[-count:]
    if first:
        turned, partner, *columns, row_off = take(5)
        instant, lagged, row_proj, col_proj = take(4)
    else:
        row_proj, col_proj, row_off = take(3)
        take(2)
        if last:
            acc_out = take(2)
        instant, lagged = take(2)
    slab, row_a, row_b, col_a, col_b, in_sem = take(6)
    if first:
        (proj_sem,) = take(1)
    if last:
        instant_end, lagged_end, tails, heads, edge_sem, out_sem = take(6)
    rows, cols = instant.shape
    units = col_proj.shape[0] - SPARE
    half = slab_rows // 2
    time_tile, col_tile = slab_rows // 3, cols // 2
    core, col, source = ids[slabs], ids[slabs + 1], ids[slabs + 2]
    number = lambda k: ids[at + k]

    def start(copies):
        for copy in copies:
            copy.start()

    def wait(copies):
        for copy in copies:
            copy.wait()

    def slab_copies(k):
        if len(here[k]) == 1:
            return [pltpu.make_async_copy(here[k][0], slab.at[k], in_sem.at[k, 0])]
        return [
            pltpu.make_async_copy(
                piece, slab.at[k, pl.ds(pl.multiple_of(place * half, 16), half)], in_sem.at[k, n]
            )
            for n, (piece, place) in enumerate(zip(here[k], (core, 1 - core)))
        ]

    loads = [slab_copies(k) for k in range(count)]
    col_loads, row_loads, edge_loads = [], [], []
    if first:
        own = rows // 2
        col_loads = [OneOf(source, columns, col_proj, proj_sem.at[0])]
        row_loads = [
            pltpu.make_async_copy(turned.at[pl.ds(0, own)], row_proj.at[pl.ds(0, own)], proj_sem.at[1]),
            pltpu.make_async_copy(partner.at[pl.ds(0, own)], row_proj.at[pl.ds(own, own)], proj_sem.at[2]),
        ]
    if last:
        for k, piece in enumerate(pieces):
            tail, head = tails.at[ids[k]], heads.at[lax.rem(ids[k] + slabs - 1, slabs)]
            if len(piece) == 1:
                edge_loads.append(pltpu.make_async_copy(piece[0].at[pl.ds(slab_rows - LAG, LAG)], tail, edge_sem.at[k, 0]))
                edge_loads.append(pltpu.make_async_copy(piece[0].at[pl.ds(0, LAG)], head, edge_sem.at[k, 1]))
            else:
                ends = [p.at[pl.ds(half - LAG, LAG)] for p in piece]
                starts = [p.at[pl.ds(0, LAG)] for p in piece]
                edge_loads.append(OneOf(1 - core, ends, tail, edge_sem.at[k, 0]))
                edge_loads.append(OneOf(core, starts, head, edge_sem.at[k, 1]))
    start([*col_loads, *loads[0]])

    row_bufs, col_bufs = (row_a, row_b), (col_a, col_b)
    for buf in col_bufs:
        buf[slab_rows:] = jnp.zeros_like(buf[slab_rows:])

    def row_tile(k, u):
        span = slice(u * time_tile, (u + 1) * time_tile)
        row_bufs[k % 2][:, span] = row_features(
            row_proj[...], slab[k, span], row_off[...], number(k) * slab_rows + u * time_tile, valid_rows
        )

    def col_tile_features(k, n):
        span = slice(n * col_tile, (n + 1) * col_tile)
        off = jnp.sum(col_proj[units:, span].astype(jnp.float32), axis=0, keepdims=True)
        col_bufs[k % 2][:slab_rows, span] = col_features(slab[k], col_proj[:units, span], off)

    def edge_rows(u):
        tile = slabs * LAG // 2
        states = tails[u * slabs // 2:(u + 1) * slabs // 2].reshape(tile, units)
        row_bufs[count % 2][:, u * tile:(u + 1) * tile] = row_features(
            row_proj[...], states, row_off[...], u * tile, (slabs - 1) * LAG
        )

    def edge_cols(n):
        span = slice(n * col_tile, (n + 1) * col_tile)
        off = jnp.sum(col_proj[units:, span].astype(jnp.float32), axis=0, keepdims=True)
        col_bufs[count % 2][:slabs * LAG, span] = col_features(
            heads[...].reshape(slabs * LAG, units), col_proj[:units, span], off
        )

    def moment_tile(k, lag, n):
        span = slice(n * col_tile, (n + 1) * col_tile)
        acc = lagged if lag else instant
        buf_r, buf_c = row_bufs[k % 2], col_bufs[k % 2]
        if k < count:
            value = jnp.dot(buf_r[...], buf_c[lag:lag + slab_rows, span], preferred_element_type=jnp.float32)
        else:
            value = jnp.dot(buf_r[:, :slabs * LAG], buf_c[:slabs * LAG, span], preferred_element_type=jnp.float32)
        if k > 0 or not first:
            value = acc[:, span] + value
        if last and k == (count if lag else count - 1):
            end = lagged_end if lag else instant_end
            value = value * (1.0 / valid_rows)
            groups = cols // 128
            for g in range(col_tile // 128):
                at = n * (col_tile // 128) + g
                end[pl.ds(at, rows, stride=groups), :] = value[:, g * 128:(g + 1) * 128]
        else:
            acc[:, span] = value

    def feature_steps(k):
        steps = [functools.partial(row_tile, k, u) for u in range(3)]
        return [functools.partial(col_tile_features, k, n) for n in range(2)] + steps

    stores = []
    if last:
        for m, (a, b) in enumerate(zip((instant_end, lagged_end), acc_out)):
            size = a.shape[0] // 2
            stores.append([
                pltpu.make_async_copy(
                    a.at[pl.ds(n * size, size)], b.at[pl.ds(pl.multiple_of(place * size, 8), size)], out_sem.at[m, n]
                )
                for n, place in enumerate((col, 1 - col))
            ])

    wait([*col_loads, *loads[0]])
    start([*row_loads, *(loads[1] if count > 1 else [])])
    col_steps, row_steps = feature_steps(0)[:2], feature_steps(0)[2:]
    for step in col_steps:
        step()
    wait(row_loads)
    start([*(c for load in loads[2:] for c in load), *edge_loads])
    for step in row_steps:
        step()
    for k in range(count):
        ahead = []
        if k + 1 < count:
            wait(loads[k + 1])
            ahead = feature_steps(k + 1)
        elif last:
            wait(edge_loads)
            ahead = [functools.partial(edge_cols, n) for n in range(2)] + [functools.partial(edge_rows, u) for u in range(2)]
        for lag, n in ((0, 0), (0, 1), (LAG, 0), (LAG, 1)):
            if ahead:
                ahead.pop(0)()
            moment_tile(k, lag, n)
            if last and k == count - 1 and lag == 0 and n == 1:
                start(stores[0])
        for step in ahead:
            step()
    if last:
        moment_tile(count, LAG, 0)
        moment_tile(count, LAG, 1)
        start(stores[1])
        wait(stores[0] + stores[1])


def moments(slabs, count, numbers, panels, acc, last, slab_rows, valid_rows):
    first = acc is None
    row_off = panels[-1]
    rows = row_off.shape[0]
    cols, units = rows // 2, slabs[0][0].shape[1]
    at = len(slabs) - count
    if not last:
        slabs = slabs[at:]
    pieces = [p for s in slabs for p in s]
    end_shape = (rows * cols // 128, 128)
    acc_shape = [pltpu.VMEM((rows, cols), jnp.float32)] * 2
    outs, out_specs = acc_shape, [vmem_spec()] * 2
    dma = pltpu.SemaphoreType.DMA
    scratch = [
        pltpu.VMEM((count, slab_rows, units), jnp.bfloat16),
        pltpu.VMEM((rows, slab_rows), jnp.bfloat16),
        pltpu.VMEM((rows, slab_rows), jnp.bfloat16),
        pltpu.VMEM((slab_rows + LAG, cols), jnp.bfloat16),
        pltpu.VMEM((slab_rows + LAG, cols), jnp.bfloat16),
        dma((count, 2)),
    ]
    args = [numbers, *pieces]
    specs = [smem_spec()] + [any_spec()] * len(pieces)
    aliases = {}
    if first:
        args += [*panels[:-1], in_vmem(row_off)]
        specs += [any_spec()] * (len(panels) - 1) + [vmem_spec()]
        outs = outs + [pltpu.VMEM((rows, units), jnp.bfloat16), pltpu.VMEM((units + SPARE, cols), jnp.bfloat16)]
        out_specs = out_specs + [vmem_spec()] * 2
        scratch.append(dma((3,)))
    else:
        if last:
            outs, out_specs = [pltpu.HBM(end_shape, jnp.float32)] * 2 + outs, [hbm_spec()] * 2 + out_specs
            scratch += [pltpu.VMEM(end_shape, jnp.float32)] * 2
            scratch += [pltpu.VMEM((len(slabs), LAG, units), jnp.bfloat16)] * 2
            scratch += [dma((len(slabs), 2)), dma((2, 2))]
        args += [in_vmem(x) for x in (*panels, *acc)]
        specs += [vmem_spec()] * 5
        aliases = {len(args) - 2 + n: len(outs) - 2 + n for n in range(2)}
    return pl.pallas_call(
        functools.partial(moments_kernel, count, at, first, last, slab_rows, valid_rows),
        in_specs=specs,
        out_specs=out_specs,
        out_shape=outs,
        scratch_shapes=scratch,
        input_output_aliases=aliases,
        compiler_params=pltpu.CompilerParams(vmem_limit_bytes=VMEM_LIMIT),
        cost_estimate=pl.CostEstimate(
            flops=2 * count * slab_rows * (units * (rows + cols) + 2 * rows * cols),
            bytes_accessed=2 * count * slab_rows * units,
            transcendentals=count * slab_rows * (rows + cols),
        ),
    )(*args)


def on_device(states, projection, offsets):
    slab_rows = states.shape[0]
    tm_count = lax.axis_size("tm")
    tm, row, col = (lax.axis_index(a) for a in AXES)
    x_hi, y, core = tm // Y, tm % Y, row % 2
    valid_rows = slab_rows * tm_count - LAG
    cols = projection.shape[1]
    swap = lambda piece: move(piece, other_core)

    y_first, y_second = y - 1 + 2 * core, y + 1 - 2 * core
    place = lambda other, at: jnp.where(other, 1 - x_hi, x_hi) * Y + at % Y
    ids = [tm, place(False, y_first), place(False, y_second), place(True, y), place(False, y + 2),
           place(True, y_first), place(True, y_second), place(True, y + 2)]
    fetched = core == y % 2
    numbers = jnp.stack([*ids, core, col, jnp.where(fetched, 0, 1)]).astype(jnp.int32)

    columns, turned, mine = prepare(core, projection, offsets, states)
    partner = move(turned, inner)
    ahead, behind, beyond = (move(columns, along_z(step)) for step in (1, -1, 2))
    y_out = move(mine, out_y)
    y_out, mine_over = lax.optimization_barrier((y_out, mine))
    over = move(mine_over, crossing)
    behind, mine_back = lax.optimization_barrier((behind, mine))
    y_back = move(mine_back, back_y)

    ahead, behind, beyond, partner = lax.optimization_barrier((ahead, behind, beyond, partner))
    y_out_b, y_back_b, over, panel_ahead = lax.optimization_barrier((y_out, y_back, over, ahead))
    steps = (row // 2 - tm // 2) % 4
    panel = jnp.where(steps == 0, columns, jnp.where(steps == 1, panel_ahead, jnp.where(steps == 2, beyond, behind)))
    swapped = swap(panel)
    swapped_out, swapped_back = swap(y_out_b), swap(y_back_b)
    partner_off = jnp.sum(partner[cols:cols + 3, :cols].astype(jnp.float32), axis=0)
    row_off = jnp.concatenate([offsets, partner_off])[:, None]

    y_far, over_out, over_back = move(y_out_b, out_y), move(over, out_y), move(y_back_b, crossing)
    swapped_over = swap(over)
    sizes = (slab_rows, valid_rows)
    slabs = [(in_hbm(states),), (y_out_b, swapped_back), (y_back_b, swapped_out)]
    *acc, row_proj, col_proj = moments(
        slabs, 3, numbers, (turned, partner, panel, swapped, row_off), None, False, *sizes
    )
    panels = (row_proj, col_proj, row_off)

    *acc, y_far, over_out, over_back = lax.optimization_barrier((*acc, y_far, over_out, over_back))
    swapped_far = swap(y_far)
    slabs += [(over, swapped_over), (y_far, swapped_far), (over_out, swap(over_back)), (over_back, swap(over_out))]
    over_far, far_over = move(over_out, out_y), move(swapped_far, crossing)
    acc = moments(slabs, 4, numbers, panels, acc, False, *sizes)

    slabs += [(over_far, far_over)]
    instant, lagged, *_ = moments(slabs, 1, numbers, panels, acc, True, *sizes)
    shape = (2 * cols, 1, cols)
    return instant.reshape(shape), lagged.reshape(shape)


def solution(mesh):
    return jax.shard_map(
        on_device,
        mesh=mesh,
        in_specs=(P("tm", None), P(None, ("row", "col")), P(("row", "col"))),
        out_specs=(P("row", "tm", "col"), P("row", "tm", "col")),
        check_vma=False,
    )
```

```python
import functools
import jax
import jax.numpy as jnp
from jax import lax
from jax.experimental import pallas as pl
from jax.experimental.pallas import tpu as pltpu
from jax.sharding import PartitionSpec as P

LAG = 64
Y = 4
AXES = ("tm", "row", "col")
SPARE = 16
MIB = 1024 * 1024


def route(target):
    tm_count, row_count, col_count = (lax.axis_size(a) for a in AXES)
    flat = lambda tm, row, col: (tm * row_count + row) * col_count + col
    pairs = []
    for tm in range(tm_count):
        for row in range(row_count):
            for col in range(col_count):
                to = target(tm // Y, tm % Y, row // 2, row % 2, col)
                if to is not None:
                    x_hi, y, z, core, x_lo = to
                    pairs.append((flat(tm, row, col), flat(x_hi * Y + y % Y, z * 2 + core, x_lo)))
    return pairs


def move(block, target):
    return lax.ppermute(block, AXES, route(target))


def crossing(x_hi, y, z, core, x_lo):
    return 1 - x_hi, y, z, core, 1 - x_lo


def inner(x_hi, y, z, core, x_lo):
    return x_hi, y, z, core, 1 - x_lo


def other_core(x_hi, y, z, core, x_lo):
    return x_hi, y, z, 1 - core, x_lo


def along_y(step):
    return lambda x_hi, y, z, core, x_lo: (x_hi, y + step, z, core, x_lo)


def out_y(x_hi, y, z, core, x_lo):
    return x_hi, y + 1 - 2 * core, z, core, x_lo


def back_y(x_hi, y, z, core, x_lo):
    return x_hi, y - 1 + 2 * core, z, core, x_lo


def along_z(step):
    def target(x_hi, y, z, core, x_lo):
        return (x_hi, y, (z + step) % 4, core, x_lo) if x_hi * Y + y == z * 2 + core else None
    return target


def any_spec():
    return pl.BlockSpec(memory_space=pl.ANY)


def vmem_spec():
    return pl.BlockSpec(memory_space=pltpu.VMEM)


def hbm_spec():
    return pl.BlockSpec(memory_space=pltpu.HBM)


def in_hbm(x):
    return pltpu.with_memory_space_constraint(x, pltpu.HBM)


def in_vmem(x):
    return pltpu.with_memory_space_constraint(x, pltpu.VMEM)


def smem_spec():
    return pl.BlockSpec(memory_space=pltpu.SMEM)


def row_features(row_proj, states, row_off, start, valid_rows):
    features = jnp.tanh(
        lax.dot_general(row_proj, states, (((1,), (1,)), ((), ())), preferred_element_type=jnp.float32) + row_off
    )
    position = start + lax.broadcasted_iota(jnp.int32, (1, states.shape[0]), 1)
    return jnp.where(position < valid_rows, features, 0.0).astype(jnp.bfloat16)


def col_features(states, col_proj, col_off):
    return jnp.tanh(
        jnp.dot(states, col_proj, preferred_element_type=jnp.float32) + col_off
    ).astype(jnp.bfloat16)


def prepare_kernel(at, numbers, projection, offsets, states, columns, turned, mine, sem):
    half = mine.shape[0]
    copy = pltpu.make_async_copy(states.at[pl.ds(pl.multiple_of(numbers[at] * half, 16), half)], mine, sem)
    copy.start()
    units, cols = projection.shape
    columns[:units] = projection[...]
    turned[:cols] = projection[...].T
    high = offsets[...].astype(jnp.bfloat16)
    rest = offsets[...] - high.astype(jnp.float32)
    middle = rest.astype(jnp.bfloat16)
    low = (rest - middle.astype(jnp.float32)).astype(jnp.bfloat16)
    parts = jnp.concatenate([high, middle, low, jnp.zeros((SPARE - 3, cols), jnp.bfloat16)], axis=0)
    columns[units:] = parts
    turned[cols:] = jnp.zeros_like(turned[cols:])
    turned[cols:, :cols] = parts
    copy.wait()


def prepare(at, numbers, projection, offsets, states):
    units, cols = projection.shape
    half = states.shape[0] // 2
    return pl.pallas_call(
        functools.partial(prepare_kernel, at),
        in_specs=[smem_spec(), vmem_spec(), vmem_spec(), hbm_spec()],
        out_specs=[vmem_spec(), vmem_spec(), vmem_spec()],
        out_shape=[jax.ShapeDtypeStruct((units + SPARE, cols), jnp.bfloat16),
                   jax.ShapeDtypeStruct((cols + SPARE, units), jnp.bfloat16),
                   jax.ShapeDtypeStruct((half, units), jnp.bfloat16)],
        scratch_shapes=[pltpu.SemaphoreType.DMA],
        compiler_params=pltpu.CompilerParams(vmem_limit_bytes=12 * MIB),
    )(numbers, projection, offsets, in_hbm(states))


class OneOf:
    def __init__(self, number, sources, dst, sem):
        self.number, self.copies = number, [pltpu.make_async_copy(x, dst, sem) for x in sources]

    def start(self):
        for n, copy in enumerate(self.copies):
            pl.when(self.number == n)(copy.start)

    def wait(self):
        self.copies[0].wait()


def pick_kernel(at, numbers, *refs):
    *sources, out, sem = refs
    copy = OneOf(numbers[at], sources, out, sem)
    copy.start()
    copy.wait()


def pick(at, numbers, *sources):
    return pl.pallas_call(
        functools.partial(pick_kernel, at),
        in_specs=[smem_spec()] + [any_spec()] * len(sources),
        out_specs=vmem_spec(),
        out_shape=jax.ShapeDtypeStruct(sources[0].shape, sources[0].dtype),
        scratch_shapes=[pltpu.SemaphoreType.DMA],
        compiler_params=pltpu.CompilerParams(vmem_limit_bytes=8 * MIB),
    )(numbers, *sources)


def slab_copies(pieces, core, dst, sems):
    if len(pieces) == 1:
        return [pltpu.make_async_copy(pieces[0], dst, sems.at[0])]
    half = pieces[0].shape[0]
    return [
        pltpu.make_async_copy(piece, dst.at[pl.ds(pl.multiple_of(place * half, 16), half)], sems.at[n])
        for n, (piece, place) in enumerate(zip(pieces, (core, 1 - core)))
    ]


def start(copies):
    for copy in copies:
        copy.start()


def wait(copies):
    for copy in copies:
        copy.wait()


def opening_kernel(count, valid_rows, ids, *refs):
    refs = list(refs)
    take = lambda n: [refs.pop(0) for _ in range(n)]
    pieces = [take(1 if k == 0 else 2) for k in range(count)]
    turned, partner, offsets = take(3)
    row_proj, row_off, slab, features, parts, proj_sem, in_sem = take(7)
    rows = row_proj.shape[0]
    own, slab_rows = rows // 2, slab.shape[1]
    core = ids[(valid_rows + LAG) // slab_rows]
    row_loads = [
        pltpu.make_async_copy(turned.at[pl.ds(0, own)], row_proj.at[pl.ds(0, own)], proj_sem.at[0]),
        pltpu.make_async_copy(partner.at[pl.ds(0, own)], row_proj.at[pl.ds(own, own)], proj_sem.at[1]),
        pltpu.make_async_copy(partner.at[pl.ds(own, SPARE)], parts, proj_sem.at[2]),
    ]
    loads = [slab_copies(pieces[k], core, slab.at[k], in_sem.at[k]) for k in range(count)]
    start([*row_loads, *loads[0], *loads[1]])
    turn = lambda line: jnp.broadcast_to(line, (8, own)).T[:, :1]
    row_off[:own] = turn(offsets[...])
    wait(row_loads)
    start([copy for load in loads[2:] for copy in load])
    row_off[own:] = turn(jnp.sum(parts[:, :own].astype(jnp.float32), axis=0, keepdims=True))
    tile = slab_rows // 3
    for k in range(count):
        wait(loads[k])
        for u in range(3):
            span = slice(u * tile, (u + 1) * tile)
            features[k, :, span] = row_features(
                row_proj[...], slab[k, span], row_off[...], ids[k] * slab_rows + u * tile, valid_rows
            )


def opening(slabs, numbers, turned, partner, offsets, slab_rows, valid_rows):
    rows, units, count = 2 * (turned.shape[0] - SPARE), turned.shape[1], len(slabs)
    pieces = [p for s in slabs for p in s]
    dma = pltpu.SemaphoreType.DMA
    return pl.pallas_call(
        functools.partial(opening_kernel, count, valid_rows),
        in_specs=[smem_spec()] + [any_spec()] * (len(pieces) + 2) + [vmem_spec()],
        out_specs=[vmem_spec()] * 4,
        out_shape=[
            pltpu.VMEM((rows, units), jnp.bfloat16),
            pltpu.VMEM((rows, 1), jnp.float32),
            pltpu.VMEM((count, slab_rows, units), jnp.bfloat16),
            pltpu.VMEM((count, rows, slab_rows), jnp.bfloat16),
        ],
        scratch_shapes=[pltpu.VMEM((SPARE, units), jnp.bfloat16), dma((3,)), dma((count, 2))],
        compiler_params=pltpu.CompilerParams(vmem_limit_bytes=12 * MIB),
        cost_estimate=pl.CostEstimate(
            flops=2 * count * slab_rows * units * rows, bytes_accessed=2 * count * slab_rows * units,
            transcendentals=count * slab_rows * rows,
        ),
    )(numbers, *pieces, turned, partner, offsets)


def moments_kernel(count, ready, at, first, last, slab_rows, valid_rows, *refs):
    refs = list(refs)
    take = lambda n: [refs.pop(0) for _ in range(n)]
    (ids,) = take(1)
    slabs = (valid_rows + LAG) // slab_rows
    pieces = [take(1 if last and k == 0 else 2) for k in range(slabs if last else count - ready)]
    here = [None] * ready + pieces[ready - count:]
    if first:
        ready_slab, ready_rows, *columns, row_proj, row_off = take(6)
        instant, lagged, col_proj = take(3)
    else:
        row_proj, row_off, col_proj = take(3)
        take(2)
        if last:
            acc_out = take(2)
        instant, lagged = take(2)
    slab, row_a, row_b, col_a, col_b, in_sem = take(6)
    if first:
        (proj_sem,) = take(1)
    if last:
        instant_end, lagged_end, tails, heads, edge_sem, out_sem = take(6)
    rows, cols = instant.shape
    units = col_proj.shape[0] - SPARE
    half = slab_rows // 2
    time_tile, col_tile = slab_rows // 3, cols // 2
    core, col, source = ids[slabs], ids[slabs + 1], ids[slabs + 2]
    number = lambda k: ids[at + k]

    loads = [[] if k < ready else slab_copies(here[k], core, slab.at[k - ready], in_sem.at[k - ready]) for k in range(count)]
    states = lambda k: ready_slab.at[k] if k < ready else slab.at[k - ready]
    rows_of = lambda k: ready_rows.at[k] if k < ready else row_bufs[k % 2]
    col_loads, edge_loads = [], []
    if first:
        col_loads = [OneOf(source, columns, col_proj, proj_sem)]
    if last:
        for k, piece in enumerate(pieces):
            tail, head = tails.at[ids[k]], heads.at[lax.rem(ids[k] + slabs - 1, slabs)]
            if len(piece) == 1:
                edge_loads.append(pltpu.make_async_copy(piece[0].at[pl.ds(slab_rows - LAG, LAG)], tail, edge_sem.at[k, 0]))
                edge_loads.append(pltpu.make_async_copy(piece[0].at[pl.ds(0, LAG)], head, edge_sem.at[k, 1]))
            else:
                ends = [p.at[pl.ds(half - LAG, LAG)] for p in piece]
                starts = [p.at[pl.ds(0, LAG)] for p in piece]
                edge_loads.append(OneOf(1 - core, ends, tail, edge_sem.at[k, 0]))
                edge_loads.append(OneOf(core, starts, head, edge_sem.at[k, 1]))
    start([*col_loads, *loads[0]])

    row_bufs, col_bufs = (row_a, row_b), (col_a, col_b)
    for buf in col_bufs:
        buf[slab_rows:] = jnp.zeros_like(buf[slab_rows:])

    def row_tile(k, u):
        span = slice(u * time_tile, (u + 1) * time_tile)
        row_bufs[k % 2][:, span] = row_features(
            row_proj[...], states(k)[span], row_off[...], number(k) * slab_rows + u * time_tile, valid_rows
        )

    def col_tile_features(k, n):
        span = slice(n * col_tile, (n + 1) * col_tile)
        off = jnp.sum(col_proj[units:, span].astype(jnp.float32), axis=0, keepdims=True)
        col_bufs[k % 2][:slab_rows, span] = col_features(states(k)[...], col_proj[:units, span], off)

    def edge_rows(u):
        tile = slabs * LAG // 2
        ends = tails[u * slabs // 2:(u + 1) * slabs // 2].reshape(tile, units)
        row_bufs[count % 2][:, u * tile:(u + 1) * tile] = row_features(
            row_proj[...], ends, row_off[...], u * tile, (slabs - 1) * LAG
        )

    def edge_cols(n):
        span = slice(n * col_tile, (n + 1) * col_tile)
        off = jnp.sum(col_proj[units:, span].astype(jnp.float32), axis=0, keepdims=True)
        col_bufs[count % 2][:slabs * LAG, span] = col_features(
            heads[...].reshape(slabs * LAG, units), col_proj[:units, span], off
        )

    def moment_tile(k, lag, n):
        span = slice(n * col_tile, (n + 1) * col_tile)
        acc = lagged if lag else instant
        buf_r, buf_c = row_bufs[k % 2] if k == count else rows_of(k), col_bufs[k % 2]
        if k < count:
            value = jnp.dot(buf_r[...], buf_c[lag:lag + slab_rows, span], preferred_element_type=jnp.float32)
        else:
            value = jnp.dot(buf_r[:, :slabs * LAG], buf_c[:slabs * LAG, span], preferred_element_type=jnp.float32)
        if k > 0 or not first:
            value = acc[:, span] + value
        if last and k == (count if lag else count - 1):
            end = lagged_end if lag else instant_end
            value = value * (1.0 / valid_rows)
            groups = cols // 128
            for g in range(col_tile // 128):
                at = n * (col_tile // 128) + g
                end[pl.ds(at, rows, stride=groups), :] = value[:, g * 128:(g + 1) * 128]
        else:
            acc[:, span] = value

    def feature_steps(k):
        steps = [] if k < ready else [functools.partial(row_tile, k, u) for u in range(3)]
        return [functools.partial(col_tile_features, k, n) for n in range(2)] + steps

    stores = []
    if last:
        for m, (a, b) in enumerate(zip((instant_end, lagged_end), acc_out)):
            size = a.shape[0] // 2
            stores.append([
                pltpu.make_async_copy(
                    a.at[pl.ds(n * size, size)], b.at[pl.ds(pl.multiple_of(place * size, 8), size)], out_sem.at[m, n]
                )
                for n, place in enumerate((col, 1 - col))
            ])

    wait([*col_loads, *loads[0]])
    start([copy for load in loads[1:] for copy in load] + edge_loads)
    for step in feature_steps(0):
        step()
    for k in range(count):
        ahead = []
        if k + 1 < count:
            wait(loads[k + 1])
            ahead = feature_steps(k + 1)
        elif last:
            wait(edge_loads)
            ahead = [functools.partial(edge_cols, n) for n in range(2)] + [functools.partial(edge_rows, u) for u in range(2)]
        for lag, n in ((0, 0), (0, 1), (LAG, 0), (LAG, 1)):
            if ahead:
                ahead.pop(0)()
            moment_tile(k, lag, n)
            if last and k == count - 1 and lag == 0 and n == 1:
                start(stores[0])
        for step in ahead:
            step()
    if last:
        moment_tile(count, LAG, 0)
        moment_tile(count, LAG, 1)
        start(stores[1])
        wait(stores[0] + stores[1])


def moments(slabs, count, numbers, ready, panels, acc, last, slab_rows, valid_rows):
    first = acc is None
    row_proj, row_off = panels[-2:] if first else panels[:2]
    rows, units = row_proj.shape
    cols = rows // 2
    at = len(slabs) - count
    ready_count = ready[0].shape[0] if first else 0
    if not last:
        slabs = slabs[at + ready_count:]
    pieces = [p for s in slabs for p in s]
    end_shape = (rows * cols // 128, 128)
    outs, out_specs = [pltpu.VMEM((rows, cols), jnp.float32)] * 2, [vmem_spec()] * 2
    dma = pltpu.SemaphoreType.DMA
    scratch = [
        pltpu.VMEM((count - ready_count, slab_rows, units), jnp.bfloat16),
        pltpu.VMEM((rows, slab_rows), jnp.bfloat16),
        pltpu.VMEM((rows, slab_rows), jnp.bfloat16),
        pltpu.VMEM((slab_rows + LAG, cols), jnp.bfloat16),
        pltpu.VMEM((slab_rows + LAG, cols), jnp.bfloat16),
        dma((count - ready_count, 2)),
    ]
    args = [numbers, *pieces]
    specs = [smem_spec()] + [any_spec()] * len(pieces)
    aliases = {}
    if first:
        args += [*map(in_vmem, ready), *panels[:2], in_vmem(row_proj), in_vmem(row_off)]
        specs += [vmem_spec()] * 2 + [any_spec()] * 2 + [vmem_spec()] * 2
        outs, out_specs = outs + [pltpu.VMEM((units + SPARE, cols), jnp.bfloat16)], out_specs + [vmem_spec()]
        scratch.append(dma)
    else:
        if last:
            outs, out_specs = [pltpu.HBM(end_shape, jnp.float32)] * 2 + outs, [hbm_spec()] * 2 + out_specs
            scratch += [pltpu.VMEM(end_shape, jnp.float32)] * 2
            scratch += [pltpu.VMEM((len(slabs), LAG, units), jnp.bfloat16)] * 2
            scratch += [dma((len(slabs), 2)), dma((2, 2))]
        args += [in_vmem(x) for x in (*panels, *acc)]
        specs += [vmem_spec()] * 5
        aliases = {len(args) - 2 + n: len(outs) - 2 + n for n in range(2)}
    return pl.pallas_call(
        functools.partial(moments_kernel, count, ready_count, at, first, last, slab_rows, valid_rows),
        in_specs=specs,
        out_specs=out_specs,
        out_shape=outs,
        scratch_shapes=scratch,
        input_output_aliases=aliases,
        compiler_params=pltpu.CompilerParams(vmem_limit_bytes=(24 if last else 18) * MIB),
        cost_estimate=pl.CostEstimate(
            flops=2 * count * slab_rows * (units * (rows + cols) + 2 * rows * cols),
            bytes_accessed=2 * count * slab_rows * units,
            transcendentals=count * slab_rows * (rows + cols),
        ),
    )(*args)


def on_device(states, projection, offsets):
    slab_rows = states.shape[0]
    tm_count = lax.axis_size("tm")
    tm, row, col = (lax.axis_index(a) for a in AXES)
    x_hi, y, core = tm // Y, tm % Y, row % 2
    valid_rows = slab_rows * tm_count - LAG
    cols = projection.shape[1]
    swap = lambda piece: move(piece, other_core)

    y_first, y_second = y - 1 + 2 * core, y + 1 - 2 * core
    place = lambda other, at: jnp.where(other, 1 - x_hi, x_hi) * Y + at % Y
    ids = [tm, place(False, y_first), place(False, y_second), place(True, y), place(False, y + 2),
           place(True, y_first), place(True, y_second), place(True, y + 2)]
    source, steps = jnp.where(core == y % 2, 0, 1), (row // 2 - tm // 2) % 4
    numbers = jnp.stack([*ids, core, col, source, steps]).astype(jnp.int32)
    after = len(ids)
    line = offsets[None, :]
    numbers, line = lax.optimization_barrier((numbers, line))
    sizes = (slab_rows, valid_rows)

    columns, turned, mine = prepare(after, numbers, projection, line, states)
    ahead, behind = move(columns, along_z(1)), move(columns, along_z(-1))
    over, partner, y_out = move(mine, crossing), move(turned, inner), move(mine, out_y)
    ahead, columns = lax.optimization_barrier((ahead, columns))
    beyond = move(columns, along_z(2))
    over, y_out, mine = lax.optimization_barrier((over, y_out, mine))
    y_back = move(mine, back_y)
    ahead, behind, beyond, over, partner, y_out = lax.optimization_barrier(
        (ahead, behind, beyond, over, partner, y_out)
    )

    panel = pick(after + 3, numbers, columns, ahead, beyond, behind)
    swapped = swap(panel)
    swapped_out, swapped_back, swapped_over = swap(y_out), swap(y_back), swap(over)
    slabs = [(in_hbm(states),), (y_out, swapped_back), (y_back, swapped_out)]
    row_proj, row_off, *ready = opening(slabs, numbers, turned, partner, line, *sizes)

    over_out, y_far, over_back = move(over, out_y), move(y_out, out_y), move(y_back, crossing)
    row_off, over_out = lax.optimization_barrier((row_off, over_out))
    over_far = move(over_out, out_y)
    slabs += [(over, swapped_over)]
    *acc, col_proj = moments(slabs, 4, numbers, ready, (panel, swapped, row_proj, row_off), None, False, *sizes)
    panels = (row_proj, row_off, col_proj)

    *acc, y_far, over_back, over_far = lax.optimization_barrier((*acc, y_far, over_back, over_far))
    slabs += [(y_far, swap(y_far)), (over_out, swap(over_back)), (over_back, swap(over_out)), (over_far, swap(over_far))]
    instant, lagged, *_ = moments(slabs, 4, numbers, None, panels, acc, True, *sizes)
    shape = (2 * cols, 1, cols)
    return instant.reshape(shape), lagged.reshape(shape)


def solution(mesh):
    return jax.shard_map(
        on_device,
        mesh=mesh,
        in_specs=(P("tm", None), P(None, ("row", "col")), P(("row", "col"))),
        out_specs=(P("row", "tm", "col"), P("row", "tm", "col")),
        check_vma=False,
    )
```

```python
import functools
import jax
import jax.numpy as jnp
from jax import lax
from jax.experimental import pallas as pl
from jax.experimental.pallas import tpu as pltpu
from jax.sharding import PartitionSpec as P

LAG = 64
Y = 4
AXES = ("tm", "row", "col")
SPARE = 16
MIB = 1024 * 1024


def route(target):
    tm_count, row_count, col_count = (lax.axis_size(a) for a in AXES)
    flat = lambda tm, row, col: (tm * row_count + row) * col_count + col
    pairs = []
    for tm in range(tm_count):
        for row in range(row_count):
            for col in range(col_count):
                to = target(tm // Y, tm % Y, row // 2, row % 2, col)
                if to is not None:
                    x_hi, y, z, core, x_lo = to
                    pairs.append((flat(tm, row, col), flat(x_hi * Y + y % Y, z * 2 + core, x_lo)))
    return pairs


def move(block, target):
    return lax.ppermute(block, AXES, route(target))


def crossing(x_hi, y, z, core, x_lo):
    return 1 - x_hi, y, z, core, 1 - x_lo


def inner(x_hi, y, z, core, x_lo):
    return x_hi, y, z, core, 1 - x_lo


def other_core(x_hi, y, z, core, x_lo):
    return x_hi, y, z, 1 - core, x_lo


def along_y(step):
    return lambda x_hi, y, z, core, x_lo: (x_hi, y + step, z, core, x_lo)


def out_y(x_hi, y, z, core, x_lo):
    return x_hi, y + 1 - 2 * core, z, core, x_lo


def back_y(x_hi, y, z, core, x_lo):
    return x_hi, y - 1 + 2 * core, z, core, x_lo


def along_z(step):
    def target(x_hi, y, z, core, x_lo):
        return (x_hi, y, (z + step) % 4, core, x_lo) if x_hi * Y + y == z * 2 + core else None
    return target


def any_spec():
    return pl.BlockSpec(memory_space=pl.ANY)


def vmem_spec():
    return pl.BlockSpec(memory_space=pltpu.VMEM)


def hbm_spec():
    return pl.BlockSpec(memory_space=pltpu.HBM)


def in_hbm(x):
    return pltpu.with_memory_space_constraint(x, pltpu.HBM)


def in_vmem(x):
    return pltpu.with_memory_space_constraint(x, pltpu.VMEM)


def smem_spec():
    return pl.BlockSpec(memory_space=pltpu.SMEM)


def row_features(row_proj, states, row_off, start, valid_rows):
    features = jnp.tanh(
        lax.dot_general(row_proj, states, (((1,), (1,)), ((), ())), preferred_element_type=jnp.float32) + row_off
    )
    position = start + lax.broadcasted_iota(jnp.int32, (1, states.shape[0]), 1)
    return jnp.where(position < valid_rows, features, 0.0).astype(jnp.bfloat16)


def col_features(states, col_proj, col_off):
    return jnp.tanh(
        jnp.dot(states, col_proj, preferred_element_type=jnp.float32) + col_off
    ).astype(jnp.bfloat16)


def prepare_kernel(at, numbers, projection, offsets, states, columns, turned, mine, sem):
    half = mine.shape[0]
    copy = pltpu.make_async_copy(states.at[pl.ds(pl.multiple_of(numbers[at] * half, 16), half)], mine, sem)
    copy.start()
    units, cols = projection.shape
    columns[:units] = projection[...]
    turned[:cols] = projection[...].T
    high = offsets[...].astype(jnp.bfloat16)
    rest = offsets[...] - high.astype(jnp.float32)
    middle = rest.astype(jnp.bfloat16)
    low = (rest - middle.astype(jnp.float32)).astype(jnp.bfloat16)
    parts = jnp.concatenate([high, middle, low, jnp.zeros((SPARE - 3, cols), jnp.bfloat16)], axis=0)
    columns[units:] = parts
    turned[cols:] = jnp.zeros_like(turned[cols:])
    turned[cols:, :cols] = parts
    copy.wait()


def prepare(at, numbers, projection, offsets, states):
    units, cols = projection.shape
    half = states.shape[0] // 2
    return pl.pallas_call(
        functools.partial(prepare_kernel, at),
        in_specs=[smem_spec(), vmem_spec(), vmem_spec(), hbm_spec()],
        out_specs=[vmem_spec(), vmem_spec(), vmem_spec()],
        out_shape=[jax.ShapeDtypeStruct((units + SPARE, cols), jnp.bfloat16),
                   jax.ShapeDtypeStruct((cols + SPARE, units), jnp.bfloat16),
                   jax.ShapeDtypeStruct((half, units), jnp.bfloat16)],
        scratch_shapes=[pltpu.SemaphoreType.DMA],
        compiler_params=pltpu.CompilerParams(vmem_limit_bytes=12 * MIB),
    )(numbers, projection, offsets, in_hbm(states))


class OneOf:
    def __init__(self, number, sources, dst, sem):
        self.number, self.copies = number, [pltpu.make_async_copy(x, dst, sem) for x in sources]

    def start(self):
        for n, copy in enumerate(self.copies):
            pl.when(self.number == n)(copy.start)

    def wait(self):
        self.copies[0].wait()


def pick_kernel(at, numbers, *refs):
    *sources, out, sem = refs
    copy = OneOf(numbers[at], sources, out, sem)
    copy.start()
    copy.wait()


def pick(at, numbers, *sources):
    return pl.pallas_call(
        functools.partial(pick_kernel, at),
        in_specs=[smem_spec()] + [any_spec()] * len(sources),
        out_specs=vmem_spec(),
        out_shape=jax.ShapeDtypeStruct(sources[0].shape, sources[0].dtype),
        scratch_shapes=[pltpu.SemaphoreType.DMA],
        compiler_params=pltpu.CompilerParams(vmem_limit_bytes=8 * MIB),
    )(numbers, *sources)


def slab_copies(pieces, core, dst, sems):
    if len(pieces) == 1:
        return [pltpu.make_async_copy(pieces[0], dst, sems.at[0])]
    half = pieces[0].shape[0]
    return [
        pltpu.make_async_copy(piece, dst.at[pl.ds(pl.multiple_of(place * half, 16), half)], sems.at[n])
        for n, (piece, place) in enumerate(zip(pieces, (core, 1 - core)))
    ]


def start(copies):
    for copy in copies:
        copy.start()


def wait(copies):
    for copy in copies:
        copy.wait()


def opening_kernel(count, valid_rows, ids, *refs):
    refs = list(refs)
    take = lambda n: [refs.pop(0) for _ in range(n)]
    pieces = [take(1 if k == 0 else 2) for k in range(count)]
    turned, partner, offsets = take(3)
    row_proj, row_off, slab, features, parts, proj_sem, in_sem = take(7)
    rows = row_proj.shape[0]
    own, slab_rows = rows // 2, slab.shape[1]
    core = ids[(valid_rows + LAG) // slab_rows]
    row_loads = [
        pltpu.make_async_copy(turned.at[pl.ds(0, own)], row_proj.at[pl.ds(0, own)], proj_sem.at[0]),
        pltpu.make_async_copy(partner.at[pl.ds(0, own)], row_proj.at[pl.ds(own, own)], proj_sem.at[1]),
        pltpu.make_async_copy(partner.at[pl.ds(own, SPARE)], parts, proj_sem.at[2]),
    ]
    loads = [slab_copies(pieces[k], core, slab.at[k], in_sem.at[k]) for k in range(count)]
    start([*row_loads, *loads[0]])
    turn = lambda line: jnp.broadcast_to(line, (8, own)).T[:, :1]
    row_off[:own] = turn(offsets[...])
    wait(row_loads)
    start([copy for load in loads[1:] for copy in load])
    row_off[own:] = turn(jnp.sum(parts[:, :own].astype(jnp.float32), axis=0, keepdims=True))
    tile = slab_rows // 3
    for k in range(count):
        wait(loads[k])
        for u in range(3):
            span = slice(u * tile, (u + 1) * tile)
            for part in (slice(0, own), slice(own, rows)):
                features[k, part, span] = row_features(
                    row_proj[part], slab[k, span], row_off[part], ids[k] * slab_rows + u * tile, valid_rows
                )


def opening(slabs, numbers, turned, partner, offsets, slab_rows, valid_rows):
    rows, units, count = 2 * (turned.shape[0] - SPARE), turned.shape[1], len(slabs)
    pieces = [p for s in slabs for p in s]
    dma = pltpu.SemaphoreType.DMA
    return pl.pallas_call(
        functools.partial(opening_kernel, count, valid_rows),
        in_specs=[smem_spec()] + [any_spec()] * (len(pieces) + 2) + [vmem_spec()],
        out_specs=[vmem_spec()] * 4,
        out_shape=[
            pltpu.VMEM((rows, units), jnp.bfloat16),
            pltpu.VMEM((rows, 1), jnp.float32),
            pltpu.VMEM((count, slab_rows, units), jnp.bfloat16),
            pltpu.VMEM((count, rows, slab_rows), jnp.bfloat16),
        ],
        scratch_shapes=[pltpu.VMEM((SPARE, units), jnp.bfloat16), dma((3,)), dma((count, 2))],
        compiler_params=pltpu.CompilerParams(vmem_limit_bytes=12 * MIB),
        cost_estimate=pl.CostEstimate(
            flops=2 * count * slab_rows * units * rows, bytes_accessed=2 * count * slab_rows * units,
            transcendentals=count * slab_rows * rows,
        ),
    )(numbers, *pieces, turned, partner, offsets)


def moments_kernel(count, ready, at, first, last, slab_rows, valid_rows, *refs):
    refs = list(refs)
    take = lambda n: [refs.pop(0) for _ in range(n)]
    (ids,) = take(1)
    slabs = (valid_rows + LAG) // slab_rows
    pieces = [take(1 if last and k == 0 else 2) for k in range(slabs if last else count - ready)]
    here = [None] * ready + pieces[ready - count:]
    if first:
        ready_slab, ready_rows, *columns, row_proj, row_off = take(6)
        instant, lagged, col_proj = take(3)
    else:
        row_proj, row_off, col_proj = take(3)
        take(2)
        if last:
            acc_out = take(2)
        instant, lagged = take(2)
    slab, row_a, row_b, col_a, col_b, in_sem = take(6)
    if first:
        (proj_sem,) = take(1)
    if last:
        instant_end, lagged_end, tails, heads, edge_sem, out_sem = take(6)
    rows, cols = instant.shape
    units = col_proj.shape[0] - SPARE
    half = slab_rows // 2
    time_tile, col_tile = slab_rows // 3, cols // 2
    core, col, source = ids[slabs], ids[slabs + 1], ids[slabs + 2]
    number = lambda k: ids[at + k]

    loads = [[] if k < ready else slab_copies(here[k], core, slab.at[k - ready], in_sem.at[k - ready]) for k in range(count)]
    states = lambda k: ready_slab.at[k] if k < ready else slab.at[k - ready]
    rows_of = lambda k: ready_rows.at[k] if k < ready else row_bufs[k % 2]
    col_loads, edge_loads = [], []
    if first:
        col_loads = [OneOf(source, columns, col_proj, proj_sem)]
    if last:
        for k, piece in enumerate(pieces):
            tail, head = tails.at[ids[k]], heads.at[lax.rem(ids[k] + slabs - 1, slabs)]
            if len(piece) == 1:
                edge_loads.append(pltpu.make_async_copy(piece[0].at[pl.ds(slab_rows - LAG, LAG)], tail, edge_sem.at[k, 0]))
                edge_loads.append(pltpu.make_async_copy(piece[0].at[pl.ds(0, LAG)], head, edge_sem.at[k, 1]))
            else:
                ends = [p.at[pl.ds(half - LAG, LAG)] for p in piece]
                starts = [p.at[pl.ds(0, LAG)] for p in piece]
                edge_loads.append(OneOf(1 - core, ends, tail, edge_sem.at[k, 0]))
                edge_loads.append(OneOf(core, starts, head, edge_sem.at[k, 1]))
    start([*col_loads, *loads[0]])

    row_bufs, col_bufs = (row_a, row_b), (col_a, col_b)
    for buf in col_bufs:
        buf[slab_rows:] = jnp.zeros_like(buf[slab_rows:])

    row_part = lambda h: slice(h * rows // 2, (h + 1) * rows // 2)

    def row_tile(k, u, h):
        span, part = slice(u * time_tile, (u + 1) * time_tile), row_part(h)
        row_bufs[k % 2][part, span] = row_features(
            row_proj[part], states(k)[span], row_off[part], number(k) * slab_rows + u * time_tile, valid_rows
        )

    def col_off(span):
        return jnp.sum(col_proj[units:, span].astype(jnp.float32), axis=0, keepdims=True)

    def col_tile_features(k, n, h):
        span, part = slice(n * col_tile, (n + 1) * col_tile), slice(h * half, (h + 1) * half)
        col_bufs[k % 2][part, span] = col_features(states(k)[part], col_proj[:units, span], col_off(span))

    def edge_rows(u, h):
        tile, part = slabs * LAG // 2, row_part(h)
        ends = tails[u * slabs // 2:(u + 1) * slabs // 2].reshape(tile, units)
        row_bufs[count % 2][part, u * tile:(u + 1) * tile] = row_features(
            row_proj[part], ends, row_off[part], u * tile, (slabs - 1) * LAG
        )

    def edge_cols(n):
        span = slice(n * col_tile, (n + 1) * col_tile)
        col_bufs[count % 2][:slabs * LAG, span] = col_features(
            heads[...].reshape(slabs * LAG, units), col_proj[:units, span], col_off(span)
        )

    def moment_tile(k, lag, n, h):
        span, part = slice(n * col_tile, (n + 1) * col_tile), row_part(h)
        acc = lagged if lag else instant
        buf_r, buf_c = row_bufs[k % 2] if k == count else rows_of(k), col_bufs[k % 2]
        if k < count:
            value = jnp.dot(buf_r[part], buf_c[lag:lag + slab_rows, span], preferred_element_type=jnp.float32)
        else:
            value = jnp.dot(buf_r[part, :slabs * LAG], buf_c[:slabs * LAG, span], preferred_element_type=jnp.float32)
        if k > 0 or not first:
            value = acc[part, span] + value
        if last and k == (count if lag else count - 1):
            end = lagged_end if lag else instant_end
            value = value * (1.0 / valid_rows)
            groups = cols // 128
            for g in range(col_tile // 128):
                at = h * (rows // 2) * groups + n * (col_tile // 128) + g
                end[pl.ds(at, rows // 2, stride=groups), :] = value[:, g * 128:(g + 1) * 128]
            if n == 1:
                start([stores[1 if lag else 0][h]])
        else:
            acc[part, span] = value

    def feature_steps(k):
        steps = [functools.partial(col_tile_features, k, n, h) for n in range(2) for h in range(2)]
        if k >= ready:
            steps += [functools.partial(row_tile, k, u, h) for u in range(3) for h in range(2)]
        return steps

    def interleave(steps, others):
        done = 0
        for n, step in enumerate(steps):
            upto = (n + 1) * len(others) // len(steps)
            for other in others[done:upto]:
                other()
            done = upto
            step()

    stores = []
    if last:
        for m, (a, b) in enumerate(zip((instant_end, lagged_end), acc_out)):
            size = a.shape[0] // 2
            stores.append([
                pltpu.make_async_copy(
                    a.at[pl.ds(n * size, size)], b.at[pl.ds(pl.multiple_of(place * size, 8), size)], out_sem.at[m, n]
                )
                for n, place in enumerate((col, 1 - col))
            ])

    wait([*col_loads, *loads[0]])
    start([copy for load in loads[1:] for copy in load] + edge_loads)
    for step in feature_steps(0):
        step()
    for k in range(count):
        ahead = []
        if k + 1 < count:
            wait(loads[k + 1])
            ahead = feature_steps(k + 1)
        elif last:
            wait(edge_loads)
            ahead = [functools.partial(edge_cols, n) for n in range(2)]
            ahead += [functools.partial(edge_rows, u, h) for u in range(2) for h in range(2)]
        interleave(
            [functools.partial(moment_tile, k, lag, n, h) for lag in (0, LAG) for h in range(2) for n in range(2)], ahead
        )
    if last:
        for h in range(2):
            for n in range(2):
                moment_tile(count, LAG, n, h)
        wait(stores[0] + stores[1])


def moments(slabs, count, numbers, ready, panels, acc, last, slab_rows, valid_rows):
    first = acc is None
    row_proj, row_off = panels[-2:] if first else panels[:2]
    rows, units = row_proj.shape
    cols = rows // 2
    at = len(slabs) - count
    ready_count = ready[0].shape[0] if first else 0
    if not last:
        slabs = slabs[at + ready_count:]
    pieces = [p for s in slabs for p in s]
    end_shape = (rows * cols // 128, 128)
    outs, out_specs = [pltpu.VMEM((rows, cols), jnp.float32)] * 2, [vmem_spec()] * 2
    dma = pltpu.SemaphoreType.DMA
    scratch = [
        pltpu.VMEM((count - ready_count, slab_rows, units), jnp.bfloat16),
        pltpu.VMEM((rows, slab_rows), jnp.bfloat16),
        pltpu.VMEM((rows, slab_rows), jnp.bfloat16),
        pltpu.VMEM((slab_rows + LAG, cols), jnp.bfloat16),
        pltpu.VMEM((slab_rows + LAG, cols), jnp.bfloat16),
        dma((count - ready_count, 2)),
    ]
    args = [numbers, *pieces]
    specs = [smem_spec()] + [any_spec()] * len(pieces)
    aliases = {}
    if first:
        args += [*map(in_vmem, ready), *panels[:2], in_vmem(row_proj), in_vmem(row_off)]
        specs += [vmem_spec()] * 2 + [any_spec()] * 2 + [vmem_spec()] * 2
        outs, out_specs = outs + [pltpu.VMEM((units + SPARE, cols), jnp.bfloat16)], out_specs + [vmem_spec()]
        scratch.append(dma)
    else:
        if last:
            outs, out_specs = [pltpu.HBM(end_shape, jnp.float32)] * 2 + outs, [hbm_spec()] * 2 + out_specs
            scratch += [pltpu.VMEM(end_shape, jnp.float32)] * 2
            scratch += [pltpu.VMEM((len(slabs), LAG, units), jnp.bfloat16)] * 2
            scratch += [dma((len(slabs), 2)), dma((2, 2))]
        args += [in_vmem(x) for x in (*panels, *acc)]
        specs += [vmem_spec()] * 5
        aliases = {len(args) - 2 + n: len(outs) - 2 + n for n in range(2)}
    return pl.pallas_call(
        functools.partial(moments_kernel, count, ready_count, at, first, last, slab_rows, valid_rows),
        in_specs=specs,
        out_specs=out_specs,
        out_shape=outs,
        scratch_shapes=scratch,
        input_output_aliases=aliases,
        compiler_params=pltpu.CompilerParams(vmem_limit_bytes=(24 if last else 18) * MIB),
        cost_estimate=pl.CostEstimate(
            flops=2 * count * slab_rows * (units * (rows + cols) + 2 * rows * cols),
            bytes_accessed=2 * count * slab_rows * units,
            transcendentals=count * slab_rows * (rows + cols),
        ),
    )(*args)


def on_device(states, projection, offsets):
    slab_rows = states.shape[0]
    tm_count = lax.axis_size("tm")
    tm, row, col = (lax.axis_index(a) for a in AXES)
    x_hi, y, core = tm // Y, tm % Y, row % 2
    valid_rows = slab_rows * tm_count - LAG
    cols = projection.shape[1]
    swap = lambda piece: move(piece, other_core)

    y_first, y_second = y - 1 + 2 * core, y + 1 - 2 * core
    place = lambda other, at: jnp.where(other, 1 - x_hi, x_hi) * Y + at % Y
    ids = [tm, place(False, y_first), place(False, y_second), place(True, y), place(False, y + 2),
           place(True, y_first), place(True, y_second), place(True, y + 2)]
    source, steps = jnp.where(core == y % 2, 0, 1), (row // 2 - tm // 2) % 4
    numbers = jnp.stack([*ids, core, col, source, steps]).astype(jnp.int32)
    after = len(ids)
    line = offsets[None, :]
    numbers, line = lax.optimization_barrier((numbers, line))
    sizes = (slab_rows, valid_rows)

    columns, turned, mine = prepare(after, numbers, projection, line, states)
    ahead, behind = move(columns, along_z(1)), move(columns, along_z(-1))
    over, partner, y_out = move(mine, crossing), move(turned, inner), move(mine, out_y)
    ahead, columns = lax.optimization_barrier((ahead, columns))
    beyond = move(columns, along_z(2))
    y_out, mine = lax.optimization_barrier((y_out, mine))
    y_back = move(mine, back_y)
    over, y_out = lax.optimization_barrier((over, y_out))
    swapped_out = swap(y_out)
    ahead, behind, beyond, partner, y_back, swapped_out = lax.optimization_barrier(
        (ahead, behind, beyond, partner, y_back, swapped_out)
    )

    panel = pick(after + 3, numbers, columns, ahead, beyond, behind)
    swapped = swap(panel)
    swapped_back, swapped_over = swap(y_back), swap(over)
    slabs = [(in_hbm(states),), (y_out, swapped_back), (y_back, swapped_out)]
    row_proj, row_off, *ready = opening(slabs, numbers, turned, partner, line, *sizes)

    over_out, y_far, over_back = move(over, out_y), move(y_out, out_y), move(y_back, crossing)
    row_off, over_out = lax.optimization_barrier((row_off, over_out))
    over_far = move(over_out, out_y)
    slabs += [(over, swapped_over)]
    *acc, col_proj = moments(slabs, 4, numbers, ready, (panel, swapped, row_proj, row_off), None, False, *sizes)
    panels = (row_proj, row_off, col_proj)

    *acc, y_far, over_back, over_far = lax.optimization_barrier((*acc, y_far, over_back, over_far))
    slabs += [(y_far, swap(y_far)), (over_out, swap(over_back)), (over_back, swap(over_out)), (over_far, swap(over_far))]
    instant, lagged, *_ = moments(slabs, 4, numbers, None, panels, acc, True, *sizes)
    shape = (2 * cols, 1, cols)
    return instant.reshape(shape), lagged.reshape(shape)


def solution(mesh):
    return jax.shard_map(
        on_device,
        mesh=mesh,
        in_specs=(P("tm", None), P(None, ("row", "col")), P(("row", "col"))),
        out_specs=(P("row", "tm", "col"), P("row", "tm", "col")),
        check_vma=False,
    )
```

```python
import functools
import jax
import jax.numpy as jnp
from jax import lax
from jax.experimental import pallas as pl
from jax.experimental.pallas import tpu as pltpu
from jax.sharding import PartitionSpec as P

LAG = 64
Y = 4
AXES = ("tm", "row", "col")
SPARE = 16
MIB = 1024 * 1024


def route(target):
    tm_count, row_count, col_count = (lax.axis_size(a) for a in AXES)
    flat = lambda tm, row, col: (tm * row_count + row) * col_count + col
    pairs = []
    for tm in range(tm_count):
        for row in range(row_count):
            for col in range(col_count):
                to = target(tm // Y, tm % Y, row // 2, row % 2, col)
                if to is not None:
                    x_hi, y, z, core, x_lo = to
                    pairs.append((flat(tm, row, col), flat(x_hi * Y + y % Y, z * 2 + core, x_lo)))
    return pairs


def move(block, target):
    return lax.ppermute(block, AXES, route(target))


def crossing(x_hi, y, z, core, x_lo):
    return 1 - x_hi, y, z, core, 1 - x_lo


def inner(x_hi, y, z, core, x_lo):
    return x_hi, y, z, core, 1 - x_lo


def other_core(x_hi, y, z, core, x_lo):
    return x_hi, y, z, 1 - core, x_lo


def along_y(step):
    return lambda x_hi, y, z, core, x_lo: (x_hi, y + step, z, core, x_lo)


def out_y(x_hi, y, z, core, x_lo):
    return x_hi, y + 1 - 2 * core, z, core, x_lo


def back_y(x_hi, y, z, core, x_lo):
    return x_hi, y - 1 + 2 * core, z, core, x_lo


def along_z(step):
    def target(x_hi, y, z, core, x_lo):
        return (x_hi, y, (z + step) % 4, core, x_lo) if x_hi * Y + y == z * 2 + core else None
    return target


def any_spec():
    return pl.BlockSpec(memory_space=pl.ANY)


def vmem_spec():
    return pl.BlockSpec(memory_space=pltpu.VMEM)


def hbm_spec():
    return pl.BlockSpec(memory_space=pltpu.HBM)


def in_hbm(x):
    return pltpu.with_memory_space_constraint(x, pltpu.HBM)


def in_vmem(x):
    return pltpu.with_memory_space_constraint(x, pltpu.VMEM)


def smem_spec():
    return pl.BlockSpec(memory_space=pltpu.SMEM)


def row_features(row_proj, turned, row_off, start, valid_rows):
    features = jnp.tanh(jnp.dot(row_proj, turned, preferred_element_type=jnp.float32) + row_off)
    position = start + lax.broadcasted_iota(jnp.int32, (1, turned.shape[1]), 1)
    return jnp.where(position < valid_rows, features, 0.0).astype(jnp.bfloat16)


def col_features(states, col_proj, col_off):
    return jnp.tanh(
        jnp.dot(states, col_proj, preferred_element_type=jnp.float32) + col_off
    ).astype(jnp.bfloat16)


def start(copies):
    for copy in copies:
        copy.start()


def wait(copies):
    for copy in copies:
        copy.wait()


def prepare_kernel(at, numbers, projection, offsets, states, columns, turned, mine, line, sems):
    half = mine.shape[0]
    units, cols = projection.shape
    copies = [
        pltpu.make_async_copy(projection, columns.at[pl.ds(0, units)], sems.at[0]),
        pltpu.make_async_copy(offsets, line, sems.at[1]),
        pltpu.make_async_copy(states.at[pl.ds(pl.multiple_of(numbers[at] * half, 16), half)], mine, sems.at[2]),
    ]
    start(copies)
    turned[cols:] = jnp.zeros_like(turned[cols:])
    wait(copies[1:2])
    high = line[...].astype(jnp.bfloat16)
    rest = line[...] - high.astype(jnp.float32)
    middle = rest.astype(jnp.bfloat16)
    low = (rest - middle.astype(jnp.float32)).astype(jnp.bfloat16)
    parts = jnp.concatenate([high, middle, low, jnp.zeros((SPARE - 3, cols), jnp.bfloat16)], axis=0)
    columns[units:] = parts
    turned[cols:, :cols] = parts
    wait(copies[:1])
    turned[:cols] = columns[:units].T
    wait(copies[2:])


def prepare(at, numbers, projection, offsets, states):
    units, cols = projection.shape
    half = states.shape[0] // 2
    return pl.pallas_call(
        functools.partial(prepare_kernel, at),
        in_specs=[smem_spec(), hbm_spec(), hbm_spec(), hbm_spec()],
        out_specs=[vmem_spec(), vmem_spec(), vmem_spec()],
        out_shape=[jax.ShapeDtypeStruct((units + SPARE, cols), jnp.bfloat16),
                   jax.ShapeDtypeStruct((cols + SPARE, units), jnp.bfloat16),
                   jax.ShapeDtypeStruct((half, units), jnp.bfloat16)],
        scratch_shapes=[pltpu.VMEM((1, cols), jnp.float32), pltpu.SemaphoreType.DMA((3,))],
        compiler_params=pltpu.CompilerParams(vmem_limit_bytes=12 * MIB),
    )(numbers, in_hbm(projection), in_hbm(offsets), in_hbm(states))


class OneOf:
    def __init__(self, number, sources, dst, sem):
        self.number, self.copies = number, [pltpu.make_async_copy(x, dst, sem) for x in sources]

    def start(self):
        for n, copy in enumerate(self.copies):
            pl.when(self.number == n)(copy.start)

    def wait(self):
        self.copies[0].wait()


def pick_kernel(at, numbers, *refs):
    *sources, out, sem = refs
    copy = OneOf(numbers[at], sources, out, sem)
    copy.start()
    copy.wait()


def pick(at, numbers, *sources):
    return pl.pallas_call(
        functools.partial(pick_kernel, at),
        in_specs=[smem_spec()] + [any_spec()] * len(sources),
        out_specs=vmem_spec(),
        out_shape=jax.ShapeDtypeStruct(sources[0].shape, sources[0].dtype),
        scratch_shapes=[pltpu.SemaphoreType.DMA],
        compiler_params=pltpu.CompilerParams(vmem_limit_bytes=8 * MIB),
    )(numbers, *sources)


def slab_copies(pieces, core, dst, sems):
    if len(pieces) == 1:
        return [pltpu.make_async_copy(pieces[0], dst, sems.at[0])]
    half = pieces[0].shape[0]
    return [
        pltpu.make_async_copy(piece, dst.at[pl.ds(pl.multiple_of(place * half, 16), half)], sems.at[n])
        for n, (piece, place) in enumerate(zip(pieces, (core, 1 - core)))
    ]


def opening_kernel(count, valid_rows, ids, *refs):
    refs = list(refs)
    take = lambda n: [refs.pop(0) for _ in range(n)]
    pieces = [take(1 if k == 0 else 2) for k in range(count)]
    turned, partner, offsets = take(3)
    row_proj, row_off, slab, features, parts, proj_sem, in_sem = take(7)
    rows = row_proj.shape[0]
    own, slab_rows = rows // 2, slab.shape[1]
    core = ids[(valid_rows + LAG) // slab_rows]
    row_loads = [
        pltpu.make_async_copy(turned.at[pl.ds(0, own)], row_proj.at[pl.ds(0, own)], proj_sem.at[0]),
        pltpu.make_async_copy(partner.at[pl.ds(0, own)], row_proj.at[pl.ds(own, own)], proj_sem.at[1]),
        pltpu.make_async_copy(partner.at[pl.ds(own, SPARE)], parts, proj_sem.at[2]),
    ]
    loads = [slab_copies(pieces[k], core, slab.at[k], in_sem.at[k]) for k in range(count)]
    start([*row_loads, *loads[0]])
    turn = lambda line: jnp.broadcast_to(line, (8, own)).T[:, :1]
    row_off[:own] = turn(offsets[...])
    wait(row_loads)
    start([copy for load in loads[1:] for copy in load])
    row_off[own:] = turn(jnp.sum(parts[:, :own].astype(jnp.float32), axis=0, keepdims=True))
    tile = slab_rows // 3
    for k in range(count):
        wait(loads[k])
        for u in range(3):
            span = slice(u * tile, (u + 1) * tile)
            turned_states = slab[k, span].T
            for part in (slice(0, own), slice(own, rows)):
                features[k, part, span] = row_features(
                    row_proj[part], turned_states, row_off[part], ids[k] * slab_rows + u * tile, valid_rows
                )


def opening(slabs, numbers, turned, partner, offsets, slab_rows, valid_rows):
    rows, units, count = 2 * (turned.shape[0] - SPARE), turned.shape[1], len(slabs)
    pieces = [p for s in slabs for p in s]
    dma = pltpu.SemaphoreType.DMA
    return pl.pallas_call(
        functools.partial(opening_kernel, count, valid_rows),
        in_specs=[smem_spec()] + [any_spec()] * (len(pieces) + 2) + [vmem_spec()],
        out_specs=[vmem_spec()] * 4,
        out_shape=[
            pltpu.VMEM((rows, units), jnp.bfloat16),
            pltpu.VMEM((rows, 1), jnp.float32),
            pltpu.VMEM((count, slab_rows, units), jnp.bfloat16),
            pltpu.VMEM((count, rows, slab_rows), jnp.bfloat16),
        ],
        scratch_shapes=[pltpu.VMEM((SPARE, units), jnp.bfloat16), dma((3,)), dma((count, 2))],
        compiler_params=pltpu.CompilerParams(vmem_limit_bytes=12 * MIB),
        cost_estimate=pl.CostEstimate(
            flops=2 * count * slab_rows * units * rows, bytes_accessed=2 * count * slab_rows * units,
            transcendentals=count * slab_rows * rows,
        ),
    )(numbers, *pieces, turned, partner, offsets)


def moments_kernel(count, ready, at, first, last, slab_rows, valid_rows, *refs):
    refs = list(refs)
    take = lambda n: [refs.pop(0) for _ in range(n)]
    (ids,) = take(1)
    slabs = (valid_rows + LAG) // slab_rows
    pieces = [take(1 if last and k == 0 else 2) for k in range(slabs if last else count - ready)]
    here = [None] * ready + pieces[ready - count:]
    if first:
        ready_slab, ready_rows, *columns, row_proj, row_off = take(6)
        instant, lagged, col_proj = take(3)
    else:
        row_proj, row_off, col_proj = take(3)
        take(2)
        if last:
            acc_out = take(2)
        instant, lagged = take(2)
    slab, turned_states, row_a, row_b, col_a, col_b, in_sem = take(7)
    if first:
        (proj_sem,) = take(1)
    if last:
        instant_end, lagged_end, tails, heads, edge_sem, out_sem = take(6)
    rows, cols = instant.shape
    units = col_proj.shape[0] - SPARE
    half = slab_rows // 2
    time_tile, col_tile = slab_rows // 3, cols // 2
    core, col, source = ids[slabs], ids[slabs + 1], ids[slabs + 2]
    number = lambda k: ids[at + k]

    loads = [[] if k < ready else slab_copies(here[k], core, slab.at[k - ready], in_sem.at[k - ready]) for k in range(count)]
    states = lambda k: ready_slab.at[k] if k < ready else slab.at[k - ready]
    rows_of = lambda k: ready_rows.at[k] if k < ready else row_bufs[k % 2]
    col_loads, edge_loads = [], []
    if first:
        col_loads = [OneOf(source, columns, col_proj, proj_sem)]
    if last:
        for k, piece in enumerate(pieces):
            tail, head = tails.at[ids[k]], heads.at[lax.rem(ids[k] + slabs - 1, slabs)]
            if len(piece) == 1:
                edge_loads.append(pltpu.make_async_copy(piece[0].at[pl.ds(slab_rows - LAG, LAG)], tail, edge_sem.at[k, 0]))
                edge_loads.append(pltpu.make_async_copy(piece[0].at[pl.ds(0, LAG)], head, edge_sem.at[k, 1]))
            else:
                ends = [p.at[pl.ds(half - LAG, LAG)] for p in piece]
                starts = [p.at[pl.ds(0, LAG)] for p in piece]
                edge_loads.append(OneOf(1 - core, ends, tail, edge_sem.at[k, 0]))
                edge_loads.append(OneOf(core, starts, head, edge_sem.at[k, 1]))
    start([*col_loads, *loads[0]])

    row_bufs, col_bufs = (row_a, row_b), (col_a, col_b)
    for buf in col_bufs:
        buf[slab_rows:] = jnp.zeros_like(buf[slab_rows:])

    row_part = lambda h: slice(h * rows // 2, (h + 1) * rows // 2)

    def row_tile(k, u, h):
        span, part = slice(u * time_tile, (u + 1) * time_tile), row_part(h)
        if h == 0:
            turned_states[...] = states(k)[span].T
        row_bufs[k % 2][part, span] = row_features(
            row_proj[part], turned_states[...], row_off[part], number(k) * slab_rows + u * time_tile, valid_rows
        )

    def col_off(span):
        return jnp.sum(col_proj[units:, span].astype(jnp.float32), axis=0, keepdims=True)

    def col_tile_features(k, n, h):
        span, part = slice(n * col_tile, (n + 1) * col_tile), slice(h * half, (h + 1) * half)
        col_bufs[k % 2][part, span] = col_features(states(k)[part], col_proj[:units, span], col_off(span))

    def edge_rows(u, h):
        tile, part = slabs * LAG // 2, row_part(h)
        if h == 0:
            turned_states[...] = tails[u * slabs // 2:(u + 1) * slabs // 2].reshape(tile, units).T
        row_bufs[count % 2][part, u * tile:(u + 1) * tile] = row_features(
            row_proj[part], turned_states[...], row_off[part], u * tile, (slabs - 1) * LAG
        )

    def edge_cols(n):
        span = slice(n * col_tile, (n + 1) * col_tile)
        col_bufs[count % 2][:slabs * LAG, span] = col_features(
            heads[...].reshape(slabs * LAG, units), col_proj[:units, span], col_off(span)
        )

    def moment_tile(k, lag, n, h):
        span, part = slice(n * col_tile, (n + 1) * col_tile), row_part(h)
        acc = lagged if lag else instant
        buf_r, buf_c = row_bufs[k % 2] if k == count else rows_of(k), col_bufs[k % 2]
        if k < count:
            value = jnp.dot(buf_r[part], buf_c[lag:lag + slab_rows, span], preferred_element_type=jnp.float32)
        else:
            value = jnp.dot(buf_r[part, :slabs * LAG], buf_c[:slabs * LAG, span], preferred_element_type=jnp.float32)
        if k > 0 or not first:
            value = acc[part, span] + value
        if last and k == (count if lag else count - 1):
            end = lagged_end if lag else instant_end
            value = value * (1.0 / valid_rows)
            groups = cols // 128
            for g in range(col_tile // 128):
                at = h * (rows // 2) * groups + n * (col_tile // 128) + g
                end[pl.ds(at, rows // 2, stride=groups), :] = value[:, g * 128:(g + 1) * 128]
            if n == 1:
                start([stores[1 if lag else 0][h]])
        else:
            acc[part, span] = value

    def feature_steps(k):
        steps = [functools.partial(col_tile_features, k, n, h) for n in range(2) for h in range(2)]
        if k >= ready:
            steps += [functools.partial(row_tile, k, u, h) for u in range(3) for h in range(2)]
        return steps

    def interleave(steps, others):
        done = 0
        for n, step in enumerate(steps):
            upto = (n + 1) * len(others) // len(steps)
            for other in others[done:upto]:
                other()
            done = upto
            step()

    stores = []
    if last:
        for m, (a, b) in enumerate(zip((instant_end, lagged_end), acc_out)):
            size = a.shape[0] // 2
            stores.append([
                pltpu.make_async_copy(
                    a.at[pl.ds(n * size, size)], b.at[pl.ds(pl.multiple_of(place * size, 8), size)], out_sem.at[m, n]
                )
                for n, place in enumerate((col, 1 - col))
            ])

    wait([*col_loads, *loads[0]])
    start([copy for load in loads[1:] for copy in load] + edge_loads)
    for step in feature_steps(0):
        step()
    for k in range(count):
        ahead = []
        if k + 1 < count:
            wait(loads[k + 1])
            ahead = feature_steps(k + 1)
        elif last:
            wait(edge_loads)
            ahead = [functools.partial(edge_cols, n) for n in range(2)]
            ahead += [functools.partial(edge_rows, u, h) for u in range(2) for h in range(2)]
        interleave(
            [functools.partial(moment_tile, k, lag, n, h) for lag in (0, LAG) for h in range(2) for n in range(2)], ahead
        )
    if last:
        for h in range(2):
            for n in range(2):
                moment_tile(count, LAG, n, h)
        wait(stores[0] + stores[1])


def moments(slabs, count, numbers, ready, panels, acc, last, slab_rows, valid_rows):
    first = acc is None
    row_proj, row_off = panels[-2:] if first else panels[:2]
    rows, units = row_proj.shape
    cols = rows // 2
    at = len(slabs) - count
    ready_count = ready[0].shape[0] if first else 0
    if not last:
        slabs = slabs[at + ready_count:]
    pieces = [p for s in slabs for p in s]
    end_shape = (rows * cols // 128, 128)
    outs, out_specs = [pltpu.VMEM((rows, cols), jnp.float32)] * 2, [vmem_spec()] * 2
    dma = pltpu.SemaphoreType.DMA
    scratch = [
        pltpu.VMEM((count - ready_count, slab_rows, units), jnp.bfloat16),
        pltpu.VMEM((units, slab_rows // 3), jnp.bfloat16),
        pltpu.VMEM((rows, slab_rows), jnp.bfloat16),
        pltpu.VMEM((rows, slab_rows), jnp.bfloat16),
        pltpu.VMEM((slab_rows + LAG, cols), jnp.bfloat16),
        pltpu.VMEM((slab_rows + LAG, cols), jnp.bfloat16),
        dma((count - ready_count, 2)),
    ]
    args = [numbers, *pieces]
    specs = [smem_spec()] + [any_spec()] * len(pieces)
    aliases = {}
    if first:
        args += [*map(in_vmem, ready), *panels[:2], in_vmem(row_proj), in_vmem(row_off)]
        specs += [vmem_spec()] * 2 + [any_spec()] * 2 + [vmem_spec()] * 2
        outs, out_specs = outs + [pltpu.VMEM((units + SPARE, cols), jnp.bfloat16)], out_specs + [vmem_spec()]
        scratch.append(dma)
    else:
        if last:
            outs, out_specs = [pltpu.HBM(end_shape, jnp.float32)] * 2 + outs, [hbm_spec()] * 2 + out_specs
            scratch += [pltpu.VMEM(end_shape, jnp.float32)] * 2
            scratch += [pltpu.VMEM((len(slabs), LAG, units), jnp.bfloat16)] * 2
            scratch += [dma((len(slabs), 2)), dma((2, 2))]
        args += [in_vmem(x) for x in (*panels, *acc)]
        specs += [vmem_spec()] * 5
        aliases = {len(args) - 2 + n: len(outs) - 2 + n for n in range(2)}
    return pl.pallas_call(
        functools.partial(moments_kernel, count, ready_count, at, first, last, slab_rows, valid_rows),
        in_specs=specs,
        out_specs=out_specs,
        out_shape=outs,
        scratch_shapes=scratch,
        input_output_aliases=aliases,
        compiler_params=pltpu.CompilerParams(vmem_limit_bytes=(24 if last else 18) * MIB),
        cost_estimate=pl.CostEstimate(
            flops=2 * count * slab_rows * (units * (rows + cols) + 2 * rows * cols),
            bytes_accessed=2 * count * slab_rows * units,
            transcendentals=count * slab_rows * (rows + cols),
        ),
    )(*args)


def on_device(states, projection, offsets):
    slab_rows = states.shape[0]
    tm_count = lax.axis_size("tm")
    tm, row, col = (lax.axis_index(a) for a in AXES)
    x_hi, y, core = tm // Y, tm % Y, row % 2
    valid_rows = slab_rows * tm_count - LAG
    cols = projection.shape[1]
    swap = lambda piece: move(piece, other_core)

    y_first, y_second = y - 1 + 2 * core, y + 1 - 2 * core
    place = lambda other, at: jnp.where(other, 1 - x_hi, x_hi) * Y + at % Y
    ids = [tm, place(False, y_first), place(False, y_second), place(True, y), place(False, y + 2),
           place(True, y_first), place(True, y_second), place(True, y + 2)]
    source, steps = jnp.where(core == y % 2, 0, 1), (row // 2 - tm // 2) % 4
    numbers = jnp.stack([*ids, core, col, source, steps]).astype(jnp.int32)
    after = len(ids)
    line = offsets[None, :]
    numbers, line = lax.optimization_barrier((numbers, line))
    sizes = (slab_rows, valid_rows)

    columns, turned, mine = prepare(after, numbers, projection, line, states)
    ahead, behind = move(columns, along_z(1)), move(columns, along_z(-1))
    over, partner, y_out = move(mine, crossing), move(turned, inner), move(mine, out_y)
    ahead, columns = lax.optimization_barrier((ahead, columns))
    beyond = move(columns, along_z(2))
    y_out, mine = lax.optimization_barrier((y_out, mine))
    y_back = move(mine, back_y)
    over, y_out = lax.optimization_barrier((over, y_out))
    swapped_out = swap(y_out)
    ahead, behind, beyond, partner, y_back, swapped_out = lax.optimization_barrier(
        (ahead, behind, beyond, partner, y_back, swapped_out)
    )

    panel = pick(after + 3, numbers, columns, ahead, beyond, behind)
    swapped = swap(panel)
    swapped_back, swapped_over = swap(y_back), swap(over)
    slabs = [(in_hbm(states),), (y_out, swapped_back), (y_back, swapped_out)]
    row_proj, row_off, *ready = opening(slabs, numbers, turned, partner, line, *sizes)

    over_out, y_far, over_back = move(over, out_y), move(y_out, out_y), move(y_back, crossing)
    row_off, over_out = lax.optimization_barrier((row_off, over_out))
    over_far = move(over_out, out_y)
    slabs += [(over, swapped_over)]
    *acc, col_proj = moments(slabs, 4, numbers, ready, (panel, swapped, row_proj, row_off), None, False, *sizes)
    panels = (row_proj, row_off, col_proj)

    *acc, y_far, over_back, over_far = lax.optimization_barrier((*acc, y_far, over_back, over_far))
    slabs += [(y_far, swap(y_far)), (over_out, swap(over_back)), (over_back, swap(over_out)), (over_far, swap(over_far))]
    instant, lagged, *_ = moments(slabs, 4, numbers, None, panels, acc, True, *sizes)
    shape = (2 * cols, 1, cols)
    return instant.reshape(shape), lagged.reshape(shape)


def solution(mesh):
    return jax.shard_map(
        on_device,
        mesh=mesh,
        in_specs=(P("tm", None), P(None, ("row", "col")), P(("row", "col"))),
        out_specs=(P("row", "tm", "col"), P("row", "tm", "col")),
        check_vma=False,
    )
```

```python
import functools
import jax
import jax.numpy as jnp
from jax import lax
from jax.experimental import pallas as pl
from jax.experimental.pallas import tpu as pltpu
from jax.sharding import PartitionSpec as P

LAG = 64
Y = 4
AXES = ("tm", "row", "col")
SPARE = 16
MIB = 1024 * 1024
TIME_TILES, COL_TILES = 1, 1


def route(target):
    tm_count, row_count, col_count = (lax.axis_size(a) for a in AXES)
    flat = lambda tm, row, col: (tm * row_count + row) * col_count + col
    pairs = []
    for tm in range(tm_count):
        for row in range(row_count):
            for col in range(col_count):
                to = target(tm // Y, tm % Y, row // 2, row % 2, col)
                if to is not None:
                    x_hi, y, z, core, x_lo = to
                    pairs.append((flat(tm, row, col), flat(x_hi * Y + y % Y, z * 2 + core, x_lo)))
    return pairs


def move(block, target):
    return lax.ppermute(block, AXES, route(target))


def crossing(x_hi, y, z, core, x_lo):
    return 1 - x_hi, y, z, core, 1 - x_lo


def inner(x_hi, y, z, core, x_lo):
    return x_hi, y, z, core, 1 - x_lo


def other_core(x_hi, y, z, core, x_lo):
    return x_hi, y, z, 1 - core, x_lo


def along_y(step):
    return lambda x_hi, y, z, core, x_lo: (x_hi, y + step, z, core, x_lo)


def out_y(x_hi, y, z, core, x_lo):
    return x_hi, y + 1 - 2 * core, z, core, x_lo


def back_y(x_hi, y, z, core, x_lo):
    return x_hi, y - 1 + 2 * core, z, core, x_lo


def along_z(step):
    def target(x_hi, y, z, core, x_lo):
        return (x_hi, y, (z + step) % 4, core, x_lo) if x_hi * Y + y == z * 2 + core else None
    return target


def any_spec():
    return pl.BlockSpec(memory_space=pl.ANY)


def vmem_spec():
    return pl.BlockSpec(memory_space=pltpu.VMEM)


def hbm_spec():
    return pl.BlockSpec(memory_space=pltpu.HBM)


def in_hbm(x):
    return pltpu.with_memory_space_constraint(x, pltpu.HBM)


def in_vmem(x):
    return pltpu.with_memory_space_constraint(x, pltpu.VMEM)


def smem_spec():
    return pl.BlockSpec(memory_space=pltpu.SMEM)


def row_features(row_proj, turned, row_off, start, valid_rows):
    row_off = jnp.concatenate([row_off] * (turned.shape[1] // row_off.shape[1]), axis=1)
    features = jnp.tanh(jnp.dot(row_proj, turned, preferred_element_type=jnp.float32) + row_off)
    position = start + lax.broadcasted_iota(jnp.int32, (1, turned.shape[1]), 1)
    return jnp.where(position < valid_rows, features, 0.0).astype(jnp.bfloat16)


def col_features(states, col_proj, col_off):
    return jnp.tanh(
        jnp.dot(states, col_proj, preferred_element_type=jnp.float32) + col_off
    ).astype(jnp.bfloat16)


def start(copies):
    for copy in copies:
        copy.start()


def wait(copies):
    for copy in copies:
        copy.wait()


def prepare_kernel(at, numbers, projection, offsets, states, columns, turned, mine, line, sems):
    half = mine.shape[0]
    units, cols = projection.shape
    copies = [
        pltpu.make_async_copy(projection, columns.at[pl.ds(0, units)], sems.at[0]),
        pltpu.make_async_copy(offsets, line, sems.at[1]),
        pltpu.make_async_copy(states.at[pl.ds(pl.multiple_of(numbers[at] * half, 16), half)], mine, sems.at[2]),
    ]
    start(copies)
    turned[cols:] = jnp.zeros_like(turned[cols:])
    wait(copies[1:2])
    high = line[...].astype(jnp.bfloat16)
    rest = line[...] - high.astype(jnp.float32)
    middle = rest.astype(jnp.bfloat16)
    low = (rest - middle.astype(jnp.float32)).astype(jnp.bfloat16)
    parts = jnp.concatenate([high, middle, low, jnp.zeros((SPARE - 3, cols), jnp.bfloat16)], axis=0)
    columns[units:] = parts
    turned[cols:, :cols] = parts
    wait(copies[:1])
    turned[:cols] = columns[:units].T
    wait(copies[2:])


def prepare(at, numbers, projection, offsets, states):
    units, cols = projection.shape
    half = states.shape[0] // 2
    return pl.pallas_call(
        functools.partial(prepare_kernel, at),
        in_specs=[smem_spec(), hbm_spec(), hbm_spec(), hbm_spec()],
        out_specs=[vmem_spec(), vmem_spec(), vmem_spec()],
        out_shape=[jax.ShapeDtypeStruct((units + SPARE, cols), jnp.bfloat16),
                   jax.ShapeDtypeStruct((cols + SPARE, units), jnp.bfloat16),
                   jax.ShapeDtypeStruct((half, units), jnp.bfloat16)],
        scratch_shapes=[pltpu.VMEM((1, cols), jnp.float32), pltpu.SemaphoreType.DMA((3,))],
        compiler_params=pltpu.CompilerParams(vmem_limit_bytes=12 * MIB),
    )(numbers, in_hbm(projection), in_hbm(offsets), in_hbm(states))


class OneOf:
    def __init__(self, number, sources, dst, sem):
        self.number, self.copies = number, [pltpu.make_async_copy(x, dst, sem) for x in sources]

    def start(self):
        for n, copy in enumerate(self.copies):
            pl.when(self.number == n)(copy.start)

    def wait(self):
        self.copies[0].wait()


def pick_kernel(at, numbers, *refs):
    *sources, out, sem = refs
    copy = OneOf(numbers[at], sources, out, sem)
    copy.start()
    copy.wait()


def pick(at, numbers, *sources):
    return pl.pallas_call(
        functools.partial(pick_kernel, at),
        in_specs=[smem_spec()] + [any_spec()] * len(sources),
        out_specs=vmem_spec(),
        out_shape=jax.ShapeDtypeStruct(sources[0].shape, sources[0].dtype),
        scratch_shapes=[pltpu.SemaphoreType.DMA],
        compiler_params=pltpu.CompilerParams(vmem_limit_bytes=8 * MIB),
    )(numbers, *sources)


def slab_copies(pieces, core, dst, sems):
    if len(pieces) == 1:
        return [pltpu.make_async_copy(pieces[0], dst, sems.at[0])]
    half = pieces[0].shape[0]
    return [
        pltpu.make_async_copy(piece, dst.at[pl.ds(pl.multiple_of(place * half, 16), half)], sems.at[n])
        for n, (piece, place) in enumerate(zip(pieces, (core, 1 - core)))
    ]


def opening_kernel(count, valid_rows, ids, *refs):
    refs = list(refs)
    take = lambda n: [refs.pop(0) for _ in range(n)]
    pieces = [take(1 if k == 0 else 2) for k in range(count)]
    turned, partner, offsets = take(3)
    row_proj, row_off, slab, features, parts, proj_sem, in_sem = take(7)
    rows = row_proj.shape[0]
    own, slab_rows = rows // 2, slab.shape[1]
    core = ids[(valid_rows + LAG) // slab_rows]
    row_loads = [
        pltpu.make_async_copy(turned.at[pl.ds(0, own)], row_proj.at[pl.ds(0, own)], proj_sem.at[0]),
        pltpu.make_async_copy(partner.at[pl.ds(0, own)], row_proj.at[pl.ds(own, own)], proj_sem.at[1]),
        pltpu.make_async_copy(partner.at[pl.ds(own, SPARE)], parts, proj_sem.at[2]),
    ]
    loads = [slab_copies(pieces[k], core, slab.at[k], in_sem.at[k]) for k in range(count)]
    start([*row_loads, *loads[0]])
    turn = lambda line: jnp.broadcast_to(line, (128, own)).T
    row_off[:own] = turn(offsets[...])
    wait(row_loads)
    start([copy for load in loads[1:] for copy in load])
    row_off[own:] = turn(jnp.sum(parts[:, :own].astype(jnp.float32), axis=0, keepdims=True))
    tile = slab_rows // TIME_TILES
    for k in range(count):
        wait(loads[k])
        for u in range(TIME_TILES):
            span = slice(u * tile, (u + 1) * tile)
            turned_states = slab[k, span].T
            for part in (slice(0, own), slice(own, rows)):
                features[k, part, span] = row_features(
                    row_proj[part], turned_states, row_off[part], ids[k] * slab_rows + u * tile, valid_rows
                )


def opening(slabs, numbers, turned, partner, offsets, slab_rows, valid_rows):
    rows, units, count = 2 * (turned.shape[0] - SPARE), turned.shape[1], len(slabs)
    pieces = [p for s in slabs for p in s]
    dma = pltpu.SemaphoreType.DMA
    return pl.pallas_call(
        functools.partial(opening_kernel, count, valid_rows),
        in_specs=[smem_spec()] + [any_spec()] * (len(pieces) + 2) + [vmem_spec()],
        out_specs=[vmem_spec()] * 4,
        out_shape=[
            pltpu.VMEM((rows, units), jnp.bfloat16),
            pltpu.VMEM((rows, 128), jnp.float32),
            pltpu.VMEM((count, slab_rows, units), jnp.bfloat16),
            pltpu.VMEM((count, rows, slab_rows), jnp.bfloat16),
        ],
        scratch_shapes=[pltpu.VMEM((SPARE, units), jnp.bfloat16), dma((3,)), dma((count, 2))],
        compiler_params=pltpu.CompilerParams(vmem_limit_bytes=12 * MIB),
        cost_estimate=pl.CostEstimate(
            flops=2 * count * slab_rows * units * rows, bytes_accessed=2 * count * slab_rows * units,
            transcendentals=count * slab_rows * rows,
        ),
    )(numbers, *pieces, turned, partner, offsets)


def moments_kernel(count, ready, at, first, last, slab_rows, valid_rows, *refs):
    refs = list(refs)
    take = lambda n: [refs.pop(0) for _ in range(n)]
    (ids,) = take(1)
    slabs = (valid_rows + LAG) // slab_rows
    pieces = [take(1 if last and k == 0 else 2) for k in range(slabs if last else count - ready)]
    here = [None] * ready + pieces[ready - count:]
    if first:
        ready_slab, ready_rows, *columns, row_proj, row_off = take(6)
        instant, lagged, col_proj = take(3)
    else:
        row_proj, row_off, col_proj = take(3)
        take(2)
        if last:
            acc_out = take(2)
        instant, lagged = take(2)
    slab, turned_states, row_a, row_b, col_a, col_b, in_sem = take(7)
    if first:
        (proj_sem,) = take(1)
    if last:
        instant_end, lagged_end, tails, heads, turned_edges, edge_sem, out_sem = take(7)
    rows, cols = instant.shape
    units = col_proj.shape[0] - SPARE
    half = slab_rows // 2
    time_tile, col_tile = slab_rows // TIME_TILES, cols // COL_TILES
    core, col, source = ids[slabs], ids[slabs + 1], ids[slabs + 2]
    number = lambda k: ids[at + k]

    loads = [[] if k < ready else slab_copies(here[k], core, slab.at[k - ready], in_sem.at[k - ready]) for k in range(count)]
    states = lambda k: ready_slab.at[k] if k < ready else slab.at[k - ready]
    rows_of = lambda k: ready_rows.at[k] if k < ready else row_bufs[k % 2]
    col_loads, edge_loads = [], []
    if first:
        col_loads = [OneOf(source, columns, col_proj, proj_sem)]
    if last:
        for k, piece in enumerate(pieces):
            tail, head = tails.at[ids[k]], heads.at[lax.rem(ids[k] + slabs - 1, slabs)]
            if len(piece) == 1:
                edge_loads.append(pltpu.make_async_copy(piece[0].at[pl.ds(slab_rows - LAG, LAG)], tail, edge_sem.at[k, 0]))
                edge_loads.append(pltpu.make_async_copy(piece[0].at[pl.ds(0, LAG)], head, edge_sem.at[k, 1]))
            else:
                ends = [p.at[pl.ds(half - LAG, LAG)] for p in piece]
                starts = [p.at[pl.ds(0, LAG)] for p in piece]
                edge_loads.append(OneOf(1 - core, ends, tail, edge_sem.at[k, 0]))
                edge_loads.append(OneOf(core, starts, head, edge_sem.at[k, 1]))
    start([*col_loads, *loads[0]])

    row_bufs, col_bufs = (row_a, row_b), (col_a, col_b)
    for buf in col_bufs:
        buf[slab_rows:] = jnp.zeros_like(buf[slab_rows:])

    row_part = lambda h: slice(h * rows // 2, (h + 1) * rows // 2)

    def row_tile(k, u, h):
        span, part = slice(u * time_tile, (u + 1) * time_tile), row_part(h)
        if h == 0:
            turned_states[...] = states(k)[span].T
        row_bufs[k % 2][part, span] = row_features(
            row_proj[part], turned_states[...], row_off[part], number(k) * slab_rows + u * time_tile, valid_rows
        )

    def col_off(span):
        return jnp.sum(col_proj[units:, span].astype(jnp.float32), axis=0, keepdims=True)

    def col_tile_features(k, n, h):
        span, part = slice(n * col_tile, (n + 1) * col_tile), slice(h * half, (h + 1) * half)
        col_bufs[k % 2][part, span] = col_features(states(k)[part], col_proj[:units, span], col_off(span))

    def edge_rows(h):
        size, part = slabs * LAG, row_part(h)
        if h == 0:
            turned_edges[...] = tails[...].reshape(size, units).T
        row_bufs[count % 2][part, :size] = row_features(
            row_proj[part], turned_edges[...], row_off[part], 0, (slabs - 1) * LAG
        )

    def edge_cols(n):
        span = slice(n * col_tile, (n + 1) * col_tile)
        col_bufs[count % 2][:slabs * LAG, span] = col_features(
            heads[...].reshape(slabs * LAG, units), col_proj[:units, span], col_off(span)
        )

    def moment_tile(k, lag, n, h):
        span, part = slice(n * col_tile, (n + 1) * col_tile), row_part(h)
        acc = lagged if lag else instant
        buf_r, buf_c = row_bufs[k % 2] if k == count else rows_of(k), col_bufs[k % 2]
        if k < count:
            value = jnp.dot(buf_r[part], buf_c[lag:lag + slab_rows, span], preferred_element_type=jnp.float32)
        else:
            value = jnp.dot(buf_r[part, :slabs * LAG], buf_c[:slabs * LAG, span], preferred_element_type=jnp.float32)
        if k > 0 or not first:
            value = acc[part, span] + value
        if last and k == (count if lag else count - 1):
            end = lagged_end if lag else instant_end
            value = value * (1.0 / valid_rows)
            groups = cols // 128
            for g in range(col_tile // 128):
                at = h * (rows // 2) * groups + n * (col_tile // 128) + g
                end[pl.ds(at, rows // 2, stride=groups), :] = value[:, g * 128:(g + 1) * 128]
            if n == COL_TILES - 1:
                start([stores[1 if lag else 0][h]])
        else:
            acc[part, span] = value

    def feature_steps(k):
        steps = [functools.partial(col_tile_features, k, n, h) for n in range(COL_TILES) for h in range(2)]
        if k >= ready:
            steps += [functools.partial(row_tile, k, u, h) for u in range(TIME_TILES) for h in range(2)]
        return steps

    def interleave(steps, others):
        done = 0
        for n, step in enumerate(steps):
            upto = (n + 1) * len(others) // len(steps)
            for other in others[done:upto]:
                other()
            done = upto
            step()

    stores = []
    if last:
        for m, (a, b) in enumerate(zip((instant_end, lagged_end), acc_out)):
            size = a.shape[0] // 2
            stores.append([
                pltpu.make_async_copy(
                    a.at[pl.ds(n * size, size)], b.at[pl.ds(pl.multiple_of(place * size, 8), size)], out_sem.at[m, n]
                )
                for n, place in enumerate((col, 1 - col))
            ])

    wait([*col_loads, *loads[0]])
    start([copy for load in loads[1:] for copy in load] + edge_loads)
    for step in feature_steps(0):
        step()
    for k in range(count):
        ahead = []
        if k + 1 < count:
            wait(loads[k + 1])
            ahead = feature_steps(k + 1)
        elif last:
            wait(edge_loads)
            ahead = [functools.partial(edge_cols, n) for n in range(COL_TILES)]
            ahead += [functools.partial(edge_rows, h) for h in range(2)]
        interleave(
            [functools.partial(moment_tile, k, lag, n, h) for lag in (0, LAG) for h in range(2) for n in range(COL_TILES)], ahead
        )
    if last:
        for h in range(2):
            for n in range(COL_TILES):
                moment_tile(count, LAG, n, h)
        wait(stores[0] + stores[1])


def moments(slabs, count, numbers, ready, panels, acc, last, slab_rows, valid_rows):
    first = acc is None
    row_proj, row_off = panels[-2:] if first else panels[:2]
    rows, units = row_proj.shape
    cols = rows // 2
    at = len(slabs) - count
    ready_count = ready[0].shape[0] if first else 0
    if not last:
        slabs = slabs[at + ready_count:]
    pieces = [p for s in slabs for p in s]
    end_shape = (rows * cols // 128, 128)
    outs, out_specs = [pltpu.VMEM((rows, cols), jnp.float32)] * 2, [vmem_spec()] * 2
    dma = pltpu.SemaphoreType.DMA
    scratch = [
        pltpu.VMEM((count - ready_count, slab_rows, units), jnp.bfloat16),
        pltpu.VMEM((units, slab_rows // TIME_TILES), jnp.bfloat16),
        pltpu.VMEM((rows, slab_rows), jnp.bfloat16),
        pltpu.VMEM((rows, slab_rows), jnp.bfloat16),
        pltpu.VMEM((slab_rows + LAG, cols), jnp.bfloat16),
        pltpu.VMEM((slab_rows + LAG, cols), jnp.bfloat16),
        dma((count - ready_count, 2)),
    ]
    args = [numbers, *pieces]
    specs = [smem_spec()] + [any_spec()] * len(pieces)
    aliases = {}
    if first:
        args += [*map(in_vmem, ready), *panels[:2], in_vmem(row_proj), in_vmem(row_off)]
        specs += [vmem_spec()] * 2 + [any_spec()] * 2 + [vmem_spec()] * 2
        outs, out_specs = outs + [pltpu.VMEM((units + SPARE, cols), jnp.bfloat16)], out_specs + [vmem_spec()]
        scratch.append(dma)
    else:
        if last:
            outs, out_specs = [pltpu.HBM(end_shape, jnp.float32)] * 2 + outs, [hbm_spec()] * 2 + out_specs
            scratch += [pltpu.VMEM(end_shape, jnp.float32)] * 2
            scratch += [pltpu.VMEM((len(slabs), LAG, units), jnp.bfloat16)] * 2
            scratch += [pltpu.VMEM((units, len(slabs) * LAG), jnp.bfloat16), dma((len(slabs), 2)), dma((2, 2))]
        args += [in_vmem(x) for x in (*panels, *acc)]
        specs += [vmem_spec()] * 5
        aliases = {len(args) - 2 + n: len(outs) - 2 + n for n in range(2)}
    return pl.pallas_call(
        functools.partial(moments_kernel, count, ready_count, at, first, last, slab_rows, valid_rows),
        in_specs=specs,
        out_specs=out_specs,
        out_shape=outs,
        scratch_shapes=scratch,
        input_output_aliases=aliases,
        compiler_params=pltpu.CompilerParams(vmem_limit_bytes=(24 if last else 18) * MIB),
        cost_estimate=pl.CostEstimate(
            flops=2 * count * slab_rows * (units * (rows + cols) + 2 * rows * cols),
            bytes_accessed=2 * count * slab_rows * units,
            transcendentals=count * slab_rows * (rows + cols),
        ),
    )(*args)


def on_device(states, projection, offsets):
    slab_rows = states.shape[0]
    tm_count = lax.axis_size("tm")
    tm, row, col = (lax.axis_index(a) for a in AXES)
    x_hi, y, core = tm // Y, tm % Y, row % 2
    valid_rows = slab_rows * tm_count - LAG
    cols = projection.shape[1]
    swap = lambda piece: move(piece, other_core)

    y_first, y_second = y - 1 + 2 * core, y + 1 - 2 * core
    place = lambda other, at: jnp.where(other, 1 - x_hi, x_hi) * Y + at % Y
    ids = [tm, place(False, y_first), place(False, y_second), place(True, y), place(False, y + 2),
           place(True, y_first), place(True, y_second), place(True, y + 2)]
    source, steps = jnp.where(core == y % 2, 0, 1), (row // 2 - tm // 2) % 4
    numbers = jnp.stack([*ids, core, col, source, steps]).astype(jnp.int32)
    after = len(ids)
    line = offsets[None, :]
    numbers, line = lax.optimization_barrier((numbers, line))
    sizes = (slab_rows, valid_rows)

    columns, turned, mine = prepare(after, numbers, projection, line, states)
    ahead, behind = move(columns, along_z(1)), move(columns, along_z(-1))
    over, partner, y_out = move(mine, crossing), move(turned, inner), move(mine, out_y)
    ahead, columns = lax.optimization_barrier((ahead, columns))
    beyond = move(columns, along_z(2))
    y_out, mine = lax.optimization_barrier((y_out, mine))
    y_back = move(mine, back_y)
    over, y_out = lax.optimization_barrier((over, y_out))
    swapped_out = swap(y_out)
    ahead, behind, beyond, partner, y_back, swapped_out = lax.optimization_barrier(
        (ahead, behind, beyond, partner, y_back, swapped_out)
    )

    panel = pick(after + 3, numbers, columns, ahead, beyond, behind)
    swapped = swap(panel)
    swapped_back, swapped_over = swap(y_back), swap(over)
    slabs = [(in_hbm(states),), (y_out, swapped_back), (y_back, swapped_out)]
    row_proj, row_off, *ready = opening(slabs, numbers, turned, partner, line, *sizes)

    over_out, y_far, over_back = move(over, out_y), move(y_out, out_y), move(y_back, crossing)
    row_off, over_out = lax.optimization_barrier((row_off, over_out))
    over_far = move(over_out, out_y)
    slabs += [(over, swapped_over)]
    *acc, col_proj = moments(slabs, 4, numbers, ready, (panel, swapped, row_proj, row_off), None, False, *sizes)
    panels = (row_proj, row_off, col_proj)

    *acc, y_far, over_back, over_far = lax.optimization_barrier((*acc, y_far, over_back, over_far))
    slabs += [(y_far, swap(y_far)), (over_out, swap(over_back)), (over_back, swap(over_out)), (over_far, swap(over_far))]
    instant, lagged, *_ = moments(slabs, 4, numbers, None, panels, acc, True, *sizes)
    shape = (2 * cols, 1, cols)
    return instant.reshape(shape), lagged.reshape(shape)


def solution(mesh):
    return jax.shard_map(
        on_device,
        mesh=mesh,
        in_specs=(P("tm", None), P(None, ("row", "col")), P(("row", "col"))),
        out_specs=(P("row", "tm", "col"), P("row", "tm", "col")),
        check_vma=False,
    )
```

```python
import functools
import jax
import jax.numpy as jnp
from jax import lax
from jax.experimental import pallas as pl
from jax.experimental.pallas import tpu as pltpu
from jax.sharding import PartitionSpec as P

LAG = 64
Y = 4
AXES = ("tm", "row", "col")
SPARE = 16
MIB = 1024 * 1024
TIME_TILES, COL_TILES = 1, 1


def route(target):
    tm_count, row_count, col_count = (lax.axis_size(a) for a in AXES)
    flat = lambda tm, row, col: (tm * row_count + row) * col_count + col
    pairs = []
    for tm in range(tm_count):
        for row in range(row_count):
            for col in range(col_count):
                to = target(tm // Y, tm % Y, row // 2, row % 2, col)
                if to is not None:
                    x_hi, y, z, core, x_lo = to
                    pairs.append((flat(tm, row, col), flat(x_hi * Y + y % Y, z * 2 + core, x_lo)))
    return pairs


def move(block, target):
    return lax.ppermute(block, AXES, route(target))


def crossing(x_hi, y, z, core, x_lo):
    return 1 - x_hi, y, z, core, 1 - x_lo


def inner(x_hi, y, z, core, x_lo):
    return x_hi, y, z, core, 1 - x_lo


def other_core(x_hi, y, z, core, x_lo):
    return x_hi, y, z, 1 - core, x_lo


def along_y(step):
    return lambda x_hi, y, z, core, x_lo: (x_hi, y + step, z, core, x_lo)


def out_y(x_hi, y, z, core, x_lo):
    return x_hi, y + 1 - 2 * core, z, core, x_lo


def back_y(x_hi, y, z, core, x_lo):
    return x_hi, y - 1 + 2 * core, z, core, x_lo


def along_z(step):
    def target(x_hi, y, z, core, x_lo):
        return (x_hi, y, (z + step) % 4, core, x_lo) if x_hi * Y + y == z * 2 + core else None
    return target


def any_spec():
    return pl.BlockSpec(memory_space=pl.ANY)


def vmem_spec():
    return pl.BlockSpec(memory_space=pltpu.VMEM)


def hbm_spec():
    return pl.BlockSpec(memory_space=pltpu.HBM)


def in_hbm(x):
    return pltpu.with_memory_space_constraint(x, pltpu.HBM)


def in_vmem(x):
    return pltpu.with_memory_space_constraint(x, pltpu.VMEM)


def smem_spec():
    return pl.BlockSpec(memory_space=pltpu.SMEM)


def row_features(row_proj, turned, row_off, start, valid_rows):
    row_off = jnp.concatenate([row_off] * (turned.shape[1] // row_off.shape[1]), axis=1)
    features = jnp.tanh(jnp.dot(row_proj, turned, preferred_element_type=jnp.float32) + row_off)
    position = start + lax.broadcasted_iota(jnp.int32, (1, turned.shape[1]), 1)
    return jnp.where(position < valid_rows, features, 0.0).astype(jnp.bfloat16)


def col_features(states, col_proj, col_off):
    return jnp.tanh(
        jnp.dot(states, col_proj, preferred_element_type=jnp.float32) + col_off
    ).astype(jnp.bfloat16)


def start(copies):
    for copy in copies:
        copy.start()


def wait(copies):
    for copy in copies:
        copy.wait()


def prepare_kernel(at, numbers, projection, offsets, states, columns, turned, mine, line, sems):
    half = mine.shape[0]
    units, cols = projection.shape
    copies = [
        pltpu.make_async_copy(projection, columns.at[pl.ds(0, units)], sems.at[0]),
        pltpu.make_async_copy(offsets, line, sems.at[1]),
        pltpu.make_async_copy(states.at[pl.ds(pl.multiple_of(numbers[at] * half, 16), half)], mine, sems.at[2]),
    ]
    start(copies)
    turned[cols:] = jnp.zeros_like(turned[cols:])
    wait(copies[1:2])
    high = line[...].astype(jnp.bfloat16)
    rest = line[...] - high.astype(jnp.float32)
    middle = rest.astype(jnp.bfloat16)
    low = (rest - middle.astype(jnp.float32)).astype(jnp.bfloat16)
    parts = jnp.concatenate([high, middle, low, jnp.zeros((SPARE - 3, cols), jnp.bfloat16)], axis=0)
    columns[units:] = parts
    turned[cols:, :cols] = parts
    wait(copies[:1])
    turned[:cols] = columns[:units].T
    wait(copies[2:])


def prepare(at, numbers, projection, offsets, states):
    units, cols = projection.shape
    half = states.shape[0] // 2
    return pl.pallas_call(
        functools.partial(prepare_kernel, at),
        in_specs=[smem_spec(), hbm_spec(), hbm_spec(), hbm_spec()],
        out_specs=[vmem_spec(), vmem_spec(), vmem_spec()],
        out_shape=[jax.ShapeDtypeStruct((units + SPARE, cols), jnp.bfloat16),
                   jax.ShapeDtypeStruct((cols + SPARE, units), jnp.bfloat16),
                   jax.ShapeDtypeStruct((half, units), jnp.bfloat16)],
        scratch_shapes=[pltpu.VMEM((1, cols), jnp.float32), pltpu.SemaphoreType.DMA((3,))],
        compiler_params=pltpu.CompilerParams(vmem_limit_bytes=12 * MIB),
    )(numbers, in_hbm(projection), in_hbm(offsets), in_hbm(states))


class OneOf:
    def __init__(self, number, sources, dst, sem):
        self.number, self.copies = number, [pltpu.make_async_copy(x, dst, sem) for x in sources]

    def start(self):
        for n, copy in enumerate(self.copies):
            pl.when(self.number == n)(copy.start)

    def wait(self):
        self.copies[0].wait()


def pick_kernel(at, numbers, *refs):
    *sources, out, sem = refs
    copy = OneOf(numbers[at], sources, out, sem)
    copy.start()
    copy.wait()


def pick(at, numbers, *sources):
    return pl.pallas_call(
        functools.partial(pick_kernel, at),
        in_specs=[smem_spec()] + [any_spec()] * len(sources),
        out_specs=vmem_spec(),
        out_shape=jax.ShapeDtypeStruct(sources[0].shape, sources[0].dtype),
        scratch_shapes=[pltpu.SemaphoreType.DMA],
        compiler_params=pltpu.CompilerParams(vmem_limit_bytes=8 * MIB),
    )(numbers, *sources)


def slab_copies(pieces, core, dst, sems):
    if len(pieces) == 1:
        return [pltpu.make_async_copy(pieces[0], dst, sems.at[0])]
    half = pieces[0].shape[0]
    return [
        pltpu.make_async_copy(piece, dst.at[pl.ds(pl.multiple_of(place * half, 16), half)], sems.at[n])
        for n, (piece, place) in enumerate(zip(pieces, (core, 1 - core)))
    ]


def lane_broadcast(line):
    return jnp.broadcast_to(line, (128, line.shape[1])).T


def opening_kernel(count, valid_rows, ids, *refs):
    refs = list(refs)
    take = lambda n: [refs.pop(0) for _ in range(n)]
    pieces = [take(1 if k == 0 else 2) for k in range(count)]
    turned, partner, offsets = take(3)
    row_proj, row_off, slab, features, parts, proj_sem, in_sem = take(7)
    rows = row_proj.shape[0]
    own, slab_rows = rows // 2, slab.shape[1]
    core = ids[(valid_rows + LAG) // slab_rows]
    row_loads = [
        pltpu.make_async_copy(turned.at[pl.ds(0, own)], row_proj.at[pl.ds(0, own)], proj_sem.at[0]),
        pltpu.make_async_copy(partner.at[pl.ds(0, own)], row_proj.at[pl.ds(own, own)], proj_sem.at[1]),
        pltpu.make_async_copy(partner.at[pl.ds(own, SPARE)], parts, proj_sem.at[2]),
    ]
    loads = [slab_copies(pieces[k], core, slab.at[k], in_sem.at[k]) for k in range(count)]
    start([row_loads[0], *loads[0], *row_loads[1:]])
    row_off[:own] = lane_broadcast(offsets[...])
    wait(row_loads[:1])
    for k in range(count):
        wait(loads[k])
        if k == 0:
            start([copy for load in loads[1:] for copy in load])
        turned_states = slab[k].T
        for n, part in enumerate((slice(0, own), slice(own, rows))):
            if k == 0 and n == 1:
                wait(row_loads[1:])
                row_off[own:] = lane_broadcast(jnp.sum(parts[:, :own].astype(jnp.float32), axis=0, keepdims=True))
            features[k, part] = row_features(
                row_proj[part], turned_states, row_off[part], ids[k] * slab_rows, valid_rows
            )


def opening(slabs, numbers, turned, partner, offsets, slab_rows, valid_rows):
    rows, units, count = 2 * (turned.shape[0] - SPARE), turned.shape[1], len(slabs)
    pieces = [p for s in slabs for p in s]
    dma = pltpu.SemaphoreType.DMA
    return pl.pallas_call(
        functools.partial(opening_kernel, count, valid_rows),
        in_specs=[smem_spec()] + [any_spec()] * (len(pieces) + 2) + [vmem_spec()],
        out_specs=[vmem_spec()] * 4,
        out_shape=[
            pltpu.VMEM((rows, units), jnp.bfloat16),
            pltpu.VMEM((rows, 128), jnp.float32),
            pltpu.VMEM((count, slab_rows, units), jnp.bfloat16),
            pltpu.VMEM((count, rows, slab_rows), jnp.bfloat16),
        ],
        scratch_shapes=[pltpu.VMEM((SPARE, units), jnp.bfloat16), dma((3,)), dma((count, 2))],
        compiler_params=pltpu.CompilerParams(vmem_limit_bytes=12 * MIB),
        cost_estimate=pl.CostEstimate(
            flops=2 * count * slab_rows * units * rows, bytes_accessed=2 * count * slab_rows * units,
            transcendentals=count * slab_rows * rows,
        ),
    )(numbers, *pieces, turned, partner, offsets)


def moments_kernel(count, ready, at, last, slab_rows, valid_rows, *refs):
    first = not last
    refs = list(refs)
    take = lambda n: [refs.pop(0) for _ in range(n)]
    (ids,) = take(1)
    slabs = (valid_rows + LAG) // slab_rows
    pieces = [take(1 if last and k == 0 else 2) for k in range(slabs if last else count - ready)]
    here = [None] * ready + pieces[ready - count:]
    if first:
        ready_slab, ready_rows, *columns, row_proj, row_off = take(6)
    else:
        row_proj, row_off, col_proj, row_next, col_next = take(5)
        take(2)
        acc_out = take(2)
    instant, lagged = take(2)
    if first:
        col_proj, row_next, col_next = take(3)
    slab, turned_states, row_a, row_b, col_a, col_b, in_sem = take(7)
    if first:
        (proj_sem,) = take(1)
    if last:
        instant_end, lagged_end, tails, heads, turned_edges, edge_sem, out_sem = take(7)
    rows, cols = instant.shape
    units = col_proj.shape[0] - SPARE
    half = slab_rows // 2
    time_tile, col_tile = slab_rows // TIME_TILES, cols // COL_TILES
    core, col, source = ids[slabs], ids[slabs + 1], ids[slabs + 2]
    number = lambda k: ids[at + k]

    loads = [[] if k < ready else slab_copies(here[k], core, slab.at[k - ready], in_sem.at[k - ready]) for k in range(count)]
    states = lambda k: ready_slab.at[k] if k < ready else slab.at[k - ready]
    between = count - 1 if first else 0
    row_bufs = lambda k: row_next if k == between else (row_a, row_b)[k % 2]
    col_bufs = lambda k: col_next if k == between else (col_a, col_b)[k % 2]
    col_loads, edge_loads = [], []
    if first:
        col_loads = [OneOf(source, columns, col_proj, proj_sem)]
    if last:
        for k, piece in enumerate(pieces):
            tail, head = tails.at[ids[k]], heads.at[lax.rem(ids[k] + slabs - 1, slabs)]
            if len(piece) == 1:
                edge_loads.append(pltpu.make_async_copy(piece[0].at[pl.ds(slab_rows - LAG, LAG)], tail, edge_sem.at[k, 0]))
                edge_loads.append(pltpu.make_async_copy(piece[0].at[pl.ds(0, LAG)], head, edge_sem.at[k, 1]))
            else:
                ends = [p.at[pl.ds(half - LAG, LAG)] for p in piece]
                starts = [p.at[pl.ds(0, LAG)] for p in piece]
                edge_loads.append(OneOf(1 - core, ends, tail, edge_sem.at[k, 0]))
                edge_loads.append(OneOf(core, starts, head, edge_sem.at[k, 1]))
    start([*col_loads, *loads[ready]])

    for buf in (col_a, col_b) + ((col_next,) if first else ()):
        buf[slab_rows:] = jnp.zeros_like(buf[slab_rows:])

    row_part = lambda h: slice(h * rows // 2, (h + 1) * rows // 2)

    def row_tile(k, u, h):
        span, part = slice(u * time_tile, (u + 1) * time_tile), row_part(h)
        if h == 0:
            turned_states[...] = states(k)[span].T
        row_bufs(k)[part, span] = row_features(
            row_proj[part], turned_states[...], row_off[part], number(k) * slab_rows + u * time_tile, valid_rows
        )

    def col_off(span):
        return jnp.sum(col_proj[units:, span].astype(jnp.float32), axis=0, keepdims=True)

    def col_tile_features(k, n, h):
        span, part = slice(n * col_tile, (n + 1) * col_tile), slice(h * half, (h + 1) * half)
        col_bufs(k)[part, span] = col_features(states(k)[part], col_proj[:units, span], col_off(span))

    def edge_rows(h):
        size, part = slabs * LAG, row_part(h)
        if h == 0:
            turned_edges[...] = tails[...].reshape(size, units).T
        row_bufs(count)[part, :size] = row_features(
            row_proj[part], turned_edges[...], row_off[part], 0, (slabs - 1) * LAG
        )

    def edge_cols(n):
        span = slice(n * col_tile, (n + 1) * col_tile)
        col_bufs(count)[:slabs * LAG, span] = col_features(
            heads[...].reshape(slabs * LAG, units), col_proj[:units, span], col_off(span)
        )

    def moment_tile(k, lag, n, h):
        span, part = slice(n * col_tile, (n + 1) * col_tile), row_part(h)
        acc = lagged if lag else instant
        buf_r, buf_c = row_bufs(k), col_bufs(k)
        if k < count:
            value = jnp.dot(ready_rows[k, part] if k < ready and first else buf_r[part], buf_c[lag:lag + slab_rows, span], preferred_element_type=jnp.float32)
        else:
            value = jnp.dot(buf_r[part, :slabs * LAG], buf_c[:slabs * LAG, span], preferred_element_type=jnp.float32)
        if k > 0 or not first:
            value = acc[part, span] + value
        if last and k == (count if lag else count - 1):
            end = lagged_end if lag else instant_end
            value = value * (1.0 / valid_rows)
            groups = cols // 128
            for g in range(col_tile // 128):
                at = h * (rows // 2) * groups + n * (col_tile // 128) + g
                end[pl.ds(at, rows // 2, stride=groups), :] = value[:, g * 128:(g + 1) * 128]
            if n == COL_TILES - 1:
                start([stores[1 if lag else 0][h]])
        else:
            acc[part, span] = value

    def feature_steps(k):
        steps = [functools.partial(col_tile_features, k, n, h) for n in range(COL_TILES) for h in range(2)]
        if k >= ready:
            steps += [functools.partial(row_tile, k, u, h) for u in range(TIME_TILES) for h in range(2)]
        return steps

    def interleave(steps, others):
        done = 0
        for n, step in enumerate(steps):
            upto = (n + 1) * len(others) // len(steps)
            for other in others[done:upto]:
                other()
            done = upto
            step()

    stores = []
    if last:
        for m, (a, b) in enumerate(zip((instant_end, lagged_end), acc_out)):
            size = a.shape[0] // 2
            stores.append([
                pltpu.make_async_copy(
                    a.at[pl.ds(n * size, size)], b.at[pl.ds(pl.multiple_of(place * size, 8), size)], out_sem.at[m, n]
                )
                for n, place in enumerate((col, 1 - col))
            ])

    if first:
        wait(col_loads)
        for step in feature_steps(0):
            step()
    for k in range(count - 1 if first else count):
        ahead = []
        steps = [functools.partial(moment_tile, k, lag, n, h) for lag in (0, LAG) for h in range(2) for n in range(COL_TILES)]
        if last and k == 0:
            steps.pop(0)()
            steps.pop(0)()
        if k + 1 < count:
            wait(loads[k + 1])
            if k == 0:
                start([copy for load in loads[ready + 1:] for copy in load] + edge_loads)
            ahead = feature_steps(k + 1)
        elif last:
            wait(edge_loads)
            ahead = [functools.partial(edge_cols, n) for n in range(COL_TILES)]
            ahead += [functools.partial(edge_rows, h) for h in range(2)]
        interleave(steps, ahead)
    if last:
        for h in range(2):
            for n in range(COL_TILES):
                moment_tile(count, LAG, n, h)
        wait(stores[0] + stores[1])


def moments(slabs, count, numbers, opened, panels, carry, slab_rows, valid_rows):
    first, last = carry is None, carry is not None
    units = slabs[0][0].shape[1]
    cols = panels[0].shape[1] if first else carry[0].shape[1]
    rows = 2 * cols
    at = len(slabs) - count
    ready = opened[0].shape[0] if first else 1
    if first:
        slabs = slabs[at + ready:]
    pieces = [p for s in slabs for p in s]
    end_shape = (rows * cols // 128, 128)
    outs = [pltpu.VMEM((rows, cols), jnp.float32)] * 2
    dma = pltpu.SemaphoreType.DMA
    scratch = [
        pltpu.VMEM((count - ready, slab_rows, units), jnp.bfloat16),
        pltpu.VMEM((units, slab_rows // TIME_TILES), jnp.bfloat16),
        pltpu.VMEM((rows, slab_rows), jnp.bfloat16),
        pltpu.VMEM((rows, slab_rows), jnp.bfloat16),
        pltpu.VMEM((slab_rows + LAG, cols), jnp.bfloat16),
        pltpu.VMEM((slab_rows + LAG, cols), jnp.bfloat16),
        dma((count - ready, 2)),
    ]
    args = [numbers, *pieces]
    specs = [smem_spec()] + [any_spec()] * len(pieces)
    aliases = {}
    if first:
        args += [*map(in_vmem, opened), *panels[:2], *map(in_vmem, panels[2:])]
        specs += [vmem_spec()] * 2 + [any_spec()] * 2 + [vmem_spec()] * 2
        outs = outs + [
            pltpu.VMEM((units + SPARE, cols), jnp.bfloat16),
            pltpu.VMEM((rows, slab_rows), jnp.bfloat16),
            pltpu.VMEM((slab_rows + LAG, cols), jnp.bfloat16),
        ]
        out_specs = [vmem_spec()] * 5
        scratch.append(dma)
    else:
        outs, out_specs = [pltpu.HBM(end_shape, jnp.float32)] * 2 + outs, [hbm_spec()] * 2 + [vmem_spec()] * 2
        scratch += [pltpu.VMEM(end_shape, jnp.float32)] * 2
        scratch += [pltpu.VMEM((len(slabs), LAG, units), jnp.bfloat16)] * 2
        scratch += [pltpu.VMEM((units, len(slabs) * LAG), jnp.bfloat16), dma((len(slabs), 2)), dma((2, 2))]
        args += [in_vmem(x) for x in (*panels, *carry[2:], *carry[:2])]
        specs += [vmem_spec()] * 7
        aliases = {len(args) - 2 + n: 2 + n for n in range(2)}
    return pl.pallas_call(
        functools.partial(moments_kernel, count, ready, at, last, slab_rows, valid_rows),
        in_specs=specs,
        out_specs=out_specs,
        out_shape=outs,
        scratch_shapes=scratch,
        input_output_aliases=aliases,
        compiler_params=pltpu.CompilerParams(vmem_limit_bytes=(24 if last else 16) * MIB),
        cost_estimate=pl.CostEstimate(
            flops=2 * count * slab_rows * (units * (rows + cols) + 2 * rows * cols),
            bytes_accessed=2 * count * slab_rows * units,
            transcendentals=count * slab_rows * (rows + cols),
        ),
    )(*args)


def on_device(states, projection, offsets):
    slab_rows = states.shape[0]
    tm_count = lax.axis_size("tm")
    tm, row, col = (lax.axis_index(a) for a in AXES)
    x_hi, y, core = tm // Y, tm % Y, row % 2
    valid_rows = slab_rows * tm_count - LAG
    cols = projection.shape[1]
    swap = lambda piece: move(piece, other_core)

    y_first, y_second = y - 1 + 2 * core, y + 1 - 2 * core
    place = lambda other, at: jnp.where(other, 1 - x_hi, x_hi) * Y + at % Y
    ids = [tm, place(False, y_first), place(False, y_second), place(True, y), place(False, y + 2),
           place(True, y_first), place(True, y_second), place(True, y + 2)]
    source, steps = jnp.where(core == y % 2, 0, 1), (row // 2 - tm // 2) % 4
    numbers = jnp.stack([*ids, core, col, source, steps]).astype(jnp.int32)
    after = len(ids)
    line = offsets[None, :]
    numbers, line = lax.optimization_barrier((numbers, line))
    sizes = (slab_rows, valid_rows)

    columns, turned, mine = prepare(after, numbers, projection, line, states)
    ahead, behind = move(columns, along_z(1)), move(columns, along_z(-1))
    over, partner, y_out = move(mine, crossing), move(turned, inner), move(mine, out_y)
    ahead, columns = lax.optimization_barrier((ahead, columns))
    beyond = move(columns, along_z(2))
    y_out, mine = lax.optimization_barrier((y_out, mine))
    y_back = move(mine, back_y)
    over, y_out = lax.optimization_barrier((over, y_out))
    swapped_out = swap(y_out)
    ahead, behind, beyond, partner, y_back, swapped_out = lax.optimization_barrier(
        (ahead, behind, beyond, partner, y_back, swapped_out)
    )

    panel = pick(after + 3, numbers, columns, ahead, beyond, behind)
    swapped = swap(panel)
    swapped_back, swapped_over = swap(y_back), swap(over)
    slabs = [(in_hbm(states),), (y_out, swapped_back), (y_back, swapped_out)]
    row_proj, row_off, *opened = opening(slabs, numbers, turned, partner, line, *sizes)

    over_out, y_far, over_back = move(over, out_y), move(y_out, out_y), move(y_back, crossing)
    row_off, over_out = lax.optimization_barrier((row_off, over_out))
    over_far = move(over_out, out_y)
    slabs += [(over, swapped_over)]
    carry = moments(slabs, 4, numbers, opened, (panel, swapped, row_proj, row_off), None, *sizes)

    *carry, y_far, over_back, over_far = lax.optimization_barrier((*carry, y_far, over_back, over_far))
    slabs += [(y_far, swap(y_far)), (over_out, swap(over_back)), (over_back, swap(over_out)), (over_far, swap(over_far))]
    instant, lagged, *_ = moments(slabs, 5, numbers, None, (row_proj, row_off), carry, *sizes)
    shape = (2 * cols, 1, cols)
    return instant.reshape(shape), lagged.reshape(shape)


def solution(mesh):
    return jax.shard_map(
        on_device,
        mesh=mesh,
        in_specs=(P("tm", None), P(None, ("row", "col")), P(("row", "col"))),
        out_specs=(P("row", "tm", "col"), P("row", "tm", "col")),
        check_vma=False,
    )
```

```python
import functools
import jax
import jax.numpy as jnp
from jax import lax
from jax.experimental import pallas as pl
from jax.experimental.pallas import tpu as pltpu
from jax.sharding import PartitionSpec as P

LAG = 64
Y = 4
AXES = ("tm", "row", "col")
SPARE = 16
MIB = 1024 * 1024
TIME_TILES, COL_TILES = 1, 1


def route(target):
    tm_count, row_count, col_count = (lax.axis_size(a) for a in AXES)
    flat = lambda tm, row, col: (tm * row_count + row) * col_count + col
    pairs = []
    for tm in range(tm_count):
        for row in range(row_count):
            for col in range(col_count):
                to = target(tm // Y, tm % Y, row // 2, row % 2, col)
                if to is not None:
                    x_hi, y, z, core, x_lo = to
                    pairs.append((flat(tm, row, col), flat(x_hi * Y + y % Y, z * 2 + core, x_lo)))
    return pairs


def move(block, target):
    return lax.ppermute(block, AXES, route(target))


def crossing(x_hi, y, z, core, x_lo):
    return 1 - x_hi, y, z, core, 1 - x_lo


def inner(x_hi, y, z, core, x_lo):
    return x_hi, y, z, core, 1 - x_lo


def other_core(x_hi, y, z, core, x_lo):
    return x_hi, y, z, 1 - core, x_lo


def along_y(step):
    return lambda x_hi, y, z, core, x_lo: (x_hi, y + step, z, core, x_lo)


def out_y(x_hi, y, z, core, x_lo):
    return x_hi, y + 1 - 2 * core, z, core, x_lo


def back_y(x_hi, y, z, core, x_lo):
    return x_hi, y - 1 + 2 * core, z, core, x_lo


def along_z(step):
    def target(x_hi, y, z, core, x_lo):
        return (x_hi, y, (z + step) % 4, core, x_lo) if x_hi * Y + y == z * 2 + core else None
    return target


def any_spec():
    return pl.BlockSpec(memory_space=pl.ANY)


def vmem_spec():
    return pl.BlockSpec(memory_space=pltpu.VMEM)


def hbm_spec():
    return pl.BlockSpec(memory_space=pltpu.HBM)


def in_hbm(x):
    return pltpu.with_memory_space_constraint(x, pltpu.HBM)


def in_vmem(x):
    return pltpu.with_memory_space_constraint(x, pltpu.VMEM)


def smem_spec():
    return pl.BlockSpec(memory_space=pltpu.SMEM)


def row_features(row_proj, turned, row_off, start, valid_rows):
    row_off = jnp.concatenate([row_off] * (turned.shape[1] // row_off.shape[1]), axis=1)
    features = jnp.tanh(jnp.dot(row_proj, turned, preferred_element_type=jnp.float32) + row_off)
    position = start + lax.broadcasted_iota(jnp.int32, (1, turned.shape[1]), 1)
    return jnp.where(position < valid_rows, features, 0.0).astype(jnp.bfloat16)


def col_features(states, col_proj, col_off):
    return jnp.tanh(
        jnp.dot(states, col_proj, preferred_element_type=jnp.float32) + col_off
    ).astype(jnp.bfloat16)


def start(copies):
    for copy in copies:
        copy.start()


def wait(copies):
    for copy in copies:
        copy.wait()


def prepare_kernel(at, numbers, projection, offsets, states, columns, turned, mine, line, sems):
    half = mine.shape[0]
    units, cols = projection.shape
    copies = [
        pltpu.make_async_copy(projection, columns.at[pl.ds(0, units)], sems.at[0]),
        pltpu.make_async_copy(offsets, line, sems.at[1]),
        pltpu.make_async_copy(states.at[pl.ds(pl.multiple_of(numbers[at] * half, 16), half)], mine, sems.at[2]),
    ]
    start(copies)
    turned[cols:] = jnp.zeros_like(turned[cols:])
    wait(copies[1:2])
    high = line[...].astype(jnp.bfloat16)
    rest = line[...] - high.astype(jnp.float32)
    middle = rest.astype(jnp.bfloat16)
    low = (rest - middle.astype(jnp.float32)).astype(jnp.bfloat16)
    parts = jnp.concatenate([high, middle, low, jnp.zeros((SPARE - 3, cols), jnp.bfloat16)], axis=0)
    columns[units:] = parts
    turned[cols:, :cols] = parts
    wait(copies[:1])
    turned[:cols] = columns[:units].T
    wait(copies[2:])


def prepare(at, numbers, projection, offsets, states):
    units, cols = projection.shape
    half = states.shape[0] // 2
    return pl.pallas_call(
        functools.partial(prepare_kernel, at),
        in_specs=[smem_spec(), hbm_spec(), hbm_spec(), hbm_spec()],
        out_specs=[vmem_spec(), vmem_spec(), vmem_spec()],
        out_shape=[jax.ShapeDtypeStruct((units + SPARE, cols), jnp.bfloat16),
                   jax.ShapeDtypeStruct((cols + SPARE, units), jnp.bfloat16),
                   jax.ShapeDtypeStruct((half, units), jnp.bfloat16)],
        scratch_shapes=[pltpu.VMEM((1, cols), jnp.float32), pltpu.SemaphoreType.DMA((3,))],
        compiler_params=pltpu.CompilerParams(vmem_limit_bytes=12 * MIB),
    )(numbers, in_hbm(projection), in_hbm(offsets), in_hbm(states))


class OneOf:
    def __init__(self, number, sources, dst, sem):
        self.number, self.copies = number, [pltpu.make_async_copy(x, dst, sem) for x in sources]

    def start(self):
        for n, copy in enumerate(self.copies):
            pl.when(self.number == n)(copy.start)

    def wait(self):
        self.copies[0].wait()


def pick_kernel(at, numbers, *refs):
    *sources, out, sem = refs
    copy = OneOf(numbers[at], sources, out, sem)
    copy.start()
    copy.wait()


def pick(at, numbers, *sources):
    return pl.pallas_call(
        functools.partial(pick_kernel, at),
        in_specs=[smem_spec()] + [any_spec()] * len(sources),
        out_specs=vmem_spec(),
        out_shape=jax.ShapeDtypeStruct(sources[0].shape, sources[0].dtype),
        scratch_shapes=[pltpu.SemaphoreType.DMA],
        compiler_params=pltpu.CompilerParams(vmem_limit_bytes=8 * MIB),
    )(numbers, *sources)


def slab_copies(pieces, core, dst, sems):
    if len(pieces) == 1:
        return [pltpu.make_async_copy(pieces[0], dst, sems.at[0])]
    half = pieces[0].shape[0]
    return [
        pltpu.make_async_copy(piece, dst.at[pl.ds(pl.multiple_of(place * half, 16), half)], sems.at[n])
        for n, (piece, place) in enumerate(zip(pieces, (core, 1 - core)))
    ]


def lane_broadcast(line):
    return jnp.broadcast_to(line, (128, line.shape[1])).T


def opening_kernel(count, valid_rows, ids, *refs):
    refs = list(refs)
    take = lambda n: [refs.pop(0) for _ in range(n)]
    pieces = [take(1 if k == 0 else 2) for k in range(count)]
    turned, partner, offsets = take(3)
    row_proj, row_off, slab, features, parts, proj_sem, in_sem = take(7)
    rows = row_proj.shape[0]
    own, slab_rows = rows // 2, slab.shape[1]
    core = ids[(valid_rows + LAG) // slab_rows]
    row_loads = [
        pltpu.make_async_copy(turned.at[pl.ds(0, own)], row_proj.at[pl.ds(0, own)], proj_sem.at[0]),
        pltpu.make_async_copy(partner.at[pl.ds(0, own)], row_proj.at[pl.ds(own, own)], proj_sem.at[1]),
        pltpu.make_async_copy(partner.at[pl.ds(own, SPARE)], parts, proj_sem.at[2]),
    ]
    loads = [slab_copies(pieces[k], core, slab.at[k], in_sem.at[k]) for k in range(count)]
    start([*row_loads, *loads[0]])
    row_off[:own] = lane_broadcast(offsets[...])
    wait(row_loads)
    start([copy for load in loads[1:] for copy in load])
    row_off[own:] = lane_broadcast(jnp.sum(parts[:, :own].astype(jnp.float32), axis=0, keepdims=True))
    tile = slab_rows // TIME_TILES
    for k in range(count):
        wait(loads[k])
        for u in range(TIME_TILES):
            span = slice(u * tile, (u + 1) * tile)
            turned_states = slab[k, span].T
            for part in (slice(0, own), slice(own, rows)):
                features[k, part, span] = row_features(
                    row_proj[part], turned_states, row_off[part], ids[k] * slab_rows + u * tile, valid_rows
                )


def opening(slabs, numbers, turned, partner, offsets, slab_rows, valid_rows):
    rows, units, count = 2 * (turned.shape[0] - SPARE), turned.shape[1], len(slabs)
    pieces = [p for s in slabs for p in s]
    dma = pltpu.SemaphoreType.DMA
    return pl.pallas_call(
        functools.partial(opening_kernel, count, valid_rows),
        in_specs=[smem_spec()] + [any_spec()] * (len(pieces) + 2) + [vmem_spec()],
        out_specs=[vmem_spec()] * 4,
        out_shape=[
            pltpu.VMEM((rows, units), jnp.bfloat16),
            pltpu.VMEM((rows, 128), jnp.float32),
            pltpu.VMEM((count, slab_rows, units), jnp.bfloat16),
            pltpu.VMEM((count, rows, slab_rows), jnp.bfloat16),
        ],
        scratch_shapes=[pltpu.VMEM((SPARE, units), jnp.bfloat16), dma((3,)), dma((count, 2))],
        compiler_params=pltpu.CompilerParams(vmem_limit_bytes=12 * MIB),
        cost_estimate=pl.CostEstimate(
            flops=2 * count * slab_rows * units * rows, bytes_accessed=2 * count * slab_rows * units,
            transcendentals=count * slab_rows * rows,
        ),
    )(numbers, *pieces, turned, partner, offsets)


def moments_kernel(count, ready, at, last, slab_rows, valid_rows, *refs):
    first = not last
    refs = list(refs)
    take = lambda n: [refs.pop(0) for _ in range(n)]
    (ids,) = take(1)
    slabs = (valid_rows + LAG) // slab_rows
    pieces = [take(1 if last and k == 0 else 2) for k in range(slabs if last else count - ready)]
    here = [None] * ready + pieces[ready - count:]
    if first:
        ready_slab, ready_rows, *columns, row_proj, row_off = take(6)
    else:
        row_proj, row_off, col_proj, row_next, col_next = take(5)
        take(2)
        acc_out = take(2)
    instant, lagged = take(2)
    if first:
        col_proj, row_next, col_next = take(3)
    slab, turned_states, row_a, row_b, col_a, col_b, in_sem = take(7)
    if first:
        (proj_sem,) = take(1)
    if last:
        tails, heads, turned_edges, edge_sem, out_sem = take(5)
    rows, cols = instant.shape
    units = col_proj.shape[0] - SPARE
    half = slab_rows // 2
    time_tile, col_tile = slab_rows // TIME_TILES, cols // COL_TILES
    core, col, source = ids[slabs], ids[slabs + 1], ids[slabs + 2]
    number = lambda k: ids[at + k]

    loads = [[] if k < ready else slab_copies(here[k], core, slab.at[k - ready], in_sem.at[k - ready]) for k in range(count)]
    states = lambda k: ready_slab.at[k] if k < ready else slab.at[k - ready]
    between = count - 1 if first else 0
    row_bufs = lambda k: row_next if k == between else (row_a, row_b)[k % 2]
    col_bufs = lambda k: col_next if k == between else (col_a, col_b)[k % 2]
    col_loads, edge_loads = [], []
    if first:
        col_loads = [OneOf(source, columns, col_proj, proj_sem)]
    if last:
        for k, piece in enumerate(pieces):
            tail, head = tails.at[ids[k]], heads.at[lax.rem(ids[k] + slabs - 1, slabs)]
            if len(piece) == 1:
                edge_loads.append(pltpu.make_async_copy(piece[0].at[pl.ds(slab_rows - LAG, LAG)], tail, edge_sem.at[k, 0]))
                edge_loads.append(pltpu.make_async_copy(piece[0].at[pl.ds(0, LAG)], head, edge_sem.at[k, 1]))
            else:
                ends = [p.at[pl.ds(half - LAG, LAG)] for p in piece]
                starts = [p.at[pl.ds(0, LAG)] for p in piece]
                edge_loads.append(OneOf(1 - core, ends, tail, edge_sem.at[k, 0]))
                edge_loads.append(OneOf(core, starts, head, edge_sem.at[k, 1]))
    start([*col_loads, *loads[ready]])

    for buf in (col_a, col_b) + ((col_next,) if first else ()):
        buf[slab_rows:] = jnp.zeros_like(buf[slab_rows:])

    row_part = lambda h: slice(h * rows // 2, (h + 1) * rows // 2)

    def row_tile(k, u, h):
        span, part = slice(u * time_tile, (u + 1) * time_tile), row_part(h)
        if h == 0:
            turned_states[...] = states(k)[span].T
        row_bufs(k)[part, span] = row_features(
            row_proj[part], turned_states[...], row_off[part], number(k) * slab_rows + u * time_tile, valid_rows
        )

    def col_off(span):
        return jnp.sum(col_proj[units:, span].astype(jnp.float32), axis=0, keepdims=True)

    def col_tile_features(k, n, h):
        span, part = slice(n * col_tile, (n + 1) * col_tile), slice(h * half, (h + 1) * half)
        col_bufs(k)[part, span] = col_features(states(k)[part], col_proj[:units, span], col_off(span))

    def edge_rows(h):
        size, part = slabs * LAG, row_part(h)
        if h == 0:
            turned_edges[...] = tails[...].reshape(size, units).T
        row_bufs(count)[part, :size] = row_features(
            row_proj[part], turned_edges[...], row_off[part], 0, (slabs - 1) * LAG
        )

    def edge_cols(n):
        span = slice(n * col_tile, (n + 1) * col_tile)
        col_bufs(count)[:slabs * LAG, span] = col_features(
            heads[...].reshape(slabs * LAG, units), col_proj[:units, span], col_off(span)
        )

    def moment_tile(k, lag, n, h):
        span, part = slice(n * col_tile, (n + 1) * col_tile), row_part(h)
        acc = lagged if lag else instant
        buf_r, buf_c = row_bufs(k), col_bufs(k)
        if k < count:
            value = jnp.dot(ready_rows[k, part] if k < ready and first else buf_r[part], buf_c[lag:lag + slab_rows, span], preferred_element_type=jnp.float32)
        else:
            value = jnp.dot(buf_r[part, :slabs * LAG], buf_c[:slabs * LAG, span], preferred_element_type=jnp.float32)
        if k > 0 or not first:
            value = acc[part, span] + value
        if last and k == (count if lag else count - 1):
            acc[part, span] = value * (1.0 / valid_rows)
            if n == COL_TILES - 1:
                start([stores[1 if lag else 0][h]])
        else:
            acc[part, span] = value

    def feature_steps(k):
        steps = [functools.partial(col_tile_features, k, n, h) for n in range(COL_TILES) for h in range(2)]
        if k >= ready:
            steps += [functools.partial(row_tile, k, u, h) for u in range(TIME_TILES) for h in range(2)]
        return steps

    def interleave(steps, others):
        done = 0
        for n, step in enumerate(steps):
            upto = (n + 1) * len(others) // len(steps)
            for other in others[done:upto]:
                other()
            done = upto
            step()

    stores = []
    if last:
        for m, (a, b) in enumerate(zip((instant, lagged), acc_out)):
            stores.append([
                pltpu.make_async_copy(
                    a.at[row_part(h)], b.at[pl.ds(pl.multiple_of(place * (rows // 2), 8), rows // 2), 0], out_sem.at[m, h]
                )
                for h, place in enumerate((col, 1 - col))
            ])

    if first:
        wait(col_loads)
        for step in feature_steps(0):
            step()
    for k in range(count - 1 if first else count):
        ahead = []
        steps = [functools.partial(moment_tile, k, lag, n, h) for lag in (0, LAG) for h in range(2) for n in range(COL_TILES)]
        if last and k == 0:
            steps.pop(0)()
            steps.pop(0)()
        if k + 1 < count:
            wait(loads[k + 1])
            if k == 0:
                start([copy for load in loads[ready + 1:] for copy in load] + edge_loads)
            ahead = feature_steps(k + 1)
        elif last:
            wait(edge_loads)
            ahead = [functools.partial(edge_cols, n) for n in range(COL_TILES)]
            ahead += [functools.partial(edge_rows, h) for h in range(2)]
        interleave(steps, ahead)
    if last:
        for h in range(2):
            for n in range(COL_TILES):
                moment_tile(count, LAG, n, h)
        wait(stores[0] + stores[1])


def moments(slabs, count, numbers, opened, panels, carry, slab_rows, valid_rows):
    first, last = carry is None, carry is not None
    units = slabs[0][0].shape[1]
    cols = panels[0].shape[1] if first else carry[0].shape[1]
    rows = 2 * cols
    at = len(slabs) - count
    ready = opened[0].shape[0] if first else 1
    if first:
        slabs = slabs[at + ready:]
    pieces = [p for s in slabs for p in s]
    end_shape = (rows, 1, cols)
    outs = [pltpu.VMEM((rows, cols), jnp.float32)] * 2
    dma = pltpu.SemaphoreType.DMA
    scratch = [
        pltpu.VMEM((count - ready, slab_rows, units), jnp.bfloat16),
        pltpu.VMEM((units, slab_rows // TIME_TILES), jnp.bfloat16),
        pltpu.VMEM((rows, slab_rows), jnp.bfloat16),
        pltpu.VMEM((rows, slab_rows), jnp.bfloat16),
        pltpu.VMEM((slab_rows + LAG, cols), jnp.bfloat16),
        pltpu.VMEM((slab_rows + LAG, cols), jnp.bfloat16),
        dma((count - ready, 2)),
    ]
    args = [numbers, *pieces]
    specs = [smem_spec()] + [any_spec()] * len(pieces)
    aliases = {}
    if first:
        args += [*map(in_vmem, opened), *panels[:2], *map(in_vmem, panels[2:])]
        specs += [vmem_spec()] * 2 + [any_spec()] * 2 + [vmem_spec()] * 2
        outs = outs + [
            pltpu.VMEM((units + SPARE, cols), jnp.bfloat16),
            pltpu.VMEM((rows, slab_rows), jnp.bfloat16),
            pltpu.VMEM((slab_rows + LAG, cols), jnp.bfloat16),
        ]
        out_specs = [vmem_spec()] * 5
        scratch.append(dma)
    else:
        outs, out_specs = [pltpu.HBM(end_shape, jnp.float32)] * 2 + outs, [hbm_spec()] * 2 + [vmem_spec()] * 2
        scratch += [pltpu.VMEM((len(slabs), LAG, units), jnp.bfloat16)] * 2
        scratch += [pltpu.VMEM((units, len(slabs) * LAG), jnp.bfloat16), dma((len(slabs), 2)), dma((2, 2))]
        args += [in_vmem(x) for x in (*panels, *carry[2:], *carry[:2])]
        specs += [vmem_spec()] * 7
        aliases = {len(args) - 2 + n: 2 + n for n in range(2)}
    return pl.pallas_call(
        functools.partial(moments_kernel, count, ready, at, last, slab_rows, valid_rows),
        in_specs=specs,
        out_specs=out_specs,
        out_shape=outs,
        scratch_shapes=scratch,
        input_output_aliases=aliases,
        compiler_params=pltpu.CompilerParams(vmem_limit_bytes=(24 if last else 16) * MIB),
        cost_estimate=pl.CostEstimate(
            flops=2 * count * slab_rows * (units * (rows + cols) + 2 * rows * cols),
            bytes_accessed=2 * count * slab_rows * units,
            transcendentals=count * slab_rows * (rows + cols),
        ),
    )(*args)


def on_device(states, projection, offsets):
    slab_rows = states.shape[0]
    tm_count = lax.axis_size("tm")
    tm, row, col = (lax.axis_index(a) for a in AXES)
    x_hi, y, core = tm // Y, tm % Y, row % 2
    valid_rows = slab_rows * tm_count - LAG
    cols = projection.shape[1]
    swap = lambda piece: move(piece, other_core)

    y_first, y_second = y - 1 + 2 * core, y + 1 - 2 * core
    place = lambda other, at: jnp.where(other, 1 - x_hi, x_hi) * Y + at % Y
    ids = [tm, place(False, y_first), place(False, y_second), place(True, y), place(False, y + 2),
           place(True, y_first), place(True, y_second), place(True, y + 2)]
    source, steps = jnp.where(core == y % 2, 0, 1), (row // 2 - tm // 2) % 4
    numbers = jnp.stack([*ids, core, col, source, steps]).astype(jnp.int32)
    after = len(ids)
    line = offsets[None, :]
    numbers, line = lax.optimization_barrier((numbers, line))
    sizes = (slab_rows, valid_rows)

    columns, turned, mine = prepare(after, numbers, projection, line, states)
    ahead, behind = move(columns, along_z(1)), move(columns, along_z(-1))
    over, partner, y_out = move(mine, crossing), move(turned, inner), move(mine, out_y)
    ahead, columns = lax.optimization_barrier((ahead, columns))
    beyond = move(columns, along_z(2))
    y_out, mine = lax.optimization_barrier((y_out, mine))
    y_back = move(mine, back_y)
    over, y_out = lax.optimization_barrier((over, y_out))
    swapped_out = swap(y_out)
    ahead, behind, beyond, partner, y_back, swapped_out = lax.optimization_barrier(
        (ahead, behind, beyond, partner, y_back, swapped_out)
    )

    panel = pick(after + 3, numbers, columns, ahead, beyond, behind)
    swapped = swap(panel)
    swapped_back, swapped_over = swap(y_back), swap(over)
    slabs = [(in_hbm(states),), (y_out, swapped_back), (y_back, swapped_out)]
    row_proj, row_off, *opened = opening(slabs, numbers, turned, partner, line, *sizes)

    over_out, y_far, over_back = move(over, out_y), move(y_out, out_y), move(y_back, crossing)
    row_off, over_out = lax.optimization_barrier((row_off, over_out))
    over_far = move(over_out, out_y)
    slabs += [(over, swapped_over)]
    carry = moments(slabs, 4, numbers, opened, (panel, swapped, row_proj, row_off), None, *sizes)

    *carry, y_far, over_back = lax.optimization_barrier((*carry, y_far, over_back))
    swapped_far, swapped_over_back = swap(y_far), swap(over_back)
    swapped_far, swapped_over_back, over_far = lax.optimization_barrier((swapped_far, swapped_over_back, over_far))
    slabs += [(y_far, swapped_far), (over_out, swapped_over_back), (over_back, swap(over_out)), (over_far, swap(over_far))]
    instant, lagged, *_ = moments(slabs, 5, numbers, None, (row_proj, row_off), carry, *sizes)
    return instant, lagged


def solution(mesh):
    return jax.shard_map(
        on_device,
        mesh=mesh,
        in_specs=(P("tm", None), P(None, ("row", "col")), P(("row", "col"))),
        out_specs=(P("row", "tm", "col"), P("row", "tm", "col")),
        check_vma=False,
    )
```

```python
import functools
import jax
import jax.numpy as jnp
from jax import lax
from jax.experimental import pallas as pl
from jax.experimental.pallas import tpu as pltpu
from jax.sharding import PartitionSpec as P

LAG = 64
Y = 4
AXES = ("tm", "row", "col")
SPARE = 16
MIB = 1024 * 1024
TIME_TILES, COL_TILES = 1, 1


def route(target):
    tm_count, row_count, col_count = (lax.axis_size(a) for a in AXES)
    flat = lambda tm, row, col: (tm * row_count + row) * col_count + col
    pairs = []
    for tm in range(tm_count):
        for row in range(row_count):
            for col in range(col_count):
                to = target(tm // Y, tm % Y, row // 2, row % 2, col)
                if to is not None:
                    x_hi, y, z, core, x_lo = to
                    pairs.append((flat(tm, row, col), flat(x_hi * Y + y % Y, z * 2 + core, x_lo)))
    return pairs


def move(block, target):
    return lax.ppermute(block, AXES, route(target))


def crossing(x_hi, y, z, core, x_lo):
    return 1 - x_hi, y, z, core, 1 - x_lo


def inner(x_hi, y, z, core, x_lo):
    return x_hi, y, z, core, 1 - x_lo


def other_core(x_hi, y, z, core, x_lo):
    return x_hi, y, z, 1 - core, x_lo


def along_y(step):
    return lambda x_hi, y, z, core, x_lo: (x_hi, y + step, z, core, x_lo)


def out_y(x_hi, y, z, core, x_lo):
    return x_hi, y + 1 - 2 * core, z, core, x_lo


def back_y(x_hi, y, z, core, x_lo):
    return x_hi, y - 1 + 2 * core, z, core, x_lo


def along_z(step):
    def target(x_hi, y, z, core, x_lo):
        return (x_hi, y, (z + step) % 4, core, x_lo) if x_hi * Y + y == z * 2 + core else None
    return target


def any_spec():
    return pl.BlockSpec(memory_space=pl.ANY)


def vmem_spec():
    return pl.BlockSpec(memory_space=pltpu.VMEM)


def hbm_spec():
    return pl.BlockSpec(memory_space=pltpu.HBM)


def in_hbm(x):
    return pltpu.with_memory_space_constraint(x, pltpu.HBM)


def in_vmem(x):
    return pltpu.with_memory_space_constraint(x, pltpu.VMEM)


def smem_spec():
    return pl.BlockSpec(memory_space=pltpu.SMEM)


def row_features(row_proj, turned, row_off, start, valid_rows):
    row_off = jnp.concatenate([row_off] * (turned.shape[1] // row_off.shape[1]), axis=1)
    features = jnp.tanh(jnp.dot(row_proj, turned, preferred_element_type=jnp.float32) + row_off)
    position = start + lax.broadcasted_iota(jnp.int32, (1, turned.shape[1]), 1)
    return jnp.where(position < valid_rows, features, 0.0).astype(jnp.bfloat16)


def col_features(states, col_proj, col_off):
    return jnp.tanh(
        jnp.dot(states, col_proj, preferred_element_type=jnp.float32) + col_off
    ).astype(jnp.bfloat16)


def start(copies):
    for copy in copies:
        copy.start()


def wait(copies):
    for copy in copies:
        copy.wait()


def prepare_kernel(at, numbers, projection, offsets, states, columns, turned, mine, line, sems):
    half = mine.shape[0]
    units, cols = projection.shape
    copies = [
        pltpu.make_async_copy(projection, columns.at[pl.ds(0, units)], sems.at[0]),
        pltpu.make_async_copy(offsets, line, sems.at[1]),
        pltpu.make_async_copy(states.at[pl.ds(pl.multiple_of(numbers[at] * half, 16), half)], mine, sems.at[2]),
    ]
    start(copies)
    turned[cols:] = jnp.zeros_like(turned[cols:])
    wait(copies[1:2])
    high = line[...].astype(jnp.bfloat16)
    rest = line[...] - high.astype(jnp.float32)
    middle = rest.astype(jnp.bfloat16)
    low = (rest - middle.astype(jnp.float32)).astype(jnp.bfloat16)
    parts = jnp.concatenate([high, middle, low, jnp.zeros((SPARE - 3, cols), jnp.bfloat16)], axis=0)
    columns[units:] = parts
    turned[cols:, :cols] = parts
    wait(copies[:1])
    turned[:cols] = columns[:units].T
    wait(copies[2:])


def prepare(at, numbers, projection, offsets, states):
    units, cols = projection.shape
    half = states.shape[0] // 2
    return pl.pallas_call(
        functools.partial(prepare_kernel, at),
        in_specs=[smem_spec(), hbm_spec(), hbm_spec(), hbm_spec()],
        out_specs=[vmem_spec(), vmem_spec(), vmem_spec()],
        out_shape=[jax.ShapeDtypeStruct((units + SPARE, cols), jnp.bfloat16),
                   jax.ShapeDtypeStruct((cols + SPARE, units), jnp.bfloat16),
                   jax.ShapeDtypeStruct((half, units), jnp.bfloat16)],
        scratch_shapes=[pltpu.VMEM((1, cols), jnp.float32), pltpu.SemaphoreType.DMA((3,))],
        compiler_params=pltpu.CompilerParams(vmem_limit_bytes=12 * MIB),
    )(numbers, in_hbm(projection), in_hbm(offsets), in_hbm(states))


class OneOf:
    def __init__(self, number, sources, dst, sem):
        self.number, self.copies = number, [pltpu.make_async_copy(x, dst, sem) for x in sources]

    def start(self):
        for n, copy in enumerate(self.copies):
            pl.when(self.number == n)(copy.start)

    def wait(self):
        self.copies[0].wait()


def pick_kernel(at, numbers, *refs):
    *sources, out, sem = refs
    copy = OneOf(numbers[at], sources, out, sem)
    copy.start()
    copy.wait()


def pick(at, numbers, *sources):
    return pl.pallas_call(
        functools.partial(pick_kernel, at),
        in_specs=[smem_spec()] + [any_spec()] * len(sources),
        out_specs=vmem_spec(),
        out_shape=jax.ShapeDtypeStruct(sources[0].shape, sources[0].dtype),
        scratch_shapes=[pltpu.SemaphoreType.DMA],
        compiler_params=pltpu.CompilerParams(vmem_limit_bytes=8 * MIB),
    )(numbers, *sources)


def slab_copies(pieces, core, dst, sems):
    if len(pieces) == 1:
        return [pltpu.make_async_copy(pieces[0], dst, sems.at[0])]
    half = pieces[0].shape[0]
    return [
        pltpu.make_async_copy(piece, dst.at[pl.ds(pl.multiple_of(place * half, 16), half)], sems.at[n])
        for n, (piece, place) in enumerate(zip(pieces, (core, 1 - core)))
    ]


def lane_broadcast(line):
    return jnp.broadcast_to(line, (128, line.shape[1])).T


def opening_kernel(count, valid_rows, ids, *refs):
    refs = list(refs)
    take = lambda n: [refs.pop(0) for _ in range(n)]
    pieces = [take(1 if k == 0 else 2) for k in range(count)]
    turned, partner, offsets = take(3)
    row_proj, row_off, slab, features, parts, proj_sem, in_sem = take(7)
    rows = row_proj.shape[0]
    own, slab_rows = rows // 2, slab.shape[1]
    core = ids[(valid_rows + LAG) // slab_rows]
    row_loads = [
        pltpu.make_async_copy(turned.at[pl.ds(0, own)], row_proj.at[pl.ds(0, own)], proj_sem.at[0]),
        pltpu.make_async_copy(partner.at[pl.ds(0, own)], row_proj.at[pl.ds(own, own)], proj_sem.at[1]),
        pltpu.make_async_copy(partner.at[pl.ds(own, SPARE)], parts, proj_sem.at[2]),
    ]
    loads = [slab_copies(pieces[k], core, slab.at[k], in_sem.at[k]) for k in range(count)]
    start([*row_loads, *loads[0]])
    row_off[:own] = lane_broadcast(offsets[...])
    wait(row_loads)
    start([copy for load in loads[1:] for copy in load])
    row_off[own:] = lane_broadcast(jnp.sum(parts[:, :own].astype(jnp.float32), axis=0, keepdims=True))
    tile = slab_rows // TIME_TILES
    for k in range(count):
        wait(loads[k])
        for u in range(TIME_TILES):
            span = slice(u * tile, (u + 1) * tile)
            turned_states = slab[k, span].T
            for part in (slice(0, own), slice(own, rows)):
                features[k, part, span] = row_features(
                    row_proj[part], turned_states, row_off[part], ids[k] * slab_rows + u * tile, valid_rows
                )


def opening(slabs, numbers, turned, partner, offsets, slab_rows, valid_rows):
    rows, units, count = 2 * (turned.shape[0] - SPARE), turned.shape[1], len(slabs)
    pieces = [p for s in slabs for p in s]
    dma = pltpu.SemaphoreType.DMA
    return pl.pallas_call(
        functools.partial(opening_kernel, count, valid_rows),
        in_specs=[smem_spec()] + [any_spec()] * (len(pieces) + 2) + [vmem_spec()],
        out_specs=[vmem_spec()] * 4,
        out_shape=[
            pltpu.VMEM((rows, units), jnp.bfloat16),
            pltpu.VMEM((rows, 128), jnp.float32),
            pltpu.VMEM((count, slab_rows, units), jnp.bfloat16),
            pltpu.VMEM((count, rows, slab_rows), jnp.bfloat16),
        ],
        scratch_shapes=[pltpu.VMEM((SPARE, units), jnp.bfloat16), dma((3,)), dma((count, 2))],
        compiler_params=pltpu.CompilerParams(vmem_limit_bytes=12 * MIB),
        cost_estimate=pl.CostEstimate(
            flops=2 * count * slab_rows * units * rows, bytes_accessed=2 * count * slab_rows * units,
            transcendentals=count * slab_rows * rows,
        ),
    )(numbers, *pieces, turned, partner, offsets)


def moments_kernel(count, ready, at, last, slab_rows, valid_rows, *refs):
    first = not last
    refs = list(refs)
    take = lambda n: [refs.pop(0) for _ in range(n)]
    (ids,) = take(1)
    slabs = (valid_rows + LAG) // slab_rows
    pieces = [take(1 if last and k == 0 else 2) for k in range(slabs if last else count - ready)]
    here = [None] * ready + pieces[ready - count:]
    if first:
        ready_slab, ready_rows, *columns, row_proj, row_off = take(6)
    else:
        row_proj, row_off, col_proj, row_next, col_next = take(5)
        take(2)
        acc_out = take(2)
    instant, lagged = take(2)
    if first:
        col_proj, row_next, col_next = take(3)
    slab, turned_states, row_a, row_b, col_a, col_b, in_sem = take(7)
    if first:
        (proj_sem,) = take(1)
    if last:
        tails, heads, turned_edges, edge_sem, out_sem = take(5)
    rows, cols = instant.shape
    units = col_proj.shape[0] - SPARE
    half = slab_rows // 2
    time_tile, col_tile = slab_rows // TIME_TILES, cols // COL_TILES
    core, col, source = ids[slabs], ids[slabs + 1], ids[slabs + 2]
    number = lambda k: ids[at + k]

    loads = [[] if k < ready else slab_copies(here[k], core, slab.at[k - ready], in_sem.at[k - ready]) for k in range(count)]
    states = lambda k: ready_slab.at[k] if k < ready else slab.at[k - ready]
    between = count - 1 if first else 0
    row_bufs = lambda k: row_next if k == between else (row_a, row_b)[k % 2]
    col_bufs = lambda k: col_next if k == between else (col_a, col_b)[k % 2]
    col_loads, edge_loads = [], []
    if first:
        col_loads = [OneOf(source, columns, col_proj, proj_sem)]
    if last:
        for k, piece in enumerate(pieces):
            tail, head = tails.at[ids[k]], heads.at[lax.rem(ids[k] + slabs - 1, slabs)]
            if len(piece) == 1:
                edge_loads.append(pltpu.make_async_copy(piece[0].at[pl.ds(slab_rows - LAG, LAG)], tail, edge_sem.at[k, 0]))
                edge_loads.append(pltpu.make_async_copy(piece[0].at[pl.ds(0, LAG)], head, edge_sem.at[k, 1]))
            else:
                ends = [p.at[pl.ds(half - LAG, LAG)] for p in piece]
                starts = [p.at[pl.ds(0, LAG)] for p in piece]
                edge_loads.append(OneOf(1 - core, ends, tail, edge_sem.at[k, 0]))
                edge_loads.append(OneOf(core, starts, head, edge_sem.at[k, 1]))
    start([*col_loads, *loads[ready]])

    for buf in (col_a, col_b) + ((col_next,) if first else ()):
        buf[slab_rows:] = jnp.zeros_like(buf[slab_rows:])

    row_part = lambda h: slice(h * rows // 2, (h + 1) * rows // 2)

    def row_tile(k, u, h):
        span, part = slice(u * time_tile, (u + 1) * time_tile), row_part(h)
        if h == 0:
            turned_states[...] = states(k)[span].T
        row_bufs(k)[part, span] = row_features(
            row_proj[part], turned_states[...], row_off[part], number(k) * slab_rows + u * time_tile, valid_rows
        )

    def col_off(span):
        return jnp.sum(col_proj[units:, span].astype(jnp.float32), axis=0, keepdims=True)

    def col_tile_features(k, n, h):
        span, part = slice(n * col_tile, (n + 1) * col_tile), slice(h * half, (h + 1) * half)
        col_bufs(k)[part, span] = col_features(states(k)[part], col_proj[:units, span], col_off(span))

    def edge_rows(h):
        size, part = slabs * LAG, row_part(h)
        if h == 0:
            turned_edges[...] = tails[...].reshape(size, units).T
        row_bufs(count)[part, :size] = row_features(
            row_proj[part], turned_edges[...], row_off[part], 0, (slabs - 1) * LAG
        )

    def edge_cols(n):
        span = slice(n * col_tile, (n + 1) * col_tile)
        col_bufs(count)[:slabs * LAG, span] = col_features(
            heads[...].reshape(slabs * LAG, units), col_proj[:units, span], col_off(span)
        )

    def moment_tile(k, lag, n, h, parts=2):
        span, part = slice(n * col_tile, (n + 1) * col_tile), slice(h * rows // parts, (h + 1) * rows // parts)
        acc = lagged if lag else instant
        buf_r, buf_c = row_bufs(k), col_bufs(k)
        if k < count:
            value = jnp.dot(ready_rows[k, part] if k < ready and first else buf_r[part], buf_c[lag:lag + slab_rows, span], preferred_element_type=jnp.float32)
        else:
            value = jnp.dot(buf_r[part, :slabs * LAG], buf_c[:slabs * LAG, span], preferred_element_type=jnp.float32)
        if k > 0 or not first:
            value = acc[part, span] + value
        if last and k == (count if lag else count - 1):
            acc[part, span] = value * (1.0 / valid_rows)
            if n == COL_TILES - 1:
                start([stores[1 if lag else 0][h]])
        else:
            acc[part, span] = value

    def feature_steps(k):
        steps = [functools.partial(col_tile_features, k, n, h) for n in range(COL_TILES) for h in range(2)]
        if k >= ready:
            steps += [functools.partial(row_tile, k, u, h) for u in range(TIME_TILES) for h in range(2)]
        return steps

    def interleave(steps, others):
        done = 0
        for n, step in enumerate(steps):
            upto = (n + 1) * len(others) // len(steps)
            for other in others[done:upto]:
                other()
            done = upto
            step()

    stores = []
    if last:
        for m, (a, b) in enumerate(zip((instant, lagged), acc_out)):
            size = rows // 2 // (m + 1)
            stores.append([
                pltpu.make_async_copy(
                    a.at[pl.ds(h * size, size)],
                    b.at[pl.ds(pl.multiple_of(place * (rows // 2) + h % (m + 1) * size, 8), size), 0], out_sem.at[m, h]
                )
                for h, place in enumerate([col] * (m + 1) + [1 - col] * (m + 1))
            ])

    if first:
        wait(col_loads)
        for step in feature_steps(0):
            step()
    for k in range(count - 1 if first else count):
        ahead = []
        steps = [functools.partial(moment_tile, k, lag, n, h) for lag in (0, LAG) for h in range(2) for n in range(COL_TILES)]
        if last and k == 0:
            steps.pop(0)()
            steps.pop(0)()
        if k + 1 < count:
            wait(loads[k + 1])
            if k + 2 < count:
                start(loads[k + 2] if last else [])
            elif last:
                start(edge_loads)
            ahead = feature_steps(k + 1)
        elif last:
            wait(edge_loads)
            ahead = [functools.partial(edge_cols, n) for n in range(COL_TILES)]
            ahead += [functools.partial(edge_rows, h) for h in range(2)]
        interleave(steps, ahead)
    if last:
        for h in range(4):
            for n in range(COL_TILES):
                moment_tile(count, LAG, n, h, 4)
        wait(stores[0] + stores[1])


def moments(slabs, count, numbers, opened, panels, carry, slab_rows, valid_rows):
    first, last = carry is None, carry is not None
    units = slabs[0][0].shape[1]
    cols = panels[0].shape[1] if first else carry[0].shape[1]
    rows = 2 * cols
    at = len(slabs) - count
    ready = opened[0].shape[0] if first else 1
    if first:
        slabs = slabs[at + ready:]
    pieces = [p for s in slabs for p in s]
    end_shape = (rows, 1, cols)
    outs = [pltpu.VMEM((rows, cols), jnp.float32)] * 2
    dma = pltpu.SemaphoreType.DMA
    scratch = [
        pltpu.VMEM((count - ready, slab_rows, units), jnp.bfloat16),
        pltpu.VMEM((units, slab_rows // TIME_TILES), jnp.bfloat16),
        pltpu.VMEM((rows, slab_rows), jnp.bfloat16),
        pltpu.VMEM((rows, slab_rows), jnp.bfloat16),
        pltpu.VMEM((slab_rows + LAG, cols), jnp.bfloat16),
        pltpu.VMEM((slab_rows + LAG, cols), jnp.bfloat16),
        dma((count - ready, 2)),
    ]
    args = [numbers, *pieces]
    specs = [smem_spec()] + [any_spec()] * len(pieces)
    aliases = {}
    if first:
        args += [*map(in_vmem, opened), *panels[:2], *map(in_vmem, panels[2:])]
        specs += [vmem_spec()] * 2 + [any_spec()] * 2 + [vmem_spec()] * 2
        outs = outs + [
            pltpu.VMEM((units + SPARE, cols), jnp.bfloat16),
            pltpu.VMEM((rows, slab_rows), jnp.bfloat16),
            pltpu.VMEM((slab_rows + LAG, cols), jnp.bfloat16),
        ]
        out_specs = [vmem_spec()] * 5
        scratch.append(dma)
    else:
        outs, out_specs = [pltpu.HBM(end_shape, jnp.float32)] * 2 + outs, [hbm_spec()] * 2 + [vmem_spec()] * 2
        scratch += [pltpu.VMEM((len(slabs), LAG, units), jnp.bfloat16)] * 2
        scratch += [pltpu.VMEM((units, len(slabs) * LAG), jnp.bfloat16), dma((len(slabs), 2)), dma((2, 4))]
        args += [in_vmem(x) for x in (*panels, *carry[2:], *carry[:2])]
        specs += [vmem_spec()] * 7
        aliases = {len(args) - 2 + n: 2 + n for n in range(2)}
    return pl.pallas_call(
        functools.partial(moments_kernel, count, ready, at, last, slab_rows, valid_rows),
        in_specs=specs,
        out_specs=out_specs,
        out_shape=outs,
        scratch_shapes=scratch,
        input_output_aliases=aliases,
        compiler_params=pltpu.CompilerParams(vmem_limit_bytes=(24 if last else 16) * MIB),
        cost_estimate=pl.CostEstimate(
            flops=2 * count * slab_rows * (units * (rows + cols) + 2 * rows * cols),
            bytes_accessed=2 * count * slab_rows * units,
            transcendentals=count * slab_rows * (rows + cols),
        ),
    )(*args)


def on_device(states, projection, offsets):
    slab_rows = states.shape[0]
    tm_count = lax.axis_size("tm")
    tm, row, col = (lax.axis_index(a) for a in AXES)
    x_hi, y, core = tm // Y, tm % Y, row % 2
    valid_rows = slab_rows * tm_count - LAG
    cols = projection.shape[1]
    swap = lambda piece: move(piece, other_core)

    y_first, y_second = y - 1 + 2 * core, y + 1 - 2 * core
    place = lambda other, at: jnp.where(other, 1 - x_hi, x_hi) * Y + at % Y
    ids = [tm, place(False, y_first), place(False, y_second), place(True, y), place(False, y + 2),
           place(True, y_first), place(True, y_second), place(True, y + 2)]
    source, steps = jnp.where(core == y % 2, 0, 1), (row // 2 - tm // 2) % 4
    numbers = jnp.stack([*ids, core, col, source, steps]).astype(jnp.int32)
    after = len(ids)
    line = offsets[None, :]
    numbers, line = lax.optimization_barrier((numbers, line))
    sizes = (slab_rows, valid_rows)

    columns, turned, mine = prepare(after, numbers, projection, line, states)
    partner, over, y_out = move(turned, inner), move(mine, crossing), move(mine, out_y)
    ahead, behind = move(columns, along_z(1)), move(columns, along_z(-1))
    ahead, columns = lax.optimization_barrier((ahead, columns))
    beyond = move(columns, along_z(2))
    y_out, mine = lax.optimization_barrier((y_out, mine))
    y_back = move(mine, back_y)
    over, y_out = lax.optimization_barrier((over, y_out))
    swapped_out = swap(y_out)
    ahead, behind, beyond, partner, y_back, swapped_out = lax.optimization_barrier(
        (ahead, behind, beyond, partner, y_back, swapped_out)
    )

    panel = pick(after + 3, numbers, columns, ahead, beyond, behind)
    swapped = swap(panel)
    swapped_back, swapped_over = swap(y_back), swap(over)
    slabs = [(in_hbm(states),), (y_out, swapped_back), (y_back, swapped_out)]
    row_proj, row_off, *opened = opening(slabs, numbers, turned, partner, line, *sizes)

    over_out, y_far, over_back = move(over, out_y), move(y_out, out_y), move(y_back, crossing)
    row_off, over_out = lax.optimization_barrier((row_off, over_out))
    over_far = move(over_out, out_y)
    slabs += [(over, swapped_over)]
    carry = moments(slabs, 4, numbers, opened, (panel, swapped, row_proj, row_off), None, *sizes)

    *carry, y_far, over_back = lax.optimization_barrier((*carry, y_far, over_back))
    swapped_far, swapped_over_back = swap(y_far), swap(over_back)
    swapped_far, swapped_over_back, over_far = lax.optimization_barrier((swapped_far, swapped_over_back, over_far))
    slabs += [(y_far, swapped_far), (over_out, swapped_over_back), (over_back, swap(over_out)), (over_far, swap(over_far))]
    instant, lagged, *_ = moments(slabs, 5, numbers, None, (row_proj, row_off), carry, *sizes)
    return instant, lagged


def solution(mesh):
    return jax.shard_map(
        on_device,
        mesh=mesh,
        in_specs=(P("tm", None), P(None, ("row", "col")), P(("row", "col"))),
        out_specs=(P("row", "tm", "col"), P("row", "tm", "col")),
        check_vma=False,
    )
```

```python
import functools
import jax
import jax.numpy as jnp
from jax import lax
from jax.experimental import pallas as pl
from jax.experimental.pallas import tpu as pltpu
from jax.sharding import PartitionSpec as P

LAG = 64
Y = 4
AXES = ("tm", "row", "col")
SPARE = 16
MIB = 1024 * 1024
TIME_TILES, COL_TILES = 1, 1


def route(target):
    tm_count, row_count, col_count = (lax.axis_size(a) for a in AXES)
    flat = lambda tm, row, col: (tm * row_count + row) * col_count + col
    pairs = []
    for tm in range(tm_count):
        for row in range(row_count):
            for col in range(col_count):
                to = target(tm // Y, tm % Y, row // 2, row % 2, col)
                if to is not None:
                    x_hi, y, z, core, x_lo = to
                    pairs.append((flat(tm, row, col), flat(x_hi * Y + y % Y, z * 2 + core, x_lo)))
    return pairs


def move(block, target):
    return lax.ppermute(block, AXES, route(target))


def crossing(x_hi, y, z, core, x_lo):
    return 1 - x_hi, y, z, core, 1 - x_lo


def inner(x_hi, y, z, core, x_lo):
    return x_hi, y, z, core, 1 - x_lo


def other_core(x_hi, y, z, core, x_lo):
    return x_hi, y, z, 1 - core, x_lo


def along_y(step):
    return lambda x_hi, y, z, core, x_lo: (x_hi, y + step, z, core, x_lo)


def out_y(x_hi, y, z, core, x_lo):
    return x_hi, y + 1 - 2 * core, z, core, x_lo


def back_y(x_hi, y, z, core, x_lo):
    return x_hi, y - 1 + 2 * core, z, core, x_lo


def along_z(step):
    def target(x_hi, y, z, core, x_lo):
        return (x_hi, y, (z + step) % 4, core, x_lo) if x_hi * Y + y == z * 2 + core else None
    return target


def any_spec():
    return pl.BlockSpec(memory_space=pl.ANY)


def vmem_spec():
    return pl.BlockSpec(memory_space=pltpu.VMEM)


def hbm_spec():
    return pl.BlockSpec(memory_space=pltpu.HBM)


def in_hbm(x):
    return pltpu.with_memory_space_constraint(x, pltpu.HBM)


def in_vmem(x):
    return pltpu.with_memory_space_constraint(x, pltpu.VMEM)


def smem_spec():
    return pl.BlockSpec(memory_space=pltpu.SMEM)


def row_features(row_proj, turned, row_off, start, valid_rows):
    row_off = jnp.concatenate([row_off] * (turned.shape[1] // row_off.shape[1]), axis=1)
    features = jnp.tanh(jnp.dot(row_proj, turned, preferred_element_type=jnp.float32) + row_off)
    position = start + lax.broadcasted_iota(jnp.int32, (1, turned.shape[1]), 1)
    return jnp.where(position < valid_rows, features, 0.0).astype(jnp.bfloat16)


def col_features(states, col_proj, col_off):
    return jnp.tanh(
        jnp.dot(states, col_proj, preferred_element_type=jnp.float32) + col_off
    ).astype(jnp.bfloat16)


def start(copies):
    for copy in copies:
        copy.start()


def wait(copies):
    for copy in copies:
        copy.wait()


def prepare_kernel(at, numbers, projection, offsets, states, columns, turned, mine, line, sems):
    half = mine.shape[0]
    units, cols = projection.shape
    copies = [
        pltpu.make_async_copy(projection, columns.at[pl.ds(0, units)], sems.at[0]),
        pltpu.make_async_copy(offsets, line, sems.at[1]),
        pltpu.make_async_copy(states.at[pl.ds(pl.multiple_of(numbers[at] * half, 16), half)], mine, sems.at[2]),
    ]
    start(copies)
    turned[cols:] = jnp.zeros_like(turned[cols:])
    wait(copies[1:2])
    high = line[...].astype(jnp.bfloat16)
    rest = line[...] - high.astype(jnp.float32)
    middle = rest.astype(jnp.bfloat16)
    low = (rest - middle.astype(jnp.float32)).astype(jnp.bfloat16)
    parts = jnp.concatenate([high, middle, low, jnp.zeros((SPARE - 3, cols), jnp.bfloat16)], axis=0)
    columns[units:] = parts
    turned[cols:, :cols] = parts
    wait(copies[:1])
    turned[:cols] = columns[:units].T
    wait(copies[2:])


def prepare(at, numbers, projection, offsets, states):
    units, cols = projection.shape
    half = states.shape[0] // 2
    return pl.pallas_call(
        functools.partial(prepare_kernel, at),
        in_specs=[smem_spec(), hbm_spec(), hbm_spec(), hbm_spec()],
        out_specs=[vmem_spec(), vmem_spec(), vmem_spec()],
        out_shape=[jax.ShapeDtypeStruct((units + SPARE, cols), jnp.bfloat16),
                   jax.ShapeDtypeStruct((cols + SPARE, units), jnp.bfloat16),
                   jax.ShapeDtypeStruct((half, units), jnp.bfloat16)],
        scratch_shapes=[pltpu.VMEM((1, cols), jnp.float32), pltpu.SemaphoreType.DMA((3,))],
        compiler_params=pltpu.CompilerParams(vmem_limit_bytes=12 * MIB),
    )(numbers, in_hbm(projection), in_hbm(offsets), in_hbm(states))


class OneOf:
    def __init__(self, number, sources, dst, sem):
        self.number, self.copies = number, [pltpu.make_async_copy(x, dst, sem) for x in sources]

    def start(self):
        for n, copy in enumerate(self.copies):
            pl.when(self.number == n)(copy.start)

    def wait(self):
        self.copies[0].wait()


def pick_kernel(at, numbers, *refs):
    *sources, out, sem = refs
    copy = OneOf(numbers[at], sources, out, sem)
    copy.start()
    copy.wait()


def pick(at, numbers, *sources):
    return pl.pallas_call(
        functools.partial(pick_kernel, at),
        in_specs=[smem_spec()] + [any_spec()] * len(sources),
        out_specs=vmem_spec(),
        out_shape=jax.ShapeDtypeStruct(sources[0].shape, sources[0].dtype),
        scratch_shapes=[pltpu.SemaphoreType.DMA],
        compiler_params=pltpu.CompilerParams(vmem_limit_bytes=8 * MIB),
    )(numbers, *sources)


def slab_copies(pieces, core, dst, sems):
    if len(pieces) == 1:
        return [pltpu.make_async_copy(pieces[0], dst, sems.at[0])]
    half = pieces[0].shape[0]
    return [
        pltpu.make_async_copy(piece, dst.at[pl.ds(pl.multiple_of(place * half, 16), half)], sems.at[n])
        for n, (piece, place) in enumerate(zip(pieces, (core, 1 - core)))
    ]


def lane_broadcast(line):
    return jnp.broadcast_to(line, (128, line.shape[1])).T


def opening_kernel(count, valid_rows, ids, *refs):
    refs = list(refs)
    take = lambda n: [refs.pop(0) for _ in range(n)]
    pieces = [take(1 if k == 0 else 2) for k in range(count)]
    turned, partner, offsets = take(3)
    row_proj, row_off, slab, features, parts, proj_sem, in_sem = take(7)
    rows = row_proj.shape[0]
    own, slab_rows = rows // 2, slab.shape[1]
    core = ids[(valid_rows + LAG) // slab_rows]
    row_loads = [
        pltpu.make_async_copy(turned.at[pl.ds(0, own)], row_proj.at[pl.ds(0, own)], proj_sem.at[0]),
        pltpu.make_async_copy(partner.at[pl.ds(0, own)], row_proj.at[pl.ds(own, own)], proj_sem.at[1]),
        pltpu.make_async_copy(partner.at[pl.ds(own, SPARE)], parts, proj_sem.at[2]),
    ]
    loads = [slab_copies(pieces[k], core, slab.at[k], in_sem.at[k]) for k in range(count)]
    start([*row_loads, *loads[0]])
    row_off[:own] = lane_broadcast(offsets[...])
    wait(row_loads)
    start([copy for load in loads[1:] for copy in load])
    row_off[own:] = lane_broadcast(jnp.sum(parts[:, :own].astype(jnp.float32), axis=0, keepdims=True))
    tile = slab_rows // TIME_TILES
    for k in range(count):
        wait(loads[k])
        for u in range(TIME_TILES):
            span = slice(u * tile, (u + 1) * tile)
            turned_states = slab[k, span].T
            for part in (slice(0, own), slice(own, rows)):
                features[k, part, span] = row_features(
                    row_proj[part], turned_states, row_off[part], ids[k] * slab_rows + u * tile, valid_rows
                )


def opening(slabs, numbers, turned, partner, offsets, slab_rows, valid_rows):
    rows, units, count = 2 * (turned.shape[0] - SPARE), turned.shape[1], len(slabs)
    pieces = [p for s in slabs for p in s]
    dma = pltpu.SemaphoreType.DMA
    return pl.pallas_call(
        functools.partial(opening_kernel, count, valid_rows),
        in_specs=[smem_spec()] + [any_spec()] * (len(pieces) + 2) + [vmem_spec()],
        out_specs=[vmem_spec()] * 4,
        out_shape=[
            pltpu.VMEM((rows, units), jnp.bfloat16),
            pltpu.VMEM((rows, 128), jnp.float32),
            pltpu.VMEM((count, slab_rows, units), jnp.bfloat16),
            pltpu.VMEM((count, rows, slab_rows), jnp.bfloat16),
        ],
        scratch_shapes=[pltpu.VMEM((SPARE, units), jnp.bfloat16), dma((3,)), dma((count, 2))],
        compiler_params=pltpu.CompilerParams(vmem_limit_bytes=12 * MIB),
        cost_estimate=pl.CostEstimate(
            flops=2 * count * slab_rows * units * rows, bytes_accessed=2 * count * slab_rows * units,
            transcendentals=count * slab_rows * rows,
        ),
    )(numbers, *pieces, turned, partner, offsets)


def moments_kernel(count, ready, at, last, slab_rows, valid_rows, *refs):
    first = not last
    refs = list(refs)
    take = lambda n: [refs.pop(0) for _ in range(n)]
    (ids,) = take(1)
    slabs = (valid_rows + LAG) // slab_rows
    pieces = [None] * ready + [take(2) for _ in range(count - ready)]
    if first:
        ready_slab, ready_rows, *columns, row_proj, row_off = take(6)
    else:
        row_proj, row_off, col_proj, row_next, col_next = take(5)
        take(4)
        acc_out = take(2)
    instant, lagged, tails, heads = take(4)
    if first:
        col_proj, row_next, col_next = take(3)
    slab, turned_states, row_a, row_b, col_a, col_b, in_sem = take(7)
    if first:
        (proj_sem,) = take(1)
    if last:
        turned_edges, out_sem = take(2)
    rows, cols = instant.shape
    units = col_proj.shape[0] - SPARE
    half = slab_rows // 2
    time_tile, col_tile = slab_rows // TIME_TILES, cols // COL_TILES
    core, col, source = ids[slabs], ids[slabs + 1], ids[slabs + 2]
    number = lambda k: ids[at + k]

    loads = [[] if k < ready else slab_copies(pieces[k], core, slab.at[k - ready], in_sem.at[k - ready]) for k in range(count)]
    states = lambda k: ready_slab.at[k] if k < ready else slab.at[k - ready]
    between = count - 1 if first else 0
    row_bufs = lambda k: row_next if k == between else (row_a, row_b)[k % 2]
    col_bufs = lambda k: col_next if k == between else (col_a, col_b)[k % 2]
    col_loads = [OneOf(source, columns, col_proj, proj_sem)] if first else []

    def keep_borders(k):
        tails[number(k)] = states(k)[slab_rows - LAG:]
        heads[lax.rem(number(k) + slabs - 1, slabs)] = states(k)[:LAG]

    start([*col_loads, *loads[ready]])

    for buf in (col_a, col_b) + ((col_next,) if first else ()):
        buf[slab_rows:] = jnp.zeros_like(buf[slab_rows:])

    row_part = lambda h: slice(h * rows // 2, (h + 1) * rows // 2)

    def row_tile(k, u, h):
        span, part = slice(u * time_tile, (u + 1) * time_tile), row_part(h)
        if h == 0:
            turned_states[...] = states(k)[span].T
        row_bufs(k)[part, span] = row_features(
            row_proj[part], turned_states[...], row_off[part], number(k) * slab_rows + u * time_tile, valid_rows
        )

    def col_off(span):
        return jnp.sum(col_proj[units:, span].astype(jnp.float32), axis=0, keepdims=True)

    def col_tile_features(k, n, h):
        span, part = slice(n * col_tile, (n + 1) * col_tile), slice(h * half, (h + 1) * half)
        col_bufs(k)[part, span] = col_features(states(k)[part], col_proj[:units, span], col_off(span))

    def edge_rows(h):
        size, part = slabs * LAG, row_part(h)
        if h == 0:
            turned_edges[...] = tails[...].reshape(size, units).T
        row_bufs(count)[part, :size] = row_features(
            row_proj[part], turned_edges[...], row_off[part], 0, (slabs - 1) * LAG
        )

    def edge_cols(n):
        span = slice(n * col_tile, (n + 1) * col_tile)
        col_bufs(count)[:slabs * LAG, span] = col_features(
            heads[...].reshape(slabs * LAG, units), col_proj[:units, span], col_off(span)
        )

    def moment_tile(k, lag, n, h, parts=2):
        span, part = slice(n * col_tile, (n + 1) * col_tile), slice(h * rows // parts, (h + 1) * rows // parts)
        acc = lagged if lag else instant
        buf_r, buf_c = row_bufs(k), col_bufs(k)
        if k < count:
            value = jnp.dot(ready_rows[k, part] if k < ready and first else buf_r[part], buf_c[lag:lag + slab_rows, span], preferred_element_type=jnp.float32)
        else:
            value = jnp.dot(buf_r[part, :slabs * LAG], buf_c[:slabs * LAG, span], preferred_element_type=jnp.float32)
        if k > 0 or not first:
            value = acc[part, span] + value
        if last and k == (count if lag else count - 1):
            acc[part, span] = value * (1.0 / valid_rows)
            if n == COL_TILES - 1:
                start([stores[1 if lag else 0][h]])
        else:
            acc[part, span] = value

    def feature_steps(k):
        steps = [functools.partial(col_tile_features, k, n, h) for n in range(COL_TILES) for h in range(2)]
        if k >= ready:
            steps += [functools.partial(row_tile, k, u, h) for u in range(TIME_TILES) for h in range(2)]
        return steps

    def interleave(steps, others):
        done = 0
        for n, step in enumerate(steps):
            upto = (n + 1) * len(others) // len(steps)
            for other in others[done:upto]:
                other()
            done = upto
            step()

    stores = []
    if last:
        for m, (a, b) in enumerate(zip((instant, lagged), acc_out)):
            size = rows // 2 // (m + 1)
            stores.append([
                pltpu.make_async_copy(
                    a.at[pl.ds(h * size, size)],
                    b.at[pl.ds(pl.multiple_of(place * (rows // 2) + h % (m + 1) * size, 8), size), 0], out_sem.at[m, h]
                )
                for h, place in enumerate([col] * (m + 1) + [1 - col] * (m + 1))
            ])

    if first:
        wait(col_loads)
        for step in feature_steps(0):
            step()
        for k in range(ready):
            keep_borders(k)
    for k in range(count - 1 if first else count):
        ahead = []
        steps = [functools.partial(moment_tile, k, lag, n, h) for lag in (0, LAG) for h in range(2) for n in range(COL_TILES)]
        if last and k == 0:
            steps.pop(0)()
            steps.pop(0)()
        if k + 1 < count:
            wait(loads[k + 1])
            if last and k + 2 < count:
                start(loads[k + 2])
            ahead = feature_steps(k + 1)
            if k + 1 >= ready:
                keep_borders(k + 1)
        elif last:
            ahead = [functools.partial(edge_cols, n) for n in range(COL_TILES)]
            ahead += [functools.partial(edge_rows, h) for h in range(2)]
        interleave(steps, ahead)
    if last:
        for h in range(4):
            for n in range(COL_TILES):
                moment_tile(count, LAG, n, h, 4)
        wait(stores[0] + stores[1])


def moments(slabs, at, numbers, opened, panels, carry, slab_rows, valid_rows):
    first, last = carry is None, carry is not None
    units = slabs[0][0].shape[1]
    cols = panels[0].shape[1] if first else carry[0].shape[1]
    rows, borders = 2 * cols, valid_rows // slab_rows + 1
    ready = opened[0].shape[0] if first else 1
    count = ready + len(slabs)
    pieces = [p for s in slabs for p in s]
    end_shape = (rows, 1, cols)
    outs = [pltpu.VMEM((rows, cols), jnp.float32)] * 2 + [pltpu.VMEM((borders, LAG, units), jnp.bfloat16)] * 2
    dma = pltpu.SemaphoreType.DMA
    scratch = [
        pltpu.VMEM((count - ready, slab_rows, units), jnp.bfloat16),
        pltpu.VMEM((units, slab_rows // TIME_TILES), jnp.bfloat16),
        pltpu.VMEM((rows, slab_rows), jnp.bfloat16),
        pltpu.VMEM((rows, slab_rows), jnp.bfloat16),
        pltpu.VMEM((slab_rows + LAG, cols), jnp.bfloat16),
        pltpu.VMEM((slab_rows + LAG, cols), jnp.bfloat16),
        dma((count - ready, 2)),
    ]
    args = [numbers, *pieces]
    specs = [smem_spec()] + [any_spec()] * len(pieces)
    aliases = {}
    if first:
        args += [*map(in_vmem, opened), *panels[:2], *map(in_vmem, panels[2:])]
        specs += [vmem_spec()] * 2 + [any_spec()] * 2 + [vmem_spec()] * 2
        outs = outs + [
            pltpu.VMEM((units + SPARE, cols), jnp.bfloat16),
            pltpu.VMEM((rows, slab_rows), jnp.bfloat16),
            pltpu.VMEM((slab_rows + LAG, cols), jnp.bfloat16),
        ]
        out_specs = [vmem_spec()] * 7
        scratch.append(dma)
    else:
        outs, out_specs = [pltpu.HBM(end_shape, jnp.float32)] * 2 + outs, [hbm_spec()] * 2 + [vmem_spec()] * 4
        scratch += [pltpu.VMEM((units, borders * LAG), jnp.bfloat16), dma((2, 4))]
        args += [in_vmem(x) for x in (*panels, *carry[4:], *carry[:4])]
        specs += [vmem_spec()] * 9
        aliases = {len(args) - 4 + n: 2 + n for n in range(4)}
    return pl.pallas_call(
        functools.partial(moments_kernel, count, ready, at, last, slab_rows, valid_rows),
        in_specs=specs,
        out_specs=out_specs,
        out_shape=outs,
        scratch_shapes=scratch,
        input_output_aliases=aliases,
        compiler_params=pltpu.CompilerParams(vmem_limit_bytes=(24 if last else 16) * MIB),
        cost_estimate=pl.CostEstimate(
            flops=2 * count * slab_rows * (units * (rows + cols) + 2 * rows * cols),
            bytes_accessed=2 * count * slab_rows * units,
            transcendentals=count * slab_rows * (rows + cols),
        ),
    )(*args)


def on_device(states, projection, offsets):
    slab_rows = states.shape[0]
    tm_count = lax.axis_size("tm")
    tm, row, col = (lax.axis_index(a) for a in AXES)
    x_hi, y, core = tm // Y, tm % Y, row % 2
    valid_rows = slab_rows * tm_count - LAG
    cols = projection.shape[1]
    swap = lambda piece: move(piece, other_core)

    y_first, y_second = y - 1 + 2 * core, y + 1 - 2 * core
    place = lambda other, at: jnp.where(other, 1 - x_hi, x_hi) * Y + at % Y
    ids = [tm, place(False, y_first), place(False, y_second), place(True, y), place(False, y + 2),
           place(True, y_first), place(True, y_second), place(True, y + 2)]
    source, steps = jnp.where(core == y % 2, 0, 1), (row // 2 - tm // 2) % 4
    numbers = jnp.stack([*ids, core, col, source, steps]).astype(jnp.int32)
    after = len(ids)
    line = offsets[None, :]
    numbers, line = lax.optimization_barrier((numbers, line))
    sizes = (slab_rows, valid_rows)

    columns, turned, mine = prepare(after, numbers, projection, line, states)
    partner, over, y_out = move(turned, inner), move(mine, crossing), move(mine, out_y)
    ahead, behind = move(columns, along_z(1)), move(columns, along_z(-1))
    ahead, columns = lax.optimization_barrier((ahead, columns))
    beyond = move(columns, along_z(2))
    y_out, mine = lax.optimization_barrier((y_out, mine))
    y_back = move(mine, back_y)
    over, y_out = lax.optimization_barrier((over, y_out))
    swapped_out = swap(y_out)
    ahead, behind, beyond, partner, y_back, swapped_out = lax.optimization_barrier(
        (ahead, behind, beyond, partner, y_back, swapped_out)
    )

    panel = pick(after + 3, numbers, columns, ahead, beyond, behind)
    swapped = swap(panel)
    swapped_back, swapped_over = swap(y_back), swap(over)
    slabs = [(in_hbm(states),), (y_out, swapped_back), (y_back, swapped_out)]
    row_proj, row_off, *opened = opening(slabs, numbers, turned, partner, line, *sizes)

    over_out, y_far, over_back = move(over, out_y), move(y_out, out_y), move(y_back, crossing)
    row_off, over_out = lax.optimization_barrier((row_off, over_out))
    over_far = move(over_out, out_y)
    carry = moments([(over, swapped_over)], 0, numbers, opened, (panel, swapped, row_proj, row_off), None, *sizes)

    *carry, y_far, over_back = lax.optimization_barrier((*carry, y_far, over_back))
    swapped_far, swapped_over_back = swap(y_far), swap(over_back)
    swapped_far, swapped_over_back, over_far = lax.optimization_barrier((swapped_far, swapped_over_back, over_far))
    slabs = [(y_far, swapped_far), (over_out, swapped_over_back), (over_back, swap(over_out)), (over_far, swap(over_far))]
    instant, lagged, *_ = moments(slabs, 3, numbers, None, (row_proj, row_off), carry, *sizes)
    return instant, lagged


def solution(mesh):
    return jax.shard_map(
        on_device,
        mesh=mesh,
        in_specs=(P("tm", None), P(None, ("row", "col")), P(("row", "col"))),
        out_specs=(P("row", "tm", "col"), P("row", "tm", "col")),
        check_vma=False,
    )
```

```python
import functools
import jax
import jax.numpy as jnp
from jax import lax
from jax.experimental import pallas as pl
from jax.experimental.pallas import tpu as pltpu
from jax.sharding import PartitionSpec as P

LAG = 64
Y = 4
AXES = ("tm", "row", "col")
SPARE = 16
MIB = 1024 * 1024
TIME_TILES, COL_TILES = 1, 1


def route(target):
    tm_count, row_count, col_count = (lax.axis_size(a) for a in AXES)
    flat = lambda tm, row, col: (tm * row_count + row) * col_count + col
    pairs = []
    for tm in range(tm_count):
        for row in range(row_count):
            for col in range(col_count):
                to = target(tm // Y, tm % Y, row // 2, row % 2, col)
                if to is not None:
                    x_hi, y, z, core, x_lo = to
                    pairs.append((flat(tm, row, col), flat(x_hi * Y + y % Y, z * 2 + core, x_lo)))
    return pairs


def move(block, target):
    return lax.ppermute(block, AXES, route(target))


def crossing(x_hi, y, z, core, x_lo):
    return 1 - x_hi, y, z, core, 1 - x_lo


def inner(x_hi, y, z, core, x_lo):
    return x_hi, y, z, core, 1 - x_lo


def other_core(x_hi, y, z, core, x_lo):
    return x_hi, y, z, 1 - core, x_lo


def along_y(step):
    return lambda x_hi, y, z, core, x_lo: (x_hi, y + step, z, core, x_lo)


def out_y(x_hi, y, z, core, x_lo):
    return x_hi, y + 1 - 2 * core, z, core, x_lo


def back_y(x_hi, y, z, core, x_lo):
    return x_hi, y - 1 + 2 * core, z, core, x_lo


def along_z(step):
    def target(x_hi, y, z, core, x_lo):
        return (x_hi, y, (z + step) % 4, core, x_lo) if x_hi * Y + y == z * 2 + core else None
    return target


def any_spec():
    return pl.BlockSpec(memory_space=pl.ANY)


def vmem_spec():
    return pl.BlockSpec(memory_space=pltpu.VMEM)


def hbm_spec():
    return pl.BlockSpec(memory_space=pltpu.HBM)


def in_hbm(x):
    return pltpu.with_memory_space_constraint(x, pltpu.HBM)


def in_vmem(x):
    return pltpu.with_memory_space_constraint(x, pltpu.VMEM)


def smem_spec():
    return pl.BlockSpec(memory_space=pltpu.SMEM)


def row_features(row_proj, turned, row_off, start, valid_rows):
    row_off = jnp.concatenate([row_off] * (turned.shape[1] // row_off.shape[1]), axis=1)
    features = jnp.tanh(jnp.dot(row_proj, turned, preferred_element_type=jnp.float32) + row_off)
    position = start + lax.broadcasted_iota(jnp.int32, (1, turned.shape[1]), 1)
    return jnp.where(position < valid_rows, features, 0.0).astype(jnp.bfloat16)


def col_features(states, col_proj, col_off):
    return jnp.tanh(
        jnp.dot(states, col_proj, preferred_element_type=jnp.float32) + col_off
    ).astype(jnp.bfloat16)


def start(copies):
    for copy in copies:
        copy.start()


def wait(copies):
    for copy in copies:
        copy.wait()


def prepare_kernel(at, numbers, projection, offsets, states, columns, turned, mine, line, sems):
    half = mine.shape[0]
    units, cols = projection.shape
    copies = [
        pltpu.make_async_copy(projection, columns.at[pl.ds(0, units)], sems.at[0]),
        pltpu.make_async_copy(offsets, line, sems.at[1]),
        pltpu.make_async_copy(states.at[pl.ds(pl.multiple_of(numbers[at] * half, 16), half)], mine, sems.at[2]),
    ]
    start(copies)
    turned[cols:] = jnp.zeros_like(turned[cols:])
    wait(copies[1:2])
    high = line[...].astype(jnp.bfloat16)
    rest = line[...] - high.astype(jnp.float32)
    middle = rest.astype(jnp.bfloat16)
    low = (rest - middle.astype(jnp.float32)).astype(jnp.bfloat16)
    parts = jnp.concatenate([high, middle, low, jnp.zeros((SPARE - 3, cols), jnp.bfloat16)], axis=0)
    columns[units:] = parts
    turned[cols:, :cols] = parts
    wait(copies[:1])
    turned[:cols] = columns[:units].T
    wait(copies[2:])


def prepare(at, numbers, projection, offsets, states):
    units, cols = projection.shape
    half = states.shape[0] // 2
    return pl.pallas_call(
        functools.partial(prepare_kernel, at),
        in_specs=[smem_spec(), hbm_spec(), hbm_spec(), hbm_spec()],
        out_specs=[vmem_spec(), vmem_spec(), vmem_spec()],
        out_shape=[jax.ShapeDtypeStruct((units + SPARE, cols), jnp.bfloat16),
                   jax.ShapeDtypeStruct((cols + SPARE, units), jnp.bfloat16),
                   jax.ShapeDtypeStruct((half, units), jnp.bfloat16)],
        scratch_shapes=[pltpu.VMEM((1, cols), jnp.float32), pltpu.SemaphoreType.DMA((3,))],
        compiler_params=pltpu.CompilerParams(vmem_limit_bytes=12 * MIB),
    )(numbers, in_hbm(projection), in_hbm(offsets), in_hbm(states))


class OneOf:
    def __init__(self, number, sources, dst, sem):
        self.number, self.copies = number, [pltpu.make_async_copy(x, dst, sem) for x in sources]

    def start(self):
        for n, copy in enumerate(self.copies):
            pl.when(self.number == n)(copy.start)

    def wait(self):
        self.copies[0].wait()


def pick_kernel(at, numbers, *refs):
    *sources, out, sem = refs
    copy = OneOf(numbers[at], sources, out, sem)
    copy.start()
    copy.wait()


def pick(at, numbers, *sources):
    return pl.pallas_call(
        functools.partial(pick_kernel, at),
        in_specs=[smem_spec()] + [any_spec()] * len(sources),
        out_specs=vmem_spec(),
        out_shape=jax.ShapeDtypeStruct(sources[0].shape, sources[0].dtype),
        scratch_shapes=[pltpu.SemaphoreType.DMA],
        compiler_params=pltpu.CompilerParams(vmem_limit_bytes=8 * MIB),
    )(numbers, *sources)


def slab_copies(pieces, core, dst, sems):
    if len(pieces) == 1:
        return [pltpu.make_async_copy(pieces[0], dst, sems.at[0])]
    half = pieces[0].shape[0]
    return [
        pltpu.make_async_copy(piece, dst.at[pl.ds(pl.multiple_of(place * half, 16), half)], sems.at[n])
        for n, (piece, place) in enumerate(zip(pieces, (core, 1 - core)))
    ]


def lane_broadcast(line):
    return jnp.broadcast_to(line, (128, line.shape[1])).T


def opening_kernel(count, valid_rows, ids, *refs):
    refs = list(refs)
    take = lambda n: [refs.pop(0) for _ in range(n)]
    pieces = [take(2) for _ in range(count)]
    states, turned, partner, offsets = take(4)
    row_off, slab, features, in_sem = take(4)
    slab_rows = states.shape[0]
    own = turned.shape[0] - SPARE
    core = ids[(valid_rows + LAG) // slab_rows]
    loads = [slab_copies(pieces[k], core, slab.at[k], in_sem.at[k]) for k in range(count)]
    start([copy for load in loads for copy in load])
    row_off[:own] = lane_broadcast(offsets[...])
    row_off[own:] = lane_broadcast(jnp.sum(partner[own:, :own].astype(jnp.float32), axis=0, keepdims=True))
    for k in range(count + 1):
        if k > 0:
            wait(loads[k - 1])
        turned_states = (slab[k - 1] if k > 0 else states[...]).T
        for half, proj in enumerate((turned, partner)):
            part = slice(half * own, (half + 1) * own)
            features[k, part] = row_features(
                proj[:own], turned_states, row_off[part], ids[k] * slab_rows, valid_rows
            )


def opening(slabs, numbers, states, turned, partner, offsets, valid_rows):
    own, units, count, slab_rows = turned.shape[0] - SPARE, turned.shape[1], len(slabs), states.shape[0]
    pieces = [p for s in slabs for p in s]
    return pl.pallas_call(
        functools.partial(opening_kernel, count, valid_rows),
        in_specs=[smem_spec()] + [any_spec()] * len(pieces) + [vmem_spec()] * 4,
        out_specs=[vmem_spec()] * 3,
        out_shape=[
            pltpu.VMEM((2 * own, 128), jnp.float32),
            pltpu.VMEM((count, slab_rows, units), jnp.bfloat16),
            pltpu.VMEM((count + 1, 2 * own, slab_rows), jnp.bfloat16),
        ],
        scratch_shapes=[pltpu.SemaphoreType.DMA((count, 2))],
        compiler_params=pltpu.CompilerParams(vmem_limit_bytes=12 * MIB),
        cost_estimate=pl.CostEstimate(
            flops=4 * (count + 1) * slab_rows * units * own, bytes_accessed=2 * count * slab_rows * units,
            transcendentals=2 * (count + 1) * slab_rows * own,
        ),
    )(numbers, *pieces, in_vmem(states), in_vmem(turned), in_vmem(partner), offsets)


def moments_kernel(count, ready, at, last, slab_rows, valid_rows, *refs):
    first = not last
    refs = list(refs)
    take = lambda n: [refs.pop(0) for _ in range(n)]
    (ids,) = take(1)
    slabs = (valid_rows + LAG) // slab_rows
    pieces = [None] * ready + [take(2) for _ in range(count - ready)]
    if first:
        own_states, ready_slab, ready_rows, panel, swapped = take(5)
    turned, partner, row_off = take(3)
    if last:
        col_proj, row_next, col_next = take(3)
        take(4)
        acc_out = take(2)
    instant, lagged, tails, heads = take(4)
    if first:
        col_proj, row_next, col_next = take(3)
    slab, turned_states, row_a, row_b, col_a, col_b, in_sem = take(7)
    if last:
        turned_edges, out_sem = take(2)
    rows, cols = instant.shape
    units = col_proj.shape[0] - SPARE
    half = slab_rows // 2
    time_tile, col_tile = slab_rows // TIME_TILES, cols // COL_TILES
    core, col, source = ids[slabs], ids[slabs + 1], ids[slabs + 2]
    number = lambda k: ids[at + k]

    loads = [[] if k < ready else slab_copies(pieces[k], core, slab.at[k - ready], in_sem.at[k - ready]) for k in range(count)]
    states = lambda k: slab.at[k - ready] if k >= ready else own_states if k == 0 else ready_slab.at[k - 1]
    row_proj = lambda h: (turned, partner)[h][:rows // 2]
    between = count - 1 if first else 0
    row_bufs = lambda k: row_next if k == between else (row_a, row_b)[k % 2]
    col_bufs = lambda k: col_next if k == between else (col_a, col_b)[k % 2]

    def keep_borders(k):
        tails[number(k)] = states(k)[slab_rows - LAG:]
        heads[lax.rem(number(k) + slabs - 1, slabs)] = states(k)[:LAG]

    start(loads[ready])

    for buf in (col_a, col_b) + ((col_next,) if first else ()):
        buf[slab_rows:] = jnp.zeros_like(buf[slab_rows:])

    row_part = lambda h: slice(h * rows // 2, (h + 1) * rows // 2)

    def row_tile(k, u, h):
        span, part = slice(u * time_tile, (u + 1) * time_tile), row_part(h)
        if h == 0:
            turned_states[...] = states(k)[span].T
        row_bufs(k)[part, span] = row_features(
            row_proj(h), turned_states[...], row_off[part], number(k) * slab_rows + u * time_tile, valid_rows
        )

    def col_off(span):
        return jnp.sum(col_proj[units:, span].astype(jnp.float32), axis=0, keepdims=True)

    def col_tile_features(k, n, h):
        span, part = slice(n * col_tile, (n + 1) * col_tile), slice(h * half, (h + 1) * half)
        col_bufs(k)[part, span] = col_features(states(k)[part], col_proj[:units, span], col_off(span))

    def edge_rows(h):
        size, part = slabs * LAG, row_part(h)
        if h == 0:
            turned_edges[...] = tails[...].reshape(size, units).T
        row_bufs(count)[part, :size] = row_features(
            row_proj(h), turned_edges[...], row_off[part], 0, (slabs - 1) * LAG
        )

    def edge_cols(n):
        span = slice(n * col_tile, (n + 1) * col_tile)
        col_bufs(count)[:slabs * LAG, span] = col_features(
            heads[...].reshape(slabs * LAG, units), col_proj[:units, span], col_off(span)
        )

    def moment_tile(k, lag, n, h, parts=2):
        span, part = slice(n * col_tile, (n + 1) * col_tile), slice(h * rows // parts, (h + 1) * rows // parts)
        acc = lagged if lag else instant
        buf_r, buf_c = row_bufs(k), col_bufs(k)
        if k < count:
            value = jnp.dot(ready_rows[k, part] if k < ready and first else buf_r[part], buf_c[lag:lag + slab_rows, span], preferred_element_type=jnp.float32)
        else:
            value = jnp.dot(buf_r[part, :slabs * LAG], buf_c[:slabs * LAG, span], preferred_element_type=jnp.float32)
        if k > 0 or not first:
            value = acc[part, span] + value
        if last and k == (count if lag else count - 1):
            acc[part, span] = value * (1.0 / valid_rows)
            if n == COL_TILES - 1:
                start([stores[1 if lag else 0][h]])
        else:
            acc[part, span] = value

    def feature_steps(k):
        steps = [functools.partial(col_tile_features, k, n, h) for n in range(COL_TILES) for h in range(2)]
        if k >= ready:
            steps += [functools.partial(row_tile, k, u, h) for u in range(TIME_TILES) for h in range(2)]
        return steps

    def interleave(steps, others):
        done = 0
        for n, step in enumerate(steps):
            upto = (n + 1) * len(others) // len(steps)
            for other in others[done:upto]:
                other()
            done = upto
            step()

    stores = []
    if last:
        for m, (a, b) in enumerate(zip((instant, lagged), acc_out)):
            size = rows // 2 // (m + 1)
            stores.append([
                pltpu.make_async_copy(
                    a.at[pl.ds(h * size, size)],
                    b.at[pl.ds(pl.multiple_of(place * (rows // 2) + h % (m + 1) * size, 8), size), 0], out_sem.at[m, h]
                )
                for h, place in enumerate([col] * (m + 1) + [1 - col] * (m + 1))
            ])

    if first:
        col_proj[...] = jnp.where(source == 0, panel[...], swapped[...])
        for step in feature_steps(0):
            step()
        for k in range(ready):
            keep_borders(k)
    for k in range(count - 1 if first else count):
        ahead = []
        steps = [functools.partial(moment_tile, k, lag, n, h) for lag in (0, LAG) for h in range(2) for n in range(COL_TILES)]
        if last and k == 0:
            steps.pop(0)()
            steps.pop(0)()
        if k + 1 < count:
            wait(loads[k + 1])
            if last and k + 2 < count:
                start(loads[k + 2])
            ahead = feature_steps(k + 1)
            if k + 1 >= ready:
                keep_borders(k + 1)
        elif last:
            ahead = [functools.partial(edge_cols, n) for n in range(COL_TILES)]
            ahead += [functools.partial(edge_rows, h) for h in range(2)]
        interleave(steps, ahead)
    if last:
        for h in range(4):
            for n in range(COL_TILES):
                moment_tile(count, LAG, n, h, 4)
        wait(stores[0] + stores[1])


def moments(slabs, at, numbers, states, opened, columns, panels, carry, slab_rows, valid_rows):
    first, last = carry is None, carry is not None
    units = slabs[0][0].shape[1]
    cols = panels[0].shape[0] - SPARE
    rows, borders = 2 * cols, valid_rows // slab_rows + 1
    ready = opened[0].shape[0] + 1 if first else 1
    count = ready + len(slabs)
    pieces = [p for s in slabs for p in s]
    end_shape = (rows, 1, cols)
    outs = [pltpu.VMEM((rows, cols), jnp.float32)] * 2 + [pltpu.VMEM((borders, LAG, units), jnp.bfloat16)] * 2
    dma = pltpu.SemaphoreType.DMA
    scratch = [
        pltpu.VMEM((count - ready, slab_rows, units), jnp.bfloat16),
        pltpu.VMEM((units, slab_rows // TIME_TILES), jnp.bfloat16),
        pltpu.VMEM((rows, slab_rows), jnp.bfloat16),
        pltpu.VMEM((rows, slab_rows), jnp.bfloat16),
        pltpu.VMEM((slab_rows + LAG, cols), jnp.bfloat16),
        pltpu.VMEM((slab_rows + LAG, cols), jnp.bfloat16),
        dma((count - ready, 2)),
    ]
    args = [numbers, *pieces]
    specs = [smem_spec()] + [any_spec()] * len(pieces)
    aliases = {}
    if first:
        args += [in_vmem(x) for x in (states, *opened, *columns, *panels)]
        specs += [vmem_spec()] * 8
        outs = outs + [
            pltpu.VMEM((units + SPARE, cols), jnp.bfloat16),
            pltpu.VMEM((rows, slab_rows), jnp.bfloat16),
            pltpu.VMEM((slab_rows + LAG, cols), jnp.bfloat16),
        ]
        out_specs = [vmem_spec()] * 7
    else:
        outs, out_specs = [pltpu.HBM(end_shape, jnp.float32)] * 2 + outs, [hbm_spec()] * 2 + [vmem_spec()] * 4
        scratch += [pltpu.VMEM((units, borders * LAG), jnp.bfloat16), dma((2, 4))]
        args += [in_vmem(x) for x in (*panels, *carry[4:], *carry[:4])]
        specs += [vmem_spec()] * 10
        aliases = {len(args) - 4 + n: 2 + n for n in range(4)}
    return pl.pallas_call(
        functools.partial(moments_kernel, count, ready, at, last, slab_rows, valid_rows),
        in_specs=specs,
        out_specs=out_specs,
        out_shape=outs,
        scratch_shapes=scratch,
        input_output_aliases=aliases,
        compiler_params=pltpu.CompilerParams(vmem_limit_bytes=(24 if last else 16) * MIB),
        cost_estimate=pl.CostEstimate(
            flops=2 * count * slab_rows * (units * (rows + cols) + 2 * rows * cols),
            bytes_accessed=2 * count * slab_rows * units,
            transcendentals=count * slab_rows * (rows + cols),
        ),
    )(*args)


def on_device(states, projection, offsets):
    slab_rows = states.shape[0]
    tm_count = lax.axis_size("tm")
    tm, row, col = (lax.axis_index(a) for a in AXES)
    x_hi, y, core = tm // Y, tm % Y, row % 2
    valid_rows = slab_rows * tm_count - LAG
    cols = projection.shape[1]
    swap = lambda piece: move(piece, other_core)

    y_first, y_second = y - 1 + 2 * core, y + 1 - 2 * core
    place = lambda other, at: jnp.where(other, 1 - x_hi, x_hi) * Y + at % Y
    ids = [tm, place(False, y_first), place(False, y_second), place(True, y), place(False, y + 2),
           place(True, y_first), place(True, y_second), place(True, y + 2)]
    source, steps = jnp.where(core == y % 2, 0, 1), (row // 2 - tm // 2) % 4
    numbers = jnp.stack([*ids, core, col, source, steps]).astype(jnp.int32)
    after = len(ids)
    line = offsets[None, :]
    numbers, line = lax.optimization_barrier((numbers, line))
    sizes = (slab_rows, valid_rows)

    columns, turned, mine = prepare(after, numbers, projection, line, states)
    partner, over, y_out = move(turned, inner), move(mine, crossing), move(mine, out_y)
    ahead, behind = move(columns, along_z(1)), move(columns, along_z(-1))
    ahead, columns = lax.optimization_barrier((ahead, columns))
    beyond = move(columns, along_z(2))
    y_out, mine = lax.optimization_barrier((y_out, mine))
    y_back = move(mine, back_y)
    over, y_out = lax.optimization_barrier((over, y_out))
    swapped_out = swap(y_out)
    ahead, behind, beyond, partner, y_back, swapped_out = lax.optimization_barrier(
        (ahead, behind, beyond, partner, y_back, swapped_out)
    )

    panel = pick(after + 3, numbers, columns, ahead, beyond, behind)
    swapped = swap(panel)
    swapped_back, swapped_over = swap(y_back), swap(over)
    slabs = [(y_out, swapped_back), (y_back, swapped_out)]
    row_off, *opened = opening(slabs, numbers, states, turned, partner, line, valid_rows)

    over_out, y_far, over_back = move(over, out_y), move(y_out, out_y), move(y_back, crossing)
    row_off, over_out = lax.optimization_barrier((row_off, over_out))
    over_far = move(over_out, out_y)
    panels = (turned, partner, row_off)
    carry = moments([(over, swapped_over)], 0, numbers, states, opened, (panel, swapped), panels, None, *sizes)

    *carry, y_far, over_back = lax.optimization_barrier((*carry, y_far, over_back))
    swapped_far, swapped_over_back = swap(y_far), swap(over_back)
    swapped_far, swapped_over_back, over_far = lax.optimization_barrier((swapped_far, swapped_over_back, over_far))
    slabs = [(y_far, swapped_far), (over_out, swapped_over_back), (over_back, swap(over_out)), (over_far, swap(over_far))]
    instant, lagged, *_ = moments(slabs, 3, numbers, None, None, None, panels, carry, *sizes)
    return instant, lagged


def solution(mesh):
    return jax.shard_map(
        on_device,
        mesh=mesh,
        in_specs=(P("tm", None), P(None, ("row", "col")), P(("row", "col"))),
        out_specs=(P("row", "tm", "col"), P("row", "tm", "col")),
        check_vma=False,
    )
```

```python
import functools
import jax
import jax.numpy as jnp
from jax import lax
from jax.experimental import pallas as pl
from jax.experimental.pallas import tpu as pltpu
from jax.sharding import PartitionSpec as P

LAG = 64
Y = 4
AXES = ("tm", "row", "col")
SPARE = 16
MIB = 1024 * 1024
TIME_TILES, COL_TILES = 1, 1


def route(target):
    tm_count, row_count, col_count = (lax.axis_size(a) for a in AXES)
    flat = lambda tm, row, col: (tm * row_count + row) * col_count + col
    pairs = []
    for tm in range(tm_count):
        for row in range(row_count):
            for col in range(col_count):
                to = target(tm // Y, tm % Y, row // 2, row % 2, col)
                if to is not None:
                    x_hi, y, z, core, x_lo = to
                    pairs.append((flat(tm, row, col), flat(x_hi * Y + y % Y, z * 2 + core, x_lo)))
    return pairs


def move(block, target):
    return lax.ppermute(block, AXES, route(target))


def crossing(x_hi, y, z, core, x_lo):
    return 1 - x_hi, y, z, core, 1 - x_lo


def inner(x_hi, y, z, core, x_lo):
    return x_hi, y, z, core, 1 - x_lo


def other_core(x_hi, y, z, core, x_lo):
    return x_hi, y, z, 1 - core, x_lo


def along_y(step):
    return lambda x_hi, y, z, core, x_lo: (x_hi, y + step, z, core, x_lo)


def out_y(x_hi, y, z, core, x_lo):
    return x_hi, y + 1 - 2 * core, z, core, x_lo


def back_y(x_hi, y, z, core, x_lo):
    return x_hi, y - 1 + 2 * core, z, core, x_lo


def along_z(step):
    def target(x_hi, y, z, core, x_lo):
        return (x_hi, y, (z + step) % 4, core, x_lo) if x_hi * Y + y == z * 2 + core else None
    return target


def any_spec():
    return pl.BlockSpec(memory_space=pl.ANY)


def vmem_spec():
    return pl.BlockSpec(memory_space=pltpu.VMEM)


def hbm_spec():
    return pl.BlockSpec(memory_space=pltpu.HBM)


def in_hbm(x):
    return pltpu.with_memory_space_constraint(x, pltpu.HBM)


def in_vmem(x):
    return pltpu.with_memory_space_constraint(x, pltpu.VMEM)


def smem_spec():
    return pl.BlockSpec(memory_space=pltpu.SMEM)


def row_features(row_proj, turned, row_off, start, valid_rows):
    row_off = jnp.concatenate([row_off] * (turned.shape[1] // row_off.shape[1]), axis=1)
    features = jnp.tanh(jnp.dot(row_proj, turned, preferred_element_type=jnp.float32) + row_off)
    position = start + lax.broadcasted_iota(jnp.int32, (1, turned.shape[1]), 1)
    return jnp.where(position < valid_rows, features, 0.0).astype(jnp.bfloat16)


def col_features(states, col_proj, col_off):
    return jnp.tanh(
        jnp.dot(states, col_proj, preferred_element_type=jnp.float32) + col_off
    ).astype(jnp.bfloat16)


def start(copies):
    for copy in copies:
        copy.start()


def wait(copies):
    for copy in copies:
        copy.wait()


def prepare_kernel(at, numbers, projection, offsets, states, columns, turned, mine, line, sems):
    half = mine.shape[0]
    units, cols = projection.shape
    copies = [
        pltpu.make_async_copy(projection, columns.at[pl.ds(0, units)], sems.at[0]),
        pltpu.make_async_copy(offsets, line, sems.at[1]),
        pltpu.make_async_copy(states.at[pl.ds(pl.multiple_of(numbers[at] * half, 16), half)], mine, sems.at[2]),
    ]
    start(copies)
    turned[cols:] = jnp.zeros_like(turned[cols:])
    wait(copies[1:2])
    high = line[...].astype(jnp.bfloat16)
    rest = line[...] - high.astype(jnp.float32)
    middle = rest.astype(jnp.bfloat16)
    low = (rest - middle.astype(jnp.float32)).astype(jnp.bfloat16)
    parts = jnp.concatenate([high, middle, low, jnp.zeros((SPARE - 3, cols), jnp.bfloat16)], axis=0)
    columns[units:] = parts
    turned[cols:, :cols] = parts
    wait(copies[:1])
    turned[:cols] = columns[:units].T
    wait(copies[2:])


def prepare(at, numbers, projection, offsets, states):
    units, cols = projection.shape
    half = states.shape[0] // 2
    return pl.pallas_call(
        functools.partial(prepare_kernel, at),
        in_specs=[smem_spec(), hbm_spec(), hbm_spec(), hbm_spec()],
        out_specs=[vmem_spec(), vmem_spec(), vmem_spec()],
        out_shape=[jax.ShapeDtypeStruct((units + SPARE, cols), jnp.bfloat16),
                   jax.ShapeDtypeStruct((cols + SPARE, units), jnp.bfloat16),
                   jax.ShapeDtypeStruct((half, units), jnp.bfloat16)],
        scratch_shapes=[pltpu.VMEM((1, cols), jnp.float32), pltpu.SemaphoreType.DMA((3,))],
        compiler_params=pltpu.CompilerParams(vmem_limit_bytes=12 * MIB),
    )(numbers, in_hbm(projection), in_hbm(offsets), in_hbm(states))


class OneOf:
    def __init__(self, number, sources, dst, sem):
        self.number, self.copies = number, [pltpu.make_async_copy(x, dst, sem) for x in sources]

    def start(self):
        for n, copy in enumerate(self.copies):
            pl.when(self.number == n)(copy.start)

    def wait(self):
        self.copies[0].wait()


def pick_kernel(at, numbers, *refs):
    *sources, out, sem = refs
    copy = OneOf(numbers[at], sources, out, sem)
    copy.start()
    copy.wait()


def pick(at, numbers, *sources):
    return pl.pallas_call(
        functools.partial(pick_kernel, at),
        in_specs=[smem_spec()] + [any_spec()] * len(sources),
        out_specs=vmem_spec(),
        out_shape=jax.ShapeDtypeStruct(sources[0].shape, sources[0].dtype),
        scratch_shapes=[pltpu.SemaphoreType.DMA],
        compiler_params=pltpu.CompilerParams(vmem_limit_bytes=8 * MIB),
    )(numbers, *sources)


def slab_copies(pieces, core, dst, sems):
    if len(pieces) == 1:
        return [pltpu.make_async_copy(pieces[0], dst, sems.at[0])]
    half = pieces[0].shape[0]
    return [
        pltpu.make_async_copy(piece, dst.at[pl.ds(pl.multiple_of(place * half, 16), half)], sems.at[n])
        for n, (piece, place) in enumerate(zip(pieces, (core, 1 - core)))
    ]


def lane_broadcast(line):
    return jnp.broadcast_to(line, (128, line.shape[1])).T


def opening_kernel(count, valid_rows, ids, *refs):
    refs = list(refs)
    take = lambda n: [refs.pop(0) for _ in range(n)]
    pieces = [take(2) for _ in range(count)]
    states, turned, partner, offsets = take(4)
    row_off, slab, features, in_sem = take(4)
    slab_rows = states.shape[0]
    own = turned.shape[0] - SPARE
    core = ids[(valid_rows + LAG) // slab_rows]
    loads = [slab_copies(pieces[k], core, slab.at[k], in_sem.at[k]) for k in range(count)]
    start([copy for load in loads for copy in load])
    row_off[:own] = lane_broadcast(offsets[...])
    row_off[own:] = lane_broadcast(jnp.sum(partner[own:, :own].astype(jnp.float32), axis=0, keepdims=True))
    for k in range(count + 1):
        if k > 0:
            wait(loads[k - 1])
        turned_states = (slab[k - 1] if k > 0 else states[...]).T
        for half, proj in enumerate((turned, partner)):
            part = slice(half * own, (half + 1) * own)
            features[k, part] = row_features(
                proj[:own], turned_states, row_off[part], ids[k] * slab_rows, valid_rows
            )


def opening(slabs, numbers, states, turned, partner, offsets, valid_rows):
    own, units, count, slab_rows = turned.shape[0] - SPARE, turned.shape[1], len(slabs), states.shape[0]
    pieces = [p for s in slabs for p in s]
    return pl.pallas_call(
        functools.partial(opening_kernel, count, valid_rows),
        in_specs=[smem_spec()] + [any_spec()] * len(pieces) + [vmem_spec()] * 4,
        out_specs=[vmem_spec()] * 3,
        out_shape=[
            pltpu.VMEM((2 * own, 128), jnp.float32),
            pltpu.VMEM((count, slab_rows, units), jnp.bfloat16),
            pltpu.VMEM((count + 1, 2 * own, slab_rows), jnp.bfloat16),
        ],
        scratch_shapes=[pltpu.SemaphoreType.DMA((count, 2))],
        compiler_params=pltpu.CompilerParams(vmem_limit_bytes=12 * MIB),
        cost_estimate=pl.CostEstimate(
            flops=4 * (count + 1) * slab_rows * units * own, bytes_accessed=2 * count * slab_rows * units,
            transcendentals=2 * (count + 1) * slab_rows * own,
        ),
    )(numbers, *pieces, in_vmem(states), in_vmem(turned), in_vmem(partner), offsets)


def moments_kernel(count, ready, at, last, slab_rows, valid_rows, *refs):
    first = not last
    refs = list(refs)
    take = lambda n: [refs.pop(0) for _ in range(n)]
    (ids,) = take(1)
    slabs = (valid_rows + LAG) // slab_rows
    pieces = [None] * ready + [take(2) for _ in range(count - ready)]
    if first:
        own_states, ready_slab, ready_rows, panel, swapped = take(5)
    turned, partner, row_off = take(3)
    if last:
        col_proj, row_next, col_next = take(3)
        take(4)
        acc_out = take(2)
    instant, lagged, tails, heads = take(4)
    if first:
        col_proj, row_next, col_next = take(3)
    slab, turned_states, row_a, row_b, col_a, col_b, in_sem = take(7)
    if last:
        turned_edges, out_sem = take(2)
    rows, cols = instant.shape
    units = col_proj.shape[0] - SPARE
    half = slab_rows // 2
    time_tile, col_tile = slab_rows // TIME_TILES, cols // COL_TILES
    core, col, source = ids[slabs], ids[slabs + 1], ids[slabs + 2]
    number = lambda k: ids[at + k]

    loads = [[] if k < ready else slab_copies(pieces[k], core, slab.at[k - ready], in_sem.at[k - ready]) for k in range(count)]
    states = lambda k: slab.at[k - ready] if k >= ready else own_states if k == 0 else ready_slab.at[k - 1]
    row_proj = lambda h: (turned, partner)[h][:rows // 2]
    between = count - 1 if first else 0
    row_bufs = lambda k: row_next if k == between else (row_a, row_b)[k % 2]
    col_bufs = lambda k: col_next if k == between else (col_a, col_b)[k % 2]

    def keep_borders(k):
        tails[number(k)] = states(k)[slab_rows - LAG:]
        heads[lax.rem(number(k) + slabs - 1, slabs)] = states(k)[:LAG]

    start(loads[ready])

    for buf in (col_a, col_b) + ((col_next,) if first else ()):
        buf[slab_rows:] = jnp.zeros_like(buf[slab_rows:])

    row_part = lambda h: slice(h * rows // 2, (h + 1) * rows // 2)

    def row_tile(k, u, h):
        span, part = slice(u * time_tile, (u + 1) * time_tile), row_part(h)
        if h == 0:
            turned_states[...] = states(k)[span].T
        row_bufs(k)[part, span] = row_features(
            row_proj(h), turned_states[...], row_off[part], number(k) * slab_rows + u * time_tile, valid_rows
        )

    def col_off(span):
        return jnp.sum(col_proj[units:, span].astype(jnp.float32), axis=0, keepdims=True)

    def col_tile_features(k, n, h):
        span, part = slice(n * col_tile, (n + 1) * col_tile), slice(h * half, (h + 1) * half)
        col_bufs(k)[part, span] = col_features(states(k)[part], col_proj[:units, span], col_off(span))

    def edge_rows(h):
        size, part = slabs * LAG, row_part(h)
        if h == 0:
            turned_edges[...] = tails[...].reshape(size, units).T
        row_bufs(count)[part, :size] = row_features(
            row_proj(h), turned_edges[...], row_off[part], 0, (slabs - 1) * LAG
        )

    def edge_cols(n):
        span = slice(n * col_tile, (n + 1) * col_tile)
        col_bufs(count)[:slabs * LAG, span] = col_features(
            heads[...].reshape(slabs * LAG, units), col_proj[:units, span], col_off(span)
        )

    def moment_tile(k, lag, n, h, parts=2):
        span, part = slice(n * col_tile, (n + 1) * col_tile), slice(h * rows // parts, (h + 1) * rows // parts)
        acc = lagged if lag else instant
        buf_r, buf_c = row_bufs(k), col_bufs(k)
        if k < count:
            value = jnp.dot(ready_rows[k, part] if k < ready and first else buf_r[part], buf_c[lag:lag + slab_rows, span], preferred_element_type=jnp.float32)
        else:
            value = jnp.dot(buf_r[part, :slabs * LAG], buf_c[:slabs * LAG, span], preferred_element_type=jnp.float32)
        if k > 0 or not first:
            value = acc[part, span] + value
        if last and k == (count if lag else count - 1):
            acc[part, span] = value * (1.0 / valid_rows)
            if n == COL_TILES - 1:
                start([stores[1 if lag else 0][h]])
        else:
            acc[part, span] = value

    def feature_steps(k):
        steps = [functools.partial(col_tile_features, k, n, h) for n in range(COL_TILES) for h in range(2)]
        if k >= ready:
            steps += [functools.partial(row_tile, k, u, h) for u in range(TIME_TILES) for h in range(2)]
        return steps

    def interleave(steps, others):
        done = 0
        for n, step in enumerate(steps):
            upto = (n + 1) * len(others) // len(steps)
            for other in others[done:upto]:
                other()
            done = upto
            step()

    stores = []
    if last:
        for m, (a, b) in enumerate(zip((instant, lagged), acc_out)):
            size = rows // 2 // (m + 1)
            stores.append([
                pltpu.make_async_copy(
                    a.at[pl.ds(h * size, size)],
                    b.at[pl.ds(pl.multiple_of(place * (rows // 2) + h % (m + 1) * size, 8), size), 0], out_sem.at[m, h]
                )
                for h, place in enumerate([col] * (m + 1) + [1 - col] * (m + 1))
            ])

    if first:
        col_proj[...] = jnp.where(source == 0, panel[...], swapped[...])
        for step in feature_steps(0):
            step()
        for k in range(ready):
            keep_borders(k)
    for k in range(count - 1 if first else count):
        ahead = []
        steps = [functools.partial(moment_tile, k, lag, n, h) for lag in (0, LAG) for h in range(2) for n in range(COL_TILES)]
        if last and k == 0:
            steps.pop(0)()
            steps.pop(0)()
        if k + 1 < count:
            wait(loads[k + 1])
            if last and k + 2 < count:
                start(loads[k + 2])
            ahead = feature_steps(k + 1)
            if k + 1 >= ready:
                keep_borders(k + 1)
        elif last:
            ahead = [functools.partial(edge_cols, n) for n in range(COL_TILES)]
            ahead += [functools.partial(edge_rows, h) for h in range(2)]
        interleave(steps, ahead)
    if last:
        for h in range(4):
            for n in range(COL_TILES):
                moment_tile(count, LAG, n, h, 4)
        wait(stores[0] + stores[1])


def moments(slabs, at, numbers, states, opened, columns, panels, carry, slab_rows, valid_rows):
    first, last = carry is None, carry is not None
    units = slabs[0][0].shape[1]
    cols = panels[0].shape[0] - SPARE
    rows, borders = 2 * cols, valid_rows // slab_rows + 1
    ready = opened[0].shape[0] + 1 if first else 1
    count = ready + len(slabs)
    pieces = [p for s in slabs for p in s]
    end_shape = (rows, 1, cols)
    outs = [pltpu.VMEM((rows, cols), jnp.float32)] * 2 + [pltpu.VMEM((borders, LAG, units), jnp.bfloat16)] * 2
    dma = pltpu.SemaphoreType.DMA
    scratch = [
        pltpu.VMEM((count - ready, slab_rows, units), jnp.bfloat16),
        pltpu.VMEM((units, slab_rows // TIME_TILES), jnp.bfloat16),
        pltpu.VMEM((rows, slab_rows), jnp.bfloat16),
        pltpu.VMEM((rows, slab_rows), jnp.bfloat16),
        pltpu.VMEM((slab_rows + LAG, cols), jnp.bfloat16),
        pltpu.VMEM((slab_rows + LAG, cols), jnp.bfloat16),
        dma((count - ready, 2)),
    ]
    args = [numbers, *pieces]
    specs = [smem_spec()] + [any_spec()] * len(pieces)
    aliases = {}
    if first:
        args += [in_vmem(x) for x in (states, *opened, *columns, *panels)]
        specs += [vmem_spec()] * 8
        outs = outs + [
            pltpu.VMEM((units + SPARE, cols), jnp.bfloat16),
            pltpu.VMEM((rows, slab_rows), jnp.bfloat16),
            pltpu.VMEM((slab_rows + LAG, cols), jnp.bfloat16),
        ]
        out_specs = [vmem_spec()] * 7
    else:
        outs, out_specs = [pltpu.HBM(end_shape, jnp.float32)] * 2 + outs, [hbm_spec()] * 2 + [vmem_spec()] * 4
        scratch += [pltpu.VMEM((units, borders * LAG), jnp.bfloat16), dma((2, 4))]
        args += [in_vmem(x) for x in (*panels, *carry[4:], *carry[:4])]
        specs += [vmem_spec()] * 10
        aliases = {len(args) - 4 + n: 2 + n for n in range(4)}
    return pl.pallas_call(
        functools.partial(moments_kernel, count, ready, at, last, slab_rows, valid_rows),
        in_specs=specs,
        out_specs=out_specs,
        out_shape=outs,
        scratch_shapes=scratch,
        input_output_aliases=aliases,
        compiler_params=pltpu.CompilerParams(vmem_limit_bytes=(24 if last else 16) * MIB),
        cost_estimate=pl.CostEstimate(
            flops=2 * count * slab_rows * (units * (rows + cols) + 2 * rows * cols),
            bytes_accessed=2 * count * slab_rows * units,
            transcendentals=count * slab_rows * (rows + cols),
        ),
    )(*args)


def on_device(states, projection, offsets):
    slab_rows = states.shape[0]
    tm_count = lax.axis_size("tm")
    tm, row, col = (lax.axis_index(a) for a in AXES)
    x_hi, y, core = tm // Y, tm % Y, row % 2
    valid_rows = slab_rows * tm_count - LAG
    cols = projection.shape[1]
    swap = lambda piece: move(piece, other_core)

    y_first, y_second = y - 1 + 2 * core, y + 1 - 2 * core
    place = lambda other, at: jnp.where(other, 1 - x_hi, x_hi) * Y + at % Y
    ids = [tm, place(False, y_first), place(False, y_second), place(True, y), place(False, y + 2),
           place(True, y_first), place(True, y_second), place(True, y + 2)]
    source, steps = jnp.where(core == y % 2, 0, 1), (row // 2 - tm // 2) % 4
    numbers = jnp.stack([*ids, core, col, source, steps]).astype(jnp.int32)
    after = len(ids)
    line = offsets[None, :]
    numbers, line = lax.optimization_barrier((numbers, line))
    sizes = (slab_rows, valid_rows)

    columns, turned, mine = prepare(after, numbers, projection, line, states)
    partner, over, y_out = move(turned, inner), move(mine, crossing), move(mine, out_y)
    ahead, behind = move(columns, along_z(1)), move(columns, along_z(-1))
    ahead, columns = lax.optimization_barrier((ahead, columns))
    beyond = move(columns, along_z(2))
    y_out, mine = lax.optimization_barrier((y_out, mine))
    y_back = move(mine, back_y)
    over_out = move(over, out_y)
    ahead, behind, beyond, partner, y_out, y_back, over_out = lax.optimization_barrier(
        (ahead, behind, beyond, partner, y_out, y_back, over_out)
    )

    panel = pick(after + 3, numbers, columns, ahead, beyond, behind)
    swapped = swap(panel)
    swapped_out, swapped_back, swapped_over = swap(y_out), swap(y_back), swap(over)
    slabs = [(y_out, swapped_back), (y_back, swapped_out)]
    row_off, *opened = opening(slabs, numbers, states, turned, partner, line, valid_rows)
    row_off, swapped_over_out = lax.optimization_barrier((row_off, swap(over_out)))

    y_far, over_back = move(y_out, out_y), move(y_back, crossing)
    over_far = move(over_out, out_y)
    panels = (turned, partner, row_off)
    carry = moments([(over, swapped_over)], 0, numbers, states, opened, (panel, swapped), panels, None, *sizes)

    *carry, y_far, over_back = lax.optimization_barrier((*carry, y_far, over_back))
    swapped_far, swapped_over_back = swap(y_far), swap(over_back)
    swapped_far, swapped_over_back, over_far = lax.optimization_barrier((swapped_far, swapped_over_back, over_far))
    slabs = [(y_far, swapped_far), (over_out, swapped_over_back), (over_back, swapped_over_out), (over_far, swap(over_far))]
    instant, lagged, *_ = moments(slabs, 3, numbers, None, None, None, panels, carry, *sizes)
    return instant, lagged


def solution(mesh):
    return jax.shard_map(
        on_device,
        mesh=mesh,
        in_specs=(P("tm", None), P(None, ("row", "col")), P(("row", "col"))),
        out_specs=(P("row", "tm", "col"), P("row", "tm", "col")),
        check_vma=False,
    )
```

```python
import functools
import jax
import jax.numpy as jnp
from jax import lax
from jax.experimental import pallas as pl
from jax.experimental.pallas import tpu as pltpu
from jax.sharding import PartitionSpec as P

LAG = 64
Y = 4
AXES = ("tm", "row", "col")
SPARE = 16
MIB = 1024 * 1024
TIME_TILES, COL_TILES = 1, 1


def route(target):
    tm_count, row_count, col_count = (lax.axis_size(a) for a in AXES)
    flat = lambda tm, row, col: (tm * row_count + row) * col_count + col
    pairs = []
    for tm in range(tm_count):
        for row in range(row_count):
            for col in range(col_count):
                to = target(tm // Y, tm % Y, row // 2, row % 2, col)
                if to is not None:
                    x_hi, y, z, core, x_lo = to
                    pairs.append((flat(tm, row, col), flat(x_hi * Y + y % Y, z * 2 + core, x_lo)))
    return pairs


def move(block, target):
    return lax.ppermute(block, AXES, route(target))


def crossing(x_hi, y, z, core, x_lo):
    return 1 - x_hi, y, z, core, 1 - x_lo


def inner(x_hi, y, z, core, x_lo):
    return x_hi, y, z, core, 1 - x_lo


def other_core(x_hi, y, z, core, x_lo):
    return x_hi, y, z, 1 - core, x_lo


def along_y(step):
    return lambda x_hi, y, z, core, x_lo: (x_hi, y + step, z, core, x_lo)


def out_y(x_hi, y, z, core, x_lo):
    return x_hi, y + 1 - 2 * core, z, core, x_lo


def back_y(x_hi, y, z, core, x_lo):
    return x_hi, y - 1 + 2 * core, z, core, x_lo


def along_z(step):
    def target(x_hi, y, z, core, x_lo):
        return (x_hi, y, (z + step) % 4, core, x_lo) if x_hi * Y + y == z * 2 + core else None
    return target


def any_spec():
    return pl.BlockSpec(memory_space=pl.ANY)


def vmem_spec():
    return pl.BlockSpec(memory_space=pltpu.VMEM)


def hbm_spec():
    return pl.BlockSpec(memory_space=pltpu.HBM)


def in_hbm(x):
    return pltpu.with_memory_space_constraint(x, pltpu.HBM)


def in_vmem(x):
    return pltpu.with_memory_space_constraint(x, pltpu.VMEM)


def smem_spec():
    return pl.BlockSpec(memory_space=pltpu.SMEM)


def row_features(row_proj, turned, row_off, start, valid_rows):
    row_off = jnp.concatenate([row_off] * (turned.shape[1] // row_off.shape[1]), axis=1)
    features = jnp.tanh(jnp.dot(row_proj, turned, preferred_element_type=jnp.float32) + row_off)
    position = start + lax.broadcasted_iota(jnp.int32, (1, turned.shape[1]), 1)
    return jnp.where(position < valid_rows, features, 0.0).astype(jnp.bfloat16)


def col_features(states, col_proj, col_off):
    return jnp.tanh(
        jnp.dot(states, col_proj, preferred_element_type=jnp.float32) + col_off
    ).astype(jnp.bfloat16)


def start(copies):
    for copy in copies:
        copy.start()


def wait(copies):
    for copy in copies:
        copy.wait()


def prepare_kernel(at, numbers, projection, offsets, states, columns, turned, mine, line, sems):
    half = mine.shape[0]
    units, cols = projection.shape
    copies = [
        pltpu.make_async_copy(projection, columns.at[pl.ds(0, units)], sems.at[0]),
        pltpu.make_async_copy(offsets, line, sems.at[1]),
        pltpu.make_async_copy(states.at[pl.ds(pl.multiple_of(numbers[at] * half, 16), half)], mine, sems.at[2]),
    ]
    start(copies)
    turned[cols:] = jnp.zeros_like(turned[cols:])
    wait(copies[1:2])
    high = line[...].astype(jnp.bfloat16)
    rest = line[...] - high.astype(jnp.float32)
    middle = rest.astype(jnp.bfloat16)
    low = (rest - middle.astype(jnp.float32)).astype(jnp.bfloat16)
    parts = jnp.concatenate([high, middle, low, jnp.zeros((SPARE - 3, cols), jnp.bfloat16)], axis=0)
    columns[units:] = parts
    turned[cols:, :cols] = parts
    wait(copies[:1])
    turned[:cols] = columns[:units].T
    wait(copies[2:])


def prepare(at, numbers, projection, offsets, states):
    units, cols = projection.shape
    half = states.shape[0] // 2
    return pl.pallas_call(
        functools.partial(prepare_kernel, at),
        in_specs=[smem_spec(), hbm_spec(), hbm_spec(), hbm_spec()],
        out_specs=[vmem_spec(), vmem_spec(), vmem_spec()],
        out_shape=[jax.ShapeDtypeStruct((units + SPARE, cols), jnp.bfloat16),
                   jax.ShapeDtypeStruct((cols + SPARE, units), jnp.bfloat16),
                   jax.ShapeDtypeStruct((half, units), jnp.bfloat16)],
        scratch_shapes=[pltpu.VMEM((1, cols), jnp.float32), pltpu.SemaphoreType.DMA((3,))],
        compiler_params=pltpu.CompilerParams(vmem_limit_bytes=12 * MIB),
    )(numbers, in_hbm(projection), in_hbm(offsets), in_hbm(states))


class OneOf:
    def __init__(self, number, sources, dst, sem):
        self.number, self.copies = number, [pltpu.make_async_copy(x, dst, sem) for x in sources]

    def start(self):
        for n, copy in enumerate(self.copies):
            pl.when(self.number == n)(copy.start)

    def wait(self):
        self.copies[0].wait()


def pick_kernel(at, numbers, *refs):
    *sources, out, sem = refs
    copy = OneOf(numbers[at], sources, out, sem)
    copy.start()
    copy.wait()


def pick(at, numbers, *sources):
    return pl.pallas_call(
        functools.partial(pick_kernel, at),
        in_specs=[smem_spec()] + [any_spec()] * len(sources),
        out_specs=vmem_spec(),
        out_shape=jax.ShapeDtypeStruct(sources[0].shape, sources[0].dtype),
        scratch_shapes=[pltpu.SemaphoreType.DMA],
        compiler_params=pltpu.CompilerParams(vmem_limit_bytes=8 * MIB),
    )(numbers, *sources)


def slab_copies(pieces, core, dst, sems):
    if len(pieces) == 1:
        return [pltpu.make_async_copy(pieces[0], dst, sems.at[0])]
    half = pieces[0].shape[0]
    return [
        pltpu.make_async_copy(piece, dst.at[pl.ds(pl.multiple_of(place * half, 16), half)], sems.at[n])
        for n, (piece, place) in enumerate(zip(pieces, (core, 1 - core)))
    ]


def lane_broadcast(line):
    return jnp.broadcast_to(line, (128, line.shape[1])).T


def opening_kernel(count, valid_rows, ids, *refs):
    refs = list(refs)
    take = lambda n: [refs.pop(0) for _ in range(n)]
    pieces = [take(2) for _ in range(count)]
    states, turned, partner, offsets = take(4)
    row_off, slab, features, in_sem = take(4)
    slab_rows = states.shape[0]
    own = turned.shape[0] - SPARE
    core = ids[(valid_rows + LAG) // slab_rows]
    loads = [slab_copies(pieces[k], core, slab.at[k], in_sem.at[k]) for k in range(count)]
    start([copy for load in loads for copy in load])
    row_off[:own] = lane_broadcast(offsets[...])
    row_off[own:] = lane_broadcast(jnp.sum(partner[own:, :own].astype(jnp.float32), axis=0, keepdims=True))
    for k in range(count + 1):
        if k > 0:
            wait(loads[k - 1])
        turned_states = (slab[k - 1] if k > 0 else states[...]).T
        for half, proj in enumerate((turned, partner)):
            part = slice(half * own, (half + 1) * own)
            features[k, part] = row_features(
                proj[:own], turned_states, row_off[part], ids[k] * slab_rows, valid_rows
            )


def opening(slabs, numbers, states, turned, partner, offsets, valid_rows):
    own, units, count, slab_rows = turned.shape[0] - SPARE, turned.shape[1], len(slabs), states.shape[0]
    pieces = [p for s in slabs for p in s]
    return pl.pallas_call(
        functools.partial(opening_kernel, count, valid_rows),
        in_specs=[smem_spec()] + [any_spec()] * len(pieces) + [vmem_spec()] * 4,
        out_specs=[vmem_spec()] * 3,
        out_shape=[
            pltpu.VMEM((2 * own, 128), jnp.float32),
            pltpu.VMEM((count, slab_rows, units), jnp.bfloat16),
            pltpu.VMEM((count + 1, 2 * own, slab_rows), jnp.bfloat16),
        ],
        scratch_shapes=[pltpu.SemaphoreType.DMA((count, 2))],
        compiler_params=pltpu.CompilerParams(vmem_limit_bytes=12 * MIB),
        cost_estimate=pl.CostEstimate(
            flops=4 * (count + 1) * slab_rows * units * own, bytes_accessed=2 * count * slab_rows * units,
            transcendentals=2 * (count + 1) * slab_rows * own,
        ),
    )(numbers, *pieces, in_vmem(states), in_vmem(turned), in_vmem(partner), offsets)


def moments_kernel(count, ready, at, last, slab_rows, valid_rows, *refs):
    first = not last
    refs = list(refs)
    take = lambda n: [refs.pop(0) for _ in range(n)]
    (ids,) = take(1)
    slabs = (valid_rows + LAG) // slab_rows
    pieces = [None] * ready + [take(2) for _ in range(count - ready)]
    if first:
        own_states, ready_slab, ready_rows, panel, swapped = take(5)
    turned, partner, row_off = take(3)
    if last:
        col_proj, row_next, col_next = take(3)
        take(4)
        acc_out = take(2)
    instant, lagged, tails, heads = take(4)
    if first:
        col_proj, row_next, col_next = take(3)
    slab, turned_states, row_a, row_b, col_a, col_b, in_sem = take(7)
    if last:
        turned_edges, out_sem = take(2)
    rows, cols = instant.shape
    units = col_proj.shape[0] - SPARE
    half = slab_rows // 2
    time_tile, col_tile = slab_rows // TIME_TILES, cols // COL_TILES
    core, col, source = ids[slabs], ids[slabs + 1], ids[slabs + 2]
    number = lambda k: ids[at + k]

    loads = [[] if k < ready else slab_copies(pieces[k], core, slab.at[k - ready], in_sem.at[k - ready]) for k in range(count)]
    states = lambda k: slab.at[k - ready] if k >= ready else own_states if k == 0 else ready_slab.at[k - 1]
    row_proj = lambda h: (turned, partner)[h][:rows // 2]
    between = count - 1 if first else 0
    row_bufs = lambda k: row_next if k == between else (row_a, row_b)[k % 2]
    col_bufs = lambda k: col_next if k == between else (col_a, col_b)[k % 2]

    def keep_borders(k):
        tails[number(k)] = states(k)[slab_rows - LAG:]
        heads[lax.rem(number(k) + slabs - 1, slabs)] = states(k)[:LAG]

    start(loads[ready])

    for buf in (col_a, col_b) + ((col_next,) if first else ()):
        buf[slab_rows:] = jnp.zeros_like(buf[slab_rows:])

    row_part = lambda h: slice(h * rows // 2, (h + 1) * rows // 2)

    def row_tile(k, u, h):
        span, part = slice(u * time_tile, (u + 1) * time_tile), row_part(h)
        if h == 0:
            turned_states[...] = states(k)[span].T
        row_bufs(k)[part, span] = row_features(
            row_proj(h), turned_states[...], row_off[part], number(k) * slab_rows + u * time_tile, valid_rows
        )

    def col_off(span):
        return jnp.sum(col_proj[units:, span].astype(jnp.float32), axis=0, keepdims=True)

    def col_tile_features(k, n, h):
        span, part = slice(n * col_tile, (n + 1) * col_tile), slice(h * half, (h + 1) * half)
        col_bufs(k)[part, span] = col_features(states(k)[part], col_proj[:units, span], col_off(span))

    def edge_rows(h):
        size, part = slabs * LAG, row_part(h)
        if h == 0:
            turned_edges[...] = tails[...].reshape(size, units).T
        row_bufs(count)[part, :size] = row_features(
            row_proj(h), turned_edges[...], row_off[part], 0, (slabs - 1) * LAG
        )

    def edge_cols(n):
        span = slice(n * col_tile, (n + 1) * col_tile)
        col_bufs(count)[:slabs * LAG, span] = col_features(
            heads[...].reshape(slabs * LAG, units), col_proj[:units, span], col_off(span)
        )

    def moment_tile(k, lag, n, h, parts=2):
        span, part = slice(n * col_tile, (n + 1) * col_tile), slice(h * rows // parts, (h + 1) * rows // parts)
        acc = lagged if lag else instant
        buf_r, buf_c = row_bufs(k), col_bufs(k)
        if k < count:
            value = jnp.dot(ready_rows[k, part] if k < ready and first else buf_r[part], buf_c[lag:lag + slab_rows, span], preferred_element_type=jnp.float32)
        else:
            value = jnp.dot(buf_r[part, :slabs * LAG], buf_c[:slabs * LAG, span], preferred_element_type=jnp.float32)
        if k > 0 or not first:
            value = acc[part, span] + value
        if last and k == (count if lag else count - 1):
            acc[part, span] = value * (1.0 / valid_rows)
            if n == COL_TILES - 1:
                start([stores[1 if lag else 0][h]])
        else:
            acc[part, span] = value

    def feature_steps(k):
        steps = [functools.partial(col_tile_features, k, n, h) for n in range(COL_TILES) for h in range(2)]
        if k >= ready:
            steps += [functools.partial(row_tile, k, u, h) for u in range(TIME_TILES) for h in range(2)]
        return steps

    def interleave(steps, others):
        done = 0
        for n, step in enumerate(steps):
            upto = (n + 1) * len(others) // len(steps)
            for other in others[done:upto]:
                other()
            done = upto
            step()

    stores = []
    if last:
        for m, (a, b) in enumerate(zip((instant, lagged), acc_out)):
            size = rows // 2 // (m + 1)
            stores.append([
                pltpu.make_async_copy(
                    a.at[pl.ds(h * size, size)],
                    b.at[pl.ds(pl.multiple_of(place * (rows // 2) + h % (m + 1) * size, 8), size), 0], out_sem.at[m, h]
                )
                for h, place in enumerate([col] * (m + 1) + [1 - col] * (m + 1))
            ])

    if first:
        col_proj[...] = jnp.where(source == 0, panel[...], swapped[...])
        for step in feature_steps(0):
            step()
        for k in range(ready):
            keep_borders(k)
    for k in range(count - 1 if first else count):
        ahead = []
        lags = (LAG,) if last and k == 0 else (0, LAG)
        steps = [functools.partial(moment_tile, k, lag, n, h) for lag in lags for h in range(2) for n in range(COL_TILES)]
        if last and k == 0:
            steps.pop(0)()
        if k + 1 < count:
            wait(loads[k + 1])
            if last and k + 2 < count:
                start(loads[k + 2])
            ahead = feature_steps(k + 1)
            if k + 1 >= ready:
                keep_borders(k + 1)
        elif last:
            ahead = [functools.partial(edge_cols, n) for n in range(COL_TILES)]
            ahead += [functools.partial(edge_rows, h) for h in range(2)]
        interleave(steps, ahead)
    if first:
        for h in range(2):
            for n in range(COL_TILES):
                moment_tile(between, 0, n, h)
    else:
        for h in range(4):
            for n in range(COL_TILES):
                moment_tile(count, LAG, n, h, 4)
        wait(stores[0] + stores[1])


def moments(slabs, at, numbers, states, opened, columns, panels, carry, slab_rows, valid_rows):
    first, last = carry is None, carry is not None
    units = slabs[0][0].shape[1]
    cols = panels[0].shape[0] - SPARE
    rows, borders = 2 * cols, valid_rows // slab_rows + 1
    ready = opened[0].shape[0] + 1 if first else 1
    count = ready + len(slabs)
    pieces = [p for s in slabs for p in s]
    end_shape = (rows, 1, cols)
    outs = [pltpu.VMEM((rows, cols), jnp.float32)] * 2 + [pltpu.VMEM((borders, LAG, units), jnp.bfloat16)] * 2
    dma = pltpu.SemaphoreType.DMA
    scratch = [
        pltpu.VMEM((count - ready, slab_rows, units), jnp.bfloat16),
        pltpu.VMEM((units, slab_rows // TIME_TILES), jnp.bfloat16),
        pltpu.VMEM((rows, slab_rows), jnp.bfloat16),
        pltpu.VMEM((rows, slab_rows), jnp.bfloat16),
        pltpu.VMEM((slab_rows + LAG, cols), jnp.bfloat16),
        pltpu.VMEM((slab_rows + LAG, cols), jnp.bfloat16),
        dma((count - ready, 2)),
    ]
    args = [numbers, *pieces]
    specs = [smem_spec()] + [any_spec()] * len(pieces)
    aliases = {}
    if first:
        args += [in_vmem(x) for x in (states, *opened, *columns, *panels)]
        specs += [vmem_spec()] * 8
        outs = outs + [
            pltpu.VMEM((units + SPARE, cols), jnp.bfloat16),
            pltpu.VMEM((rows, slab_rows), jnp.bfloat16),
            pltpu.VMEM((slab_rows + LAG, cols), jnp.bfloat16),
        ]
        out_specs = [vmem_spec()] * 7
    else:
        outs, out_specs = [pltpu.HBM(end_shape, jnp.float32)] * 2 + outs, [hbm_spec()] * 2 + [vmem_spec()] * 4
        scratch += [pltpu.VMEM((units, borders * LAG), jnp.bfloat16), dma((2, 4))]
        args += [in_vmem(x) for x in (*panels, *carry[4:], *carry[:4])]
        specs += [vmem_spec()] * 10
        aliases = {len(args) - 4 + n: 2 + n for n in range(4)}
    return pl.pallas_call(
        functools.partial(moments_kernel, count, ready, at, last, slab_rows, valid_rows),
        in_specs=specs,
        out_specs=out_specs,
        out_shape=outs,
        scratch_shapes=scratch,
        input_output_aliases=aliases,
        compiler_params=pltpu.CompilerParams(vmem_limit_bytes=(24 if last else 16) * MIB),
        cost_estimate=pl.CostEstimate(
            flops=2 * count * slab_rows * (units * (rows + cols) + 2 * rows * cols),
            bytes_accessed=2 * count * slab_rows * units,
            transcendentals=count * slab_rows * (rows + cols),
        ),
    )(*args)


def on_device(states, projection, offsets):
    slab_rows = states.shape[0]
    tm_count = lax.axis_size("tm")
    tm, row, col = (lax.axis_index(a) for a in AXES)
    x_hi, y, core = tm // Y, tm % Y, row % 2
    valid_rows = slab_rows * tm_count - LAG
    cols = projection.shape[1]
    swap = lambda piece: move(piece, other_core)

    y_first, y_second = y - 1 + 2 * core, y + 1 - 2 * core
    place = lambda other, at: jnp.where(other, 1 - x_hi, x_hi) * Y + at % Y
    ids = [tm, place(False, y_first), place(False, y_second), place(True, y), place(False, y + 2),
           place(True, y_first), place(True, y_second), place(True, y + 2)]
    source, steps = jnp.where(core == y % 2, 0, 1), (row // 2 - tm // 2) % 4
    numbers = jnp.stack([*ids, core, col, source, steps]).astype(jnp.int32)
    after = len(ids)
    line = offsets[None, :]
    numbers, line = lax.optimization_barrier((numbers, line))
    sizes = (slab_rows, valid_rows)

    columns, turned, mine = prepare(after, numbers, projection, line, states)
    partner, over, y_out = move(turned, inner), move(mine, crossing), move(mine, out_y)
    ahead, behind = move(columns, along_z(1)), move(columns, along_z(-1))
    ahead, columns = lax.optimization_barrier((ahead, columns))
    beyond = move(columns, along_z(2))
    y_out, mine = lax.optimization_barrier((y_out, mine))
    y_back = move(mine, back_y)
    over, y_out = lax.optimization_barrier((over, y_out))
    swapped_out = swap(y_out)
    ahead, behind, beyond, partner, y_back, swapped_out = lax.optimization_barrier(
        (ahead, behind, beyond, partner, y_back, swapped_out)
    )

    panel = pick(after + 3, numbers, columns, ahead, beyond, behind)
    swapped = swap(panel)
    swapped_back, swapped_over = swap(y_back), swap(over)
    slabs = [(y_out, swapped_back), (y_back, swapped_out)]
    row_off, *opened = opening(slabs, numbers, states, turned, partner, line, valid_rows)

    over_out, y_far, over_back = move(over, out_y), move(y_out, out_y), move(y_back, crossing)
    row_off, over_out = lax.optimization_barrier((row_off, over_out))
    over_far = move(over_out, out_y)
    panels = (turned, partner, row_off)
    carry = moments([(over, swapped_over)], 0, numbers, states, opened, (panel, swapped), panels, None, *sizes)

    *carry, y_far, over_back = lax.optimization_barrier((*carry, y_far, over_back))
    swapped_far, swapped_over_back = swap(y_far), swap(over_back)
    swapped_far, swapped_over_back, over_far = lax.optimization_barrier((swapped_far, swapped_over_back, over_far))
    slabs = [(y_far, swapped_far), (over_out, swapped_over_back), (over_back, swap(over_out)), (over_far, swap(over_far))]
    instant, lagged, *_ = moments(slabs, 3, numbers, None, None, None, panels, carry, *sizes)
    return instant, lagged


def solution(mesh):
    return jax.shard_map(
        on_device,
        mesh=mesh,
        in_specs=(P("tm", None), P(None, ("row", "col")), P(("row", "col"))),
        out_specs=(P("row", "tm", "col"), P("row", "tm", "col")),
        check_vma=False,
    )
```

```python
import functools
import jax
import jax.numpy as jnp
from jax import lax
from jax.experimental import pallas as pl
from jax.experimental.pallas import tpu as pltpu
from jax.sharding import PartitionSpec as P

LAG = 64
Y = 4
AXES = ("tm", "row", "col")
SPARE = 16
MIB = 1024 * 1024
TIME_TILES, COL_TILES = 1, 1


def route(target):
    tm_count, row_count, col_count = (lax.axis_size(a) for a in AXES)
    flat = lambda tm, row, col: (tm * row_count + row) * col_count + col
    pairs = []
    for tm in range(tm_count):
        for row in range(row_count):
            for col in range(col_count):
                to = target(tm // Y, tm % Y, row // 2, row % 2, col)
                if to is not None:
                    x_hi, y, z, core, x_lo = to
                    pairs.append((flat(tm, row, col), flat(x_hi * Y + y % Y, z * 2 + core, x_lo)))
    return pairs


def move(block, target):
    return lax.ppermute(block, AXES, route(target))


def crossing(x_hi, y, z, core, x_lo):
    return 1 - x_hi, y, z, core, 1 - x_lo


def inner(x_hi, y, z, core, x_lo):
    return x_hi, y, z, core, 1 - x_lo


def other_core(x_hi, y, z, core, x_lo):
    return x_hi, y, z, 1 - core, x_lo


def along_y(step):
    return lambda x_hi, y, z, core, x_lo: (x_hi, y + step, z, core, x_lo)


def out_y(x_hi, y, z, core, x_lo):
    return x_hi, y + 1 - 2 * core, z, core, x_lo


def back_y(x_hi, y, z, core, x_lo):
    return x_hi, y - 1 + 2 * core, z, core, x_lo


def along_z(step):
    def target(x_hi, y, z, core, x_lo):
        return (x_hi, y, (z + step) % 4, core, x_lo) if x_hi * Y + y == z * 2 + core else None
    return target


def any_spec():
    return pl.BlockSpec(memory_space=pl.ANY)


def vmem_spec():
    return pl.BlockSpec(memory_space=pltpu.VMEM)


def hbm_spec():
    return pl.BlockSpec(memory_space=pltpu.HBM)


def in_hbm(x):
    return pltpu.with_memory_space_constraint(x, pltpu.HBM)


def in_vmem(x):
    return pltpu.with_memory_space_constraint(x, pltpu.VMEM)


def smem_spec():
    return pl.BlockSpec(memory_space=pltpu.SMEM)


def row_features(row_proj, turned, row_off, start, valid_rows):
    row_off = jnp.concatenate([row_off] * (turned.shape[1] // row_off.shape[1]), axis=1)
    features = jnp.tanh(jnp.dot(row_proj, turned, preferred_element_type=jnp.float32) + row_off)
    position = start + lax.broadcasted_iota(jnp.int32, (1, turned.shape[1]), 1)
    return jnp.where(position < valid_rows, features, 0.0).astype(jnp.bfloat16)


def col_features(states, col_proj, col_off):
    return jnp.tanh(
        jnp.dot(states, col_proj, preferred_element_type=jnp.float32) + col_off
    ).astype(jnp.bfloat16)


def start(copies):
    for copy in copies:
        copy.start()


def wait(copies):
    for copy in copies:
        copy.wait()


def prepare_kernel(at, numbers, projection, offsets, states, columns, turned, mine, line, sems):
    half = mine.shape[0]
    units, cols = projection.shape
    copies = [
        pltpu.make_async_copy(projection, columns.at[pl.ds(0, units)], sems.at[0]),
        pltpu.make_async_copy(offsets, line, sems.at[1]),
        pltpu.make_async_copy(states.at[pl.ds(pl.multiple_of(numbers[at] * half, 16), half)], mine, sems.at[2]),
    ]
    start(copies)
    turned[cols:] = jnp.zeros_like(turned[cols:])
    wait(copies[1:2])
    high = line[...].astype(jnp.bfloat16)
    rest = line[...] - high.astype(jnp.float32)
    middle = rest.astype(jnp.bfloat16)
    low = (rest - middle.astype(jnp.float32)).astype(jnp.bfloat16)
    parts = jnp.concatenate([high, middle, low, jnp.zeros((SPARE - 3, cols), jnp.bfloat16)], axis=0)
    columns[units:] = parts
    turned[cols:, :cols] = parts
    wait(copies[:1])
    turned[:cols] = columns[:units].T
    wait(copies[2:])


def prepare(at, numbers, projection, offsets, states):
    units, cols = projection.shape
    half = states.shape[0] // 2
    return pl.pallas_call(
        functools.partial(prepare_kernel, at),
        in_specs=[smem_spec(), hbm_spec(), hbm_spec(), hbm_spec()],
        out_specs=[vmem_spec(), vmem_spec(), vmem_spec()],
        out_shape=[jax.ShapeDtypeStruct((units + SPARE, cols), jnp.bfloat16),
                   jax.ShapeDtypeStruct((cols + SPARE, units), jnp.bfloat16),
                   jax.ShapeDtypeStruct((half, units), jnp.bfloat16)],
        scratch_shapes=[pltpu.VMEM((1, cols), jnp.float32), pltpu.SemaphoreType.DMA((3,))],
        compiler_params=pltpu.CompilerParams(vmem_limit_bytes=12 * MIB),
    )(numbers, in_hbm(projection), in_hbm(offsets), in_hbm(states))


class OneOf:
    def __init__(self, number, sources, dst, sem):
        self.number, self.copies = number, [pltpu.make_async_copy(x, dst, sem) for x in sources]

    def start(self):
        for n, copy in enumerate(self.copies):
            pl.when(self.number == n)(copy.start)

    def wait(self):
        self.copies[0].wait()


def pick_kernel(at, numbers, *refs):
    *sources, out, sem = refs
    copy = OneOf(numbers[at], sources, out, sem)
    copy.start()
    copy.wait()


def pick(at, numbers, *sources):
    return pl.pallas_call(
        functools.partial(pick_kernel, at),
        in_specs=[smem_spec()] + [any_spec()] * len(sources),
        out_specs=vmem_spec(),
        out_shape=jax.ShapeDtypeStruct(sources[0].shape, sources[0].dtype),
        scratch_shapes=[pltpu.SemaphoreType.DMA],
        compiler_params=pltpu.CompilerParams(vmem_limit_bytes=8 * MIB),
    )(numbers, *sources)


def slab_copies(pieces, core, dst, sems):
    if len(pieces) == 1:
        return [pltpu.make_async_copy(pieces[0], dst, sems.at[0])]
    half = pieces[0].shape[0]
    return [
        pltpu.make_async_copy(piece, dst.at[pl.ds(pl.multiple_of(place * half, 16), half)], sems.at[n])
        for n, (piece, place) in enumerate(zip(pieces, (core, 1 - core)))
    ]


def lane_broadcast(line):
    return jnp.broadcast_to(line, (128, line.shape[1])).T


def opening_kernel(count, valid_rows, ids, *refs):
    refs = list(refs)
    take = lambda n: [refs.pop(0) for _ in range(n)]
    pieces = [take(2) for _ in range(count)]
    states, turned, partner, offsets = take(4)
    row_off, slab, features, in_sem = take(4)
    slab_rows = states.shape[0]
    own = turned.shape[0] - SPARE
    core = ids[(valid_rows + LAG) // slab_rows]
    loads = [slab_copies(pieces[k], core, slab.at[k], in_sem.at[k]) for k in range(count)]
    start([copy for load in loads for copy in load])
    row_off[:own] = lane_broadcast(offsets[...])
    row_off[own:] = lane_broadcast(jnp.sum(partner[own:, :own].astype(jnp.float32), axis=0, keepdims=True))
    for k in range(count + 1):
        if k > 0:
            wait(loads[k - 1])
        turned_states = (slab[k - 1] if k > 0 else states[...]).T
        for half, proj in enumerate((turned, partner)):
            part = slice(half * own, (half + 1) * own)
            features[k, part] = row_features(
                proj[:own], turned_states, row_off[part], ids[k] * slab_rows, valid_rows
            )


def opening(slabs, numbers, states, turned, partner, offsets, valid_rows):
    own, units, count, slab_rows = turned.shape[0] - SPARE, turned.shape[1], len(slabs), states.shape[0]
    pieces = [p for s in slabs for p in s]
    return pl.pallas_call(
        functools.partial(opening_kernel, count, valid_rows),
        in_specs=[smem_spec()] + [any_spec()] * len(pieces) + [vmem_spec()] * 4,
        out_specs=[vmem_spec()] * 3,
        out_shape=[
            pltpu.VMEM((2 * own, 128), jnp.float32),
            pltpu.VMEM((count, slab_rows, units), jnp.bfloat16),
            pltpu.VMEM((count + 1, 2 * own, slab_rows), jnp.bfloat16),
        ],
        scratch_shapes=[pltpu.SemaphoreType.DMA((count, 2))],
        compiler_params=pltpu.CompilerParams(vmem_limit_bytes=12 * MIB),
        cost_estimate=pl.CostEstimate(
            flops=4 * (count + 1) * slab_rows * units * own, bytes_accessed=2 * count * slab_rows * units,
            transcendentals=2 * (count + 1) * slab_rows * own,
        ),
    )(numbers, *pieces, in_vmem(states), in_vmem(turned), in_vmem(partner), offsets)


def moments_kernel(count, ready, at, last, slab_rows, valid_rows, *refs):
    first = not last
    refs = list(refs)
    take = lambda n: [refs.pop(0) for _ in range(n)]
    (ids,) = take(1)
    slabs = (valid_rows + LAG) // slab_rows
    pieces = [None] * ready + [take(2) for _ in range(count - ready)]
    if first:
        own_states, ready_slab, ready_rows, panel, swapped = take(5)
    turned, partner, row_off = take(3)
    if last:
        col_proj, row_next, col_next = take(3)
        take(4)
        acc_out = take(2)
    instant, lagged, tails, heads = take(4)
    if first:
        col_proj, row_next, col_next = take(3)
    slab, turned_states, row_a, row_b, col_a, col_b, in_sem = take(7)
    if last:
        turned_edges, out_sem = take(2)
    rows, cols = instant.shape
    units = col_proj.shape[0] - SPARE
    half = slab_rows // 2
    time_tile, col_tile = slab_rows // TIME_TILES, cols // COL_TILES
    core, col, source = ids[slabs], ids[slabs + 1], ids[slabs + 2]
    number = lambda k: ids[at + k]

    loads = [[] if k < ready else slab_copies(pieces[k], core, slab.at[k - ready], in_sem.at[k - ready]) for k in range(count)]
    states = lambda k: slab.at[k - ready] if k >= ready else own_states if k == 0 else ready_slab.at[k - 1]
    row_proj = lambda h: (turned, partner)[h][:rows // 2]
    between = count - 1 if first else 0
    row_bufs = lambda k: row_next if k == between else (row_a, row_b)[k % 2]
    col_bufs = lambda k: col_next if k == between else (col_a, col_b)[k % 2]

    def keep_borders(k):
        tails[number(k)] = states(k)[slab_rows - LAG:]
        heads[lax.rem(number(k) + slabs - 1, slabs)] = states(k)[:LAG]

    start(loads[ready])

    for buf in (col_a, col_b) + ((col_next,) if first else ()):
        buf[slab_rows:] = jnp.zeros_like(buf[slab_rows:])

    row_part = lambda h: slice(h * rows // 2, (h + 1) * rows // 2)

    def row_tile(k, u, h):
        span, part = slice(u * time_tile, (u + 1) * time_tile), row_part(h)
        if h == 0:
            turned_states[...] = states(k)[span].T
        row_bufs(k)[part, span] = row_features(
            row_proj(h), turned_states[...], row_off[part], number(k) * slab_rows + u * time_tile, valid_rows
        )

    def col_off(span):
        return jnp.sum(col_proj[units:, span].astype(jnp.float32), axis=0, keepdims=True)

    def col_tile_features(k, n, h):
        span, part = slice(n * col_tile, (n + 1) * col_tile), slice(h * half, (h + 1) * half)
        col_bufs(k)[part, span] = col_features(states(k)[part], col_proj[:units, span], col_off(span))

    def edge_rows(h):
        size, part = slabs * LAG, row_part(h)
        if h == 0:
            turned_edges[...] = tails[...].reshape(size, units).T
        row_bufs(count)[part, :size] = row_features(
            row_proj(h), turned_edges[...], row_off[part], 0, (slabs - 1) * LAG
        )

    def edge_cols(n):
        span = slice(n * col_tile, (n + 1) * col_tile)
        col_bufs(count)[:slabs * LAG, span] = col_features(
            heads[...].reshape(slabs * LAG, units), col_proj[:units, span], col_off(span)
        )

    def moment_tile(k, lag, n, h, parts=2):
        span, part = slice(n * col_tile, (n + 1) * col_tile), slice(h * rows // parts, (h + 1) * rows // parts)
        acc = lagged if lag else instant
        buf_r, buf_c = row_bufs(k), col_bufs(k)
        if k < count:
            value = jnp.dot(ready_rows[k, part] if k < ready and first else buf_r[part], buf_c[lag:lag + slab_rows, span], preferred_element_type=jnp.float32)
        else:
            value = jnp.dot(buf_r[part, :slabs * LAG], buf_c[:slabs * LAG, span], preferred_element_type=jnp.float32)
        if k > 0 or not first:
            value = acc[part, span] + value
        if last and k == (count if lag else count - 1):
            acc[part, span] = value * (1.0 / valid_rows)
            if n == COL_TILES - 1:
                start([stores[1 if lag else 0][h]])
        else:
            acc[part, span] = value

    def feature_steps(k):
        steps = [functools.partial(col_tile_features, k, n, h) for n in range(COL_TILES) for h in range(2)]
        if k >= ready:
            steps += [functools.partial(row_tile, k, u, h) for u in range(TIME_TILES) for h in range(2)]
        return steps

    def interleave(steps, others):
        done = 0
        for n, step in enumerate(steps):
            upto = (n + 1) * len(others) // len(steps)
            for other in others[done:upto]:
                other()
            done = upto
            step()

    stores = []
    if last:
        for m, (a, b) in enumerate(zip((instant, lagged), acc_out)):
            size = rows // 2 // (m + 1)
            stores.append([
                pltpu.make_async_copy(
                    a.at[pl.ds(h * size, size)],
                    b.at[pl.ds(pl.multiple_of(place * (rows // 2) + h % (m + 1) * size, 8), size), 0], out_sem.at[m, h]
                )
                for h, place in enumerate([col] * (m + 1) + [1 - col] * (m + 1))
            ])

    if first:
        col_proj[...] = jnp.where(source == 0, panel[...], swapped[...])
        for step in feature_steps(0):
            step()
        for k in range(ready):
            keep_borders(k)
    for k in range(count - 1 if first else count):
        ahead = []
        lags = (LAG,) if last and k == 0 else (0, LAG)
        steps = [functools.partial(moment_tile, k, lag, n, h) for lag in lags for h in range(2) for n in range(COL_TILES)]
        if last and k == 0:
            steps = steps[COL_TILES:]
        if last and k == 0:
            steps.pop(0)()
        if k + 1 < count:
            wait(loads[k + 1])
            if last and k + 2 < count:
                start(loads[k + 2])
            ahead = feature_steps(k + 1)
            if k + 1 >= ready:
                keep_borders(k + 1)
        elif last:
            ahead = [functools.partial(edge_cols, n) for n in range(COL_TILES)]
            ahead += [functools.partial(edge_rows, h) for h in range(2)]
        interleave(steps or [lambda: None], ahead)
    if first:
        for lag, h in ((0, 0), (0, 1), (LAG, 0)):
            for n in range(COL_TILES):
                moment_tile(between, lag, n, h)
    else:
        for h in range(4):
            for n in range(COL_TILES):
                moment_tile(count, LAG, n, h, 4)
        wait(stores[0] + stores[1])


def moments(slabs, at, numbers, states, opened, columns, panels, carry, slab_rows, valid_rows):
    first, last = carry is None, carry is not None
    units = slabs[0][0].shape[1]
    cols = panels[0].shape[0] - SPARE
    rows, borders = 2 * cols, valid_rows // slab_rows + 1
    ready = opened[0].shape[0] + 1 if first else 1
    count = ready + len(slabs)
    pieces = [p for s in slabs for p in s]
    end_shape = (rows, 1, cols)
    outs = [pltpu.VMEM((rows, cols), jnp.float32)] * 2 + [pltpu.VMEM((borders, LAG, units), jnp.bfloat16)] * 2
    dma = pltpu.SemaphoreType.DMA
    scratch = [
        pltpu.VMEM((count - ready, slab_rows, units), jnp.bfloat16),
        pltpu.VMEM((units, slab_rows // TIME_TILES), jnp.bfloat16),
        pltpu.VMEM((rows, slab_rows), jnp.bfloat16),
        pltpu.VMEM((rows, slab_rows), jnp.bfloat16),
        pltpu.VMEM((slab_rows + LAG, cols), jnp.bfloat16),
        pltpu.VMEM((slab_rows + LAG, cols), jnp.bfloat16),
        dma((count - ready, 2)),
    ]
    args = [numbers, *pieces]
    specs = [smem_spec()] + [any_spec()] * len(pieces)
    aliases = {}
    if first:
        args += [in_vmem(x) for x in (states, *opened, *columns, *panels)]
        specs += [vmem_spec()] * 8
        outs = outs + [
            pltpu.VMEM((units + SPARE, cols), jnp.bfloat16),
            pltpu.VMEM((rows, slab_rows), jnp.bfloat16),
            pltpu.VMEM((slab_rows + LAG, cols), jnp.bfloat16),
        ]
        out_specs = [vmem_spec()] * 7
    else:
        outs, out_specs = [pltpu.HBM(end_shape, jnp.float32)] * 2 + outs, [hbm_spec()] * 2 + [vmem_spec()] * 4
        scratch += [pltpu.VMEM((units, borders * LAG), jnp.bfloat16), dma((2, 4))]
        args += [in_vmem(x) for x in (*panels, *carry[4:], *carry[:4])]
        specs += [vmem_spec()] * 10
        aliases = {len(args) - 4 + n: 2 + n for n in range(4)}
    return pl.pallas_call(
        functools.partial(moments_kernel, count, ready, at, last, slab_rows, valid_rows),
        in_specs=specs,
        out_specs=out_specs,
        out_shape=outs,
        scratch_shapes=scratch,
        input_output_aliases=aliases,
        compiler_params=pltpu.CompilerParams(vmem_limit_bytes=(24 if last else 16) * MIB),
        cost_estimate=pl.CostEstimate(
            flops=2 * count * slab_rows * (units * (rows + cols) + 2 * rows * cols),
            bytes_accessed=2 * count * slab_rows * units,
            transcendentals=count * slab_rows * (rows + cols),
        ),
    )(*args)


def on_device(states, projection, offsets):
    slab_rows = states.shape[0]
    tm_count = lax.axis_size("tm")
    tm, row, col = (lax.axis_index(a) for a in AXES)
    x_hi, y, core = tm // Y, tm % Y, row % 2
    valid_rows = slab_rows * tm_count - LAG
    cols = projection.shape[1]
    swap = lambda piece: move(piece, other_core)

    y_first, y_second = y - 1 + 2 * core, y + 1 - 2 * core
    place = lambda other, at: jnp.where(other, 1 - x_hi, x_hi) * Y + at % Y
    ids = [tm, place(False, y_first), place(False, y_second), place(True, y), place(False, y + 2),
           place(True, y_first), place(True, y_second), place(True, y + 2)]
    source, steps = jnp.where(core == y % 2, 0, 1), (row // 2 - tm // 2) % 4
    numbers = jnp.stack([*ids, core, col, source, steps]).astype(jnp.int32)
    after = len(ids)
    line = offsets[None, :]
    numbers, line = lax.optimization_barrier((numbers, line))
    sizes = (slab_rows, valid_rows)

    columns, turned, mine = prepare(after, numbers, projection, line, states)
    partner, over, y_out = move(turned, inner), move(mine, crossing), move(mine, out_y)
    ahead, behind = move(columns, along_z(1)), move(columns, along_z(-1))
    ahead, columns = lax.optimization_barrier((ahead, columns))
    beyond = move(columns, along_z(2))
    y_out, mine = lax.optimization_barrier((y_out, mine))
    y_back = move(mine, back_y)
    over, y_out = lax.optimization_barrier((over, y_out))
    swapped_out = swap(y_out)
    ahead, behind, beyond, partner, y_back, swapped_out = lax.optimization_barrier(
        (ahead, behind, beyond, partner, y_back, swapped_out)
    )

    panel = pick(after + 3, numbers, columns, ahead, beyond, behind)
    swapped = swap(panel)
    swapped_back, swapped_over = swap(y_back), swap(over)
    slabs = [(y_out, swapped_back), (y_back, swapped_out)]
    row_off, *opened = opening(slabs, numbers, states, turned, partner, line, valid_rows)

    over_out, y_far, over_back = move(over, out_y), move(y_out, out_y), move(y_back, crossing)
    row_off, over_out = lax.optimization_barrier((row_off, over_out))
    over_far = move(over_out, out_y)
    panels = (turned, partner, row_off)
    carry = moments([(over, swapped_over)], 0, numbers, states, opened, (panel, swapped), panels, None, *sizes)

    *carry, y_far, over_back = lax.optimization_barrier((*carry, y_far, over_back))
    swapped_far, swapped_over_back = swap(y_far), swap(over_back)
    swapped_far, swapped_over_back, over_far = lax.optimization_barrier((swapped_far, swapped_over_back, over_far))
    slabs = [(y_far, swapped_far), (over_out, swapped_over_back), (over_back, swap(over_out)), (over_far, swap(over_far))]
    instant, lagged, *_ = moments(slabs, 3, numbers, None, None, None, panels, carry, *sizes)
    return instant, lagged


def solution(mesh):
    return jax.shard_map(
        on_device,
        mesh=mesh,
        in_specs=(P("tm", None), P(None, ("row", "col")), P(("row", "col"))),
        out_specs=(P("row", "tm", "col"), P("row", "tm", "col")),
        check_vma=False,
    )
```
